32 devices in a mesh: dp: 16 (over z, x, core), tensor: 2 (over y).
Axes of the slice: x: 2, y: 2, z: 4, core: 2. Of those that a mesh axis runs over, the one named last changes fastest.
Arguments:
- tokens: bfloat16 [8192, 2048], P('dp'), may hold values from -6 to 6
- out_grad: bfloat16 [8192, 2048], P('dp'), may hold values from -6 to 6
- lengths: int32 [8], replicated, may hold values from 1 to 4096, 8192 in all
- attn_gain: float32 [2048], replicated, may hold values from 0.5 to 1.5
- q_weight: bfloat16 [2048, 2048], P('dp', 'tensor'), may hold values from -0.125 to 0.125
- key_matrix: bfloat16 [2048, 1024], P('dp', 'tensor'), may hold values from -0.125 to 0.125
- value_matrix: bfloat16 [2048, 1024], P('dp', 'tensor'), may hold values from -0.125 to 0.125
- o_weight: bfloat16 [2048, 2048], P('dp', 'tensor'), may hold values from -0.5 to 0.5
- q_gain: float32 [128], replicated, may hold values from 1 to 2
- k_gain: float32 [128], replicated, may hold values from 0.75 to 1.5
- mlp_gain: float32 [2048], replicated, may hold values from 0.5 to 1.5
- gate_weight: bfloat16 [2048, 6144], P('dp', 'tensor'), may hold values from -0.125 to 0.125
- up_weight: bfloat16 [2048, 6144], P('dp', 'tensor'), may hold values from -0.125 to 0.125
- down_weight: bfloat16 [2048, 6144], P('dp', 'tensor'), may hold values from -0.078125 to 0.078125
Outputs:
- output: bfloat16 [8192, 2048], P('dp')
- input_grad: float32 [8192, 2048], P('dp')
- grad_attn_gain: float32 [2048], replicated
- grad_q_weight: float32 [2048, 2048], P('dp', 'tensor')
- grad_k_weight: float32 [2048, 1024], P('dp', 'tensor')
- grad_v_weight: float32 [2048, 1024], P('dp', 'tensor')
- grad_o_weight: float32 [2048, 2048], P('dp', 'tensor')
- grad_q_gain: float32 [128], replicated
- grad_k_gain: float32 [128], replicated
- grad_mlp_gain: float32 [2048], replicated
- grad_gate_weight: float32 [2048, 6144], P('dp', 'tensor')
- grad_up_weight: float32 [2048, 6144], P('dp', 'tensor')
- grad_down_weight: float32 [2048, 6144], P('dp', 'tensor')
The draws below stay inside these ranges and needn't reach their ends.
Inputs may be any that keep to these rules, and one draw needn't show every extreme that they name: Sequence lengths in pack order; they sum to 8192 and the longest is exactly 4096.
All inputs are finite; a program needn't handle non-finite values.
Results may differ from the reference program's by a relative error of at most 0.02.
Values may be sent and summed in bfloat16 or wider, within the bound.
A program may use at most 320 MiB of HBM per device.

```python
import math
import jax
import jax.numpy as jnp
import numpy as np
from jax import lax

MODEL_WIDTH = 2048
QUERY_HEADS = 16
KEY_VALUE_HEADS = 8
HEAD_SIZE = 128
FF = 6144
TOKENS_PER_SHARD = 512
LONGEST = 4096
REACH = 8
PACK_TOKENS = 8192
NSEQ = 8


def shard_levels(own_key, dims, cuts, least, largest):
    loudness, own = 1.0, jax.random.fold_in(own_key, 6)
    for axis_at, parts in cuts:
        steps = jnp.exp(jax.random.uniform(jax.random.fold_in(own, axis_at), (parts,), jnp.float32, least / len(cuts), largest / len(cuts)))
        loudness = loudness * jnp.repeat(steps, dims[axis_at] // parts).reshape([-1 if axis == axis_at else 1 for axis in range(len(dims))])
    return loudness


def length_profile(amount, total, reach, slope):
    portions = [(1 << 20) // math.isqrt(grade ** slope) + 1 for grade in range(2, amount + 1)]
    spare, given = total - reach - (amount - 1), [1] * (amount - 1)
    while spare > 0:
        movable = [i for i in range(amount - 1) if given[i] < reach]
        pool, budget = sum([portions[i] for i in movable]), spare
        for i in movable:
            more = min(reach - given[i], max(1, budget * portions[i] // pool), spare)
            given[i] = given[i] + more
            spare = spare - more
    return np.array([reach] + given)


def ragged(stream_key, count, total, reach, slope):
    if count == 2:
        one = jax.random.randint(stream_key, (), max(1, total - reach), min(reach, total - 1) + 1)
        return jnp.stack([one, total - one])
    sizes = jnp.asarray(length_profile(count, total, reach, slope), jnp.int32)
    couples = (count - 1) // 2
    donor, receiver = sizes[1:1 + 2 * couples:2], sizes[2:2 + 2 * couples:2]
    slack = jnp.minimum(donor - 1, reach - receiver)
    moved = jax.random.randint(jax.random.fold_in(stream_key, 1), (couples,), 0, 1 << 20) % (slack + 1)
    sizes = sizes.at[1:1 + 2 * couples:2].set(donor - moved).at[2:2 + 2 * couples:2].set(receiver + moved)
    return sizes[jax.random.permutation(jax.random.fold_in(stream_key, 2), count)]


def bell_draw(stream_key, extent, deviation, most, cuts=(), kind=jnp.bfloat16):
    result = deviation * jax.random.normal(stream_key, extent, jnp.float32)
    if cuts:
        result = result * shard_levels(stream_key, extent, cuts, -0.22, 0.18)
    return jnp.clip(result, -most, most).astype(kind)


def setup_inputs(seed: int = 0) -> dict:
    streams_of = jax.random.split(jax.random.key(seed), 15)
    tokens = bell_draw(streams_of[0], (PACK_TOKENS, MODEL_WIDTH), 1.0, 6.0, ((0, 16),))
    out_grad = bell_draw(streams_of[1], (PACK_TOKENS, MODEL_WIDTH), 1.0, 6.0, ((0, 16),))
    lengths = ragged(streams_of[2], NSEQ, PACK_TOKENS, LONGEST, 2).astype(jnp.int32)
    attn_gain = jnp.clip(1.0 + 0.1 * jax.random.normal(streams_of[3], (MODEL_WIDTH,), jnp.float32), 0.5, 1.5)
    q_weight = bell_draw(streams_of[4], (MODEL_WIDTH, QUERY_HEADS * HEAD_SIZE), MODEL_WIDTH ** -0.5, 0.125, ((0, 16), (1, 2)))
    key_matrix = bell_draw(streams_of[5], (MODEL_WIDTH, KEY_VALUE_HEADS * HEAD_SIZE), MODEL_WIDTH ** -0.5, 0.125, ((0, 16), (1, 2)))
    value_matrix = bell_draw(streams_of[6], (MODEL_WIDTH, KEY_VALUE_HEADS * HEAD_SIZE), MODEL_WIDTH ** -0.5, 0.125, ((0, 16), (1, 2)))
    o_weight = bell_draw(streams_of[7], (MODEL_WIDTH, QUERY_HEADS * HEAD_SIZE), (QUERY_HEADS * HEAD_SIZE // 16) ** -0.5, 0.5, ((0, 16), (1, 2)))
    q_gain = jnp.clip(jax.random.uniform(streams_of[8], (HEAD_SIZE,), jnp.float32, 1.0, 2.0), 1.0, 2.0)
    k_gain = jnp.clip(jax.random.uniform(streams_of[9], (HEAD_SIZE,), jnp.float32, 0.75, 1.5), 0.75, 1.5)
    mlp_gain = jnp.clip(1.0 + 0.1 * jax.random.normal(streams_of[10], (MODEL_WIDTH,), jnp.float32), 0.5, 1.5)
    gate_weight = bell_draw(streams_of[11], (MODEL_WIDTH, FF), MODEL_WIDTH ** -0.5, 0.125, ((0, 16), (1, 2)))
    up_weight = bell_draw(streams_of[12], (MODEL_WIDTH, FF), MODEL_WIDTH ** -0.5, 0.125, ((0, 16), (1, 2)))
    down_weight = bell_draw(streams_of[13], (MODEL_WIDTH, FF), FF ** -0.5, 0.078125, ((0, 16), (1, 2)))
    return dict(tokens=tokens, out_grad=out_grad, lengths=lengths, attn_gain=attn_gain, q_weight=q_weight, key_matrix=key_matrix, value_matrix=value_matrix, o_weight=o_weight, q_gain=q_gain, k_gain=k_gain, mlp_gain=mlp_gain, gate_weight=gate_weight, up_weight=up_weight, down_weight=down_weight)


EPS = 1e-06
THETA = 1000000.0
MASKED = -1e+30

@jax.custom_vjp
def reduced_copy(v):
    return lax.optimization_barrier(v.astype(jnp.bfloat16)).astype(jnp.float32)

@jax.custom_vjp
def low_back(v):
    return v

def low_keep(v):
    return (reduced_copy(v), None)

def low_pass(kept, grad):
    return (grad,)

def back_keep(v):
    return (v, None)

def back_low(kept, grad):
    return (reduced_copy(grad),)
reduced_copy.defvjp(low_keep, low_pass)
low_back.defvjp(back_keep, back_low)

def matmul_high(left, right):
    return jnp.dot(left, right, precision=lax.Precision.HIGHEST, preferred_element_type=jnp.float32)

def rms_rows(values, gain_vec):
    return values * lax.rsqrt(lax.optimization_barrier(jnp.mean(values * values, axis=-1, keepdims=True)) + EPS) * gain_vec

def rotate(values):
    half_size = values.shape[-1] // 2
    return jnp.concatenate([-values[..., half_size:], values[..., :half_size]], axis=-1)

def head_prep(projected, gain_vec, cosine, sine_vals):
    heads_view = projected.reshape(projected.shape[0], -1, gain_vec.shape[0])
    normed = rms_rows(heads_view, gain_vec)
    return normed * cosine[:, None, :] + rotate(normed) * sine_vals[:, None, :]

def place_info(index, lengths):
    ends = jnp.cumsum(lengths).astype(jnp.int32)
    starts = ends - lengths
    seg_id = lax.optimization_barrier(jnp.sum((index[:, None] >= ends[None, :]).astype(jnp.int32), axis=1))
    inside = (index[:, None] >= starts[None, :]) & (index[:, None] < ends[None, :])
    position = index - lax.optimization_barrier(jnp.sum(jnp.where(inside, starts[None, :], 0), axis=1)).astype(jnp.int32)
    return (seg_id, position)

def angles(position, head_dim):
    freq = THETA ** (-(jnp.arange(0, head_dim, 2, dtype=jnp.float32) / head_dim))
    turn = position.astype(jnp.float32)[:, None] * freq[None, :]
    turn = jnp.concatenate([turn, turn], axis=-1)
    return (jnp.cos(turn), jnp.sin(turn))

def reference(tokens, out_grad, lengths, attn_gain, q_weight, key_matrix, value_matrix, o_weight, q_gain, k_gain, mlp_gain, gate_weight, up_weight, down_weight):
    index_all = jnp.arange(PACK_TOKENS, dtype=jnp.int32)
    unused_seg, position = place_info(index_all, lengths)
    cosine, sine_vals = angles(position, HEAD_SIZE)
    query_group_width = QUERY_HEADS // KEY_VALUE_HEADS
    score_factor_scale = 1.0 / math.sqrt(HEAD_SIZE)
    window_length = REACH * TOKENS_PER_SHARD

    def attention(query_reduced, key_reduced, value_reduced):
        key_padded = jnp.concatenate([jnp.zeros((window_length, KEY_VALUE_HEADS, HEAD_SIZE), jnp.float32), key_reduced], axis=0)
        value_padded = jnp.concatenate([jnp.zeros((window_length, KEY_VALUE_HEADS, HEAD_SIZE), jnp.float32), value_reduced], axis=0)

        def one_block(block_id):
            first_row_index = block_id * TOKENS_PER_SHARD
            query_row_slice = lax.dynamic_slice_in_dim(query_reduced, first_row_index, TOKENS_PER_SHARD, 0).reshape(TOKENS_PER_SHARD, KEY_VALUE_HEADS, query_group_width, HEAD_SIZE)
            key_row_slice = lax.dynamic_slice_in_dim(key_padded, first_row_index, window_length + TOKENS_PER_SHARD, 0)
            value_row_slice = lax.dynamic_slice_in_dim(value_padded, first_row_index, window_length + TOKENS_PER_SHARD, 0)
            q_index = first_row_index + jnp.arange(TOKENS_PER_SHARD, dtype=jnp.int32)
            k_index = first_row_index - window_length + jnp.arange(window_length + TOKENS_PER_SHARD, dtype=jnp.int32)
            q_seg, unused_q = place_info(q_index, lengths)
            k_seg, unused_k = place_info(k_index, lengths)
            allowed = (q_seg[:, None] == k_seg[None, :]) & (k_index[None, :] <= q_index[:, None]) & (k_index[None, :] >= 0)
            unscaled_score = jnp.einsum('cmyx,imx->myci', query_row_slice, key_row_slice, precision=lax.Precision.HIGHEST) * score_factor_scale
            score_now = low_back(jnp.where(allowed[None, None], unscaled_score, MASKED))
            row_top = lax.optimization_barrier(jnp.max(score_now, axis=-1, keepdims=True))
            exp_score = jnp.exp(score_now - row_top)
            prob_row_slice = exp_score / lax.optimization_barrier(jnp.sum(exp_score, axis=-1, keepdims=True))
            blended_heads = jnp.einsum('nlcu,une->cnle', reduced_copy(prob_row_slice), value_row_slice, precision=lax.Precision.HIGHEST)
            return blended_heads.reshape(TOKENS_PER_SHARD, QUERY_HEADS, HEAD_SIZE)
        blocks_out = lax.map(jax.checkpoint(one_block), jnp.arange(PACK_TOKENS // TOKENS_PER_SHARD, dtype=jnp.int32))
        return blocks_out.reshape(PACK_TOKENS, QUERY_HEADS, HEAD_SIZE)

    def feed_forward(second_low, w_gate, w_up, w_down):

        def mlp_one(part_rows):
            gate_pre = low_back(matmul_high(part_rows, w_gate))
            up_pre = low_back(matmul_high(part_rows, w_up))
            act_low = reduced_copy(jax.nn.silu(gate_pre) * up_pre)
            return matmul_high(act_low, w_down.T)
        parts_out = lax.map(jax.checkpoint(mlp_one), second_low.reshape(PACK_TOKENS // TOKENS_PER_SHARD, TOKENS_PER_SHARD, MODEL_WIDTH))
        return parts_out.reshape(PACK_TOKENS, MODEL_WIDTH)

    def whole_layer(x_in, attn_g, w_query, w_key, w_value, w_out, gain_q, gain_k, mlp_g, w_gate, w_up, w_down):
        first_low = reduced_copy(rms_rows(x_in, attn_g))
        q_proj = low_back(matmul_high(first_low, w_query))
        k_proj = low_back(matmul_high(first_low, w_key))
        value_projected = low_back(matmul_high(first_low, w_value))
        query_reduced = reduced_copy(head_prep(q_proj, gain_q, cosine, sine_vals))
        key_reduced = reduced_copy(head_prep(k_proj, gain_k, cosine, sine_vals))
        value_reduced = reduced_copy(value_projected).reshape(PACK_TOKENS, KEY_VALUE_HEADS, HEAD_SIZE)
        heads_all = attention(query_reduced, key_reduced, value_reduced)
        attn_low = reduced_copy(low_back(heads_all.reshape(PACK_TOKENS, QUERY_HEADS * HEAD_SIZE)))
        attn_out = low_back(matmul_high(attn_low, w_out.T))
        middle = x_in + attn_out
        second_low = reduced_copy(rms_rows(middle, mlp_g))
        mlp_out = low_back(feed_forward(second_low, w_gate, w_up, w_down))
        return middle + mlp_out
    output, pullback = jax.vjp(whole_layer, tokens.astype(jnp.float32), attn_gain, q_weight.astype(jnp.float32), key_matrix.astype(jnp.float32), value_matrix.astype(jnp.float32), o_weight.astype(jnp.float32), q_gain, k_gain, mlp_gain, gate_weight.astype(jnp.float32), up_weight.astype(jnp.float32), down_weight.astype(jnp.float32))
    grads = pullback(out_grad.astype(jnp.float32))
    return (output.astype(jnp.bfloat16), grads[0], grads[1], grads[2], grads[3], grads[4], grads[5], grads[6], grads[7], grads[8], grads[9], grads[10], grads[11])
```

```python
from functools import partial
import math

import jax
import jax.numpy as jnp
from jax import lax
from jax.experimental import pallas as pl
from jax.experimental.pallas import tpu as pltpu
from jax.sharding import PartitionSpec as P

REACH = 8
EPS = 1e-06
THETA = 1000000.0
LOG2E = 1.4426950408889634
F32 = jnp.float32
BF16 = jnp.bfloat16
VMEM_LIMIT = 60 * 1024 * 1024

NT = (((1,), (1,)), ((), ()))
NN = (((1,), (0,)), ((), ()))
TN = (((0,), (0,)), ((), ()))
MESH = pl.DeviceIdType.MESH


def dot(a, b, dims=NN):
    return lax.dot_general(a, b, dims, preferred_element_type=F32)


def over_quads(value, by):
    n = lax.axis_size("dp")
    return lax.ppermute(value, "dp", [(i, (i + 4 * by) % n) for i in range(n)])


def shift_quads(value, by):
    n = lax.axis_size("dp")
    return lax.ppermute(
        value, "dp", [(i, i + 4 * by) for i in range(n) if 0 <= i + 4 * by < n]
    )


def swap_x(value):
    return lax.ppermute(value, "dp", [(i, i ^ 2) for i in range(lax.axis_size("dp"))])


def swap_core(value):
    return lax.ppermute(value, "dp", [(i, i ^ 1) for i in range(lax.axis_size("dp"))])


def swap_tensor(value):
    return lax.ppermute(value, "tensor", [(0, 1), (1, 0)])


def tensor_sum(part):
    low = part.astype(BF16)
    return low.astype(F32) + swap_tensor(low).astype(F32)


def rms_rows(values, gain_vec):
    return values * lax.rsqrt(jnp.mean(values * values, axis=-1, keepdims=True) + EPS) * gain_vec


def rotate(values):
    half_size = values.shape[-1] // 2
    return jnp.concatenate([-values[..., half_size:], values[..., :half_size]], axis=-1)


def head_prep(heads_view, gain_vec, cosine, sine_vals):
    normed = rms_rows(heads_view, gain_vec)
    return normed * cosine[:, None, :] + rotate(normed) * sine_vals[:, None, :]


def starts_of(index, lengths):
    ends = jnp.cumsum(lengths)
    starts = ends - lengths
    inside = (index[:, None] >= starts[None, :]) & (index[:, None] < ends[None, :])
    return jnp.sum(jnp.where(inside, starts[None, :], 0), axis=1)


def angles(position, head_dim):
    freq = THETA ** (-(jnp.arange(0, head_dim, 2, dtype=F32) / head_dim))
    turn = position.astype(F32)[:, None] * freq[None, :]
    turn = jnp.concatenate([turn, turn], axis=-1)
    return (jnp.cos(turn), jnp.sin(turn))


def attn_bwd_kernel(
    rows, blocks, info, q_ref, g_ref, k_ref, v_ref, start_ref, l_ref, r_ref, dq_ref, dk_ref, dv_ref
):
    i = pl.program_id(0)
    d = k_ref.shape[1]
    scale = 1.0 / math.sqrt(d)

    @pl.when(i == 0)
    def _():
        dk_ref[...] = jnp.zeros_like(dk_ref)
        dv_ref[...] = jnp.zeros_like(dv_ref)

    dq_ref[...] = jnp.zeros_like(dq_ref)
    q2 = jnp.concatenate([q_ref[:, :d], q_ref[:, d:]], axis=0)
    g2 = jnp.concatenate([g_ref[:, :d], g_ref[:, d:]], axis=0)
    log_total = jnp.concatenate([l_ref[0:1, :], l_ref[1:2, :]], axis=1)
    row_dot = jnp.concatenate([r_ref[0:1, :], r_ref[1:2, :]], axis=1)
    q_block = info[0, i]

    def step(j, carry):
        k_block = info[1, j]
        need = (k_block <= q_block) & (k_block >= 0) & (k_block * rows + rows - 1 >= info[2, i])
        whole = (k_block < q_block) & (k_block * rows >= info[3, i])
        at = pl.ds(pl.multiple_of(j * rows, rows), rows)

        def part(masked):
            k_now = k_ref[at, :]
            score = dot(k_now, q2, NT)
            prob = jnp.exp2(score * (scale * LOG2E) - log_total)
            if masked:
                k_pos = k_block * rows + lax.broadcasted_iota(jnp.int32, (rows, rows), 0)
                q_pos = q_block * rows + lax.broadcasted_iota(jnp.int32, (rows, rows), 1)
                keep = (k_pos <= q_pos) & (k_pos >= start_ref[...])
                prob = jnp.where(jnp.concatenate([keep, keep], axis=1), prob, 0.0)
            d_prob = dot(v_ref[at, :], g2, NT)
            d_score = (prob * (d_prob - row_dot)).astype(BF16)
            dv_ref[at, :] += dot(prob.astype(BF16), g2)
            dk_ref[at, :] += dot(d_score, q2)
            d_q = dot(d_score, k_now, TN)
            dq_ref[:, :d] += d_q[:rows]
            dq_ref[:, d:] += d_q[rows:]

        pl.when(need & whole)(lambda: part(False))
        pl.when(need & jnp.logical_not(whole))(lambda: part(True))
        return carry

    lax.fori_loop(0, blocks, step, 0)


def attn_bwd(info, q, g, k, v, start, log_total, row_dot, rows):
    n_q, width = q.shape[0] // rows, q.shape[1]
    blocks = k.shape[0] // rows
    whole = lambda i, s: (0, 0)
    part = lambda i, s: (i, 0)
    row = lambda i, s: (0, i)
    return pl.pallas_call(
        partial(attn_bwd_kernel, rows, blocks),
        grid_spec=pltpu.PrefetchScalarGridSpec(
            num_scalar_prefetch=1,
            grid=(n_q,),
            in_specs=[
                pl.BlockSpec((rows, width), part),
                pl.BlockSpec((rows, width), part),
                pl.BlockSpec(k.shape, whole),
                pl.BlockSpec(v.shape, whole),
                pl.BlockSpec((1, rows), row),
                pl.BlockSpec((2, rows), row),
                pl.BlockSpec((2, rows), row),
            ],
            out_specs=[
                pl.BlockSpec((rows, width), part),
                pl.BlockSpec(k.shape, whole),
                pl.BlockSpec(k.shape, whole),
            ],
        ),
        out_shape=[
            jax.ShapeDtypeStruct(q.shape, F32),
            jax.ShapeDtypeStruct(k.shape, F32),
            jax.ShapeDtypeStruct(k.shape, F32),
        ],
        compiler_params=pltpu.CompilerParams(vmem_limit_bytes=VMEM_LIMIT),
        cost_estimate=pl.CostEstimate(flops=50 * 10**9, bytes_accessed=10**7, transcendentals=10**7),
        name="attn_bwd",
    )(info, q, g, k, v, start, log_total, row_dot)


def ffn_kernel(pieces, block, offs, s_ref, g_ref, st_ref, gt_ref, w_gate, w_up, w_down, mlp_ref, ds_ref, *grads):
    f = pl.program_id(0)

    @pl.when(f == 0)
    def _():
        mlp_ref[...] = jnp.zeros_like(mlp_ref)
        ds_ref[...] = jnp.zeros_like(ds_ref)

    s, g = s_ref[...], g_ref[...]
    gate = dot(s, w_gate[...])
    up = dot(s, w_up[...])
    d_act = dot(g, w_down[...])
    sig = 1.0 / (1.0 + jnp.exp(-gate))
    silu = gate * sig
    act = (silu * up).astype(BF16)
    d_gate = (d_act * up * sig * (1.0 + gate * (1.0 - sig))).astype(BF16)
    d_up = (d_act * silu).astype(BF16)
    mlp_ref[...] += dot(act, w_down[...], NT)
    ds_ref[...] += dot(d_gate, w_gate[...], NT) + dot(d_up, w_up[...], NT)
    half = pieces // 2
    for k, (left, right) in enumerate(((st_ref, d_gate), (st_ref, d_up), (gt_ref, act))):
        for j in range(pieces):
            at = pl.ds(pl.multiple_of(offs[j], block), block)
            grads[2 * k + j // half][j % half] = dot(left[at, :], right).astype(BF16)


def ffn_chunk(offs, s, g, st, gt, full_w, block):
    units = full_w.shape[1] // 3
    ft = min(256, units)
    n = offs.shape[0]
    tokens, width = s.shape
    steps = units // ft
    whole = lambda a: pl.BlockSpec(a.shape, lambda f, o: (0, 0))
    w_specs = [pl.BlockSpec((width, ft), lambda f, o, k=kind: (0, k * steps + f)) for kind in range(3)]
    grad_spec = pl.BlockSpec((n // 2, block, ft), lambda f, o: (0, 0, f))
    return pl.pallas_call(
        partial(ffn_kernel, n, block),
        grid_spec=pltpu.PrefetchScalarGridSpec(
            num_scalar_prefetch=1,
            grid=(steps,),
            in_specs=[whole(a) for a in (s, g, st, gt)] + w_specs,
            out_specs=[whole(s)] * 2 + [grad_spec] * 6,
        ),
        out_shape=[jax.ShapeDtypeStruct(s.shape, F32)] * 2
        + [jax.ShapeDtypeStruct((n // 2, block, units), BF16)] * 6,
        compiler_params=pltpu.CompilerParams(vmem_limit_bytes=VMEM_LIMIT),
        cost_estimate=pl.CostEstimate(
            flops=18 * tokens * width * units, bytes_accessed=10**7, transcendentals=tokens * units
        ),
        name="ffn",
    )(offs, s, g, st, gt, full_w, full_w, full_w)


class Net:
    def __init__(self, sems):
        me = lax.axis_index("dp")
        self.me, self.tensor = me, lax.axis_index("tensor")
        self.core = lax.rem(me, 2)
        self.x = lax.rem(lax.div(me, 2), 2)
        self.quad = lax.div(me, 4)
        self.quads = lax.axis_size("dp") // 4
        self.sems, self.used = sems, 0
        self.pending = []

    def sem(self):
        self.used += 1
        return self.sems.at[self.used - 1]

    def at(self, quad=None, x=None, core=None, tensor=None):
        quad = self.quad if quad is None else quad
        x = self.x if x is None else x
        core = self.core if core is None else core
        tensor = self.tensor if tensor is None else tensor
        return (quad * 4 + x * 2 + core, tensor)

    def other_core(self):
        return self.at(core=1 - self.core)

    def other_x(self):
        return self.at(x=1 - self.x)

    def other_tensor(self):
        return self.at(tensor=1 - self.tensor)

    def greet(self):
        targets = [self.other_core(), self.other_x(), self.other_tensor()]
        for s in range(1, self.quads):
            for c in range(2):
                targets.append(self.at(quad=lax.rem(self.quad + s, self.quads), core=c))
        barrier = pltpu.get_barrier_semaphore()
        for t in targets:
            pl.semaphore_signal(barrier, inc=1, device_id=t, device_id_type=MESH)
        pl.semaphore_wait(barrier, len(targets))

    def copy(self, src, dst, to, send=None, recv=None):
        return pltpu.make_async_remote_copy(
            src_ref=src,
            dst_ref=dst,
            send_sem=self.sem() if send is None else send,
            recv_sem=self.sem() if recv is None else recv,
            device_id=to,
            device_id_type=MESH,
        )

    def send(self, src, dst, to):
        c = self.copy(src, dst, to)
        c.start()
        self.pending.append(c.wait_send)
        return c

    def keep(self, src, dst):
        c = pltpu.make_async_copy(src, dst, self.sem())
        c.start()
        self.pending.append(c.wait)
        return c

    def finish(self):
        for wait in self.pending:
            wait()
        self.pending = []


def wait_bytes(ref, sem):
    pltpu.make_async_copy(ref, ref, sem).wait()


class Gather:
    def __init__(self, net, full, shard, kinds):
        self.net, self.full, self.shard, self.kinds = net, full, shard, kinds
        self.z_sem = [net.sem() for _ in range(net.quads)]
        self.x_sem = [net.sem() for _ in range(net.quads)]
        self.z_sent, self.x_sent, self.own = net.sem(), net.sem(), net.sem()

    def rows(self, s, x):
        n = self.net
        at = (lax.rem(n.quad + n.quads - s, n.quads) * 4 + 2 * x) * self.shard
        return self.full.at[pl.ds(pl.multiple_of(at, self.shard), 2 * self.shard)]

    def start(self):
        n = self.net
        mine = pl.ds(pl.multiple_of(n.me * self.shard, self.shard), self.shard)
        for arr, first, wide, into in self.kinds:
            half = arr.shape[1] // 2
            there = self.full.at[mine, pl.ds(into, wide)]

            def cut(core):
                return arr.at[:, pl.ds(pl.multiple_of(core * half + first, 128), wide)]

            pltpu.make_async_copy(cut(n.core), there, self.own).start()
            n.copy(cut(1 - n.core), there, n.other_core(), self.z_sent, self.z_sem[0]).start()
            for s in range(1, n.quads):
                to = lax.rem(n.quad + s, n.quads)
                for c in range(2):
                    n.copy(cut(c), there, n.at(quad=to, core=c), self.z_sent, self.z_sem[s]).start()

    def forward(self, s):
        n = self.net
        if s == 0:
            half = self.full.at[pl.ds(0, self.shard)]
            wait_bytes(half, self.own)
            wait_bytes(half, self.z_sem[0])
        else:
            wait_bytes(self.rows(s, n.x), self.z_sem[s])
        block = self.rows(s, n.x)
        n.copy(block, block, n.other_x(), self.x_sent, self.x_sem[s]).start()

    def forward_all(self):
        for s in range(self.net.quads):
            self.forward(s)

    def arrived(self):
        n = self.net
        for s in range(n.quads):
            wait_bytes(self.rows(s, 1 - n.x), self.x_sem[s])

    def finish(self):
        q = self.net.quads
        wait_bytes(self.full.at[pl.ds(0, (2 * q - 1) * self.shard)], self.z_sent)
        wait_bytes(self.full.at[pl.ds(0, 2 * q * self.shard)], self.x_sent)


def forward_kernel(
    tokens,
    out_grad,
    attn_gain,
    mlp_gain,
    q_gain,
    k_gain,
    cosine,
    sine,
    start,
    wq,
    wk,
    wv,
    wo,
    wg,
    wu,
    wd,
    first_out,
    grad_out,
    proj_out,
    plane_out,
    k_out,
    v_out,
    heads_out,
    stat_out,
    attn_out,
    middle_out,
    second_out,
    qkv_full,
    o_full,
    ff0,
    ff1,
    ff2,
    sems,
    first,
    w_qkv,
    proj,
    low,
    plane,
    kx,
    vx,
    acc,
    heads,
    stat,
    attn,
    w_o,
    core_send,
    core_recv,
    low_send,
    low_recv,
    middle,
    second,
):
    n = Net(sems)
    rows, width = tokens.shape
    d = q_gain.shape[1]
    shard = wq.shape[0]
    units = ff0.shape[1] // 3
    my_rows = pl.ds(pl.multiple_of(n.core * rows, rows), rows)
    chip_rows = pl.ds(pl.multiple_of(n.x * 2 * rows, 2 * rows), 2 * rows)
    back = kx.shape[0] - 1
    n.greet()

    qkv = Gather(n, qkv_full, shard, [(wq, 0, 4 * d, 0), (wk, 0, 2 * d, 4 * d), (wv, 0, 2 * d, 6 * d)])
    o_w = Gather(n, o_full, shard, [(wo, 0, 4 * d, 0)])
    ff = [
        Gather(
            n,
            full,
            shard,
            [(wg, i * units, units, 0), (wu, i * units, units, units), (wd, i * units, units, 2 * units)],
        )
        for i, full in enumerate((ff0, ff1, ff2))
    ]
    qkv.start()
    o_w.start()

    step = 128

    def norm_first(i, carry):
        at = pl.ds(pl.multiple_of(i * step, step), step)
        to = pl.ds(pl.multiple_of(n.core * rows + i * step, step), step)
        first[to, :] = rms_rows(tokens[at, :].astype(F32), attn_gain[...]).astype(BF16)
        return carry

    lax.fori_loop(0, rows // step, norm_first, 0)
    first_copy = n.send(first.at[my_rows], first.at[my_rows], n.other_core())
    grad_copy = n.send(out_grad, grad_out.at[my_rows], n.other_core())
    n.keep(out_grad, grad_out.at[my_rows])
    vx[:, :, d:] = jnp.ones(vx.shape[:2] + (d,), BF16)
    acc[...] = jnp.zeros_like(acc)

    qkv.forward_all()
    first_copy.wait_recv()
    o_w.forward_all()
    ff[0].start()
    qkv.arrived()
    load = pltpu.make_async_copy(qkv_full, w_qkv, n.sem())
    load.start()
    load.wait()

    tall = 256

    def project(i, carry):
        at = pl.ds(pl.multiple_of(i * tall, tall), tall)
        proj[at, :] = dot(first[at, :], w_qkv[...])
        cos, sin = cosine[at, :], sine[at, :]

        def prep(col, gain):
            u = proj[at, pl.ds(col, d)]
            u = rms_rows(u, gain[...])
            return (u * cos + pltpu.roll(u, d // 2, 1) * sin).astype(BF16)

        for h in range(2):
            for g in range(2):
                low[h, at, pl.ds(g * d, d)] = prep((2 * h + g) * d, q_gain)
            low[h, at, pl.ds(2 * d, d)] = prep((4 + h) * d, k_gain)
            low[h, at, pl.ds(3 * d, d)] = proj[at, pl.ds((6 + h) * d, d)].astype(BF16)
        return carry

    lax.fori_loop(0, 2 * rows // tall, project, 0)
    head_copy = n.send(low.at[1 - n.x], plane.at[chip_rows], n.other_x())
    n.keep(proj, proj_out)
    plane[chip_rows, :] = low[n.x]
    head_copy.wait_recv()
    kx[0] = plane[:, 2 * d : 3 * d]
    vx[0, :, :d] = plane[:, 3 * d :]
    n.keep(plane, plane_out)

    ahead = n.at(quad=jnp.minimum(n.quad + 1, n.quads - 1))
    hops = []
    for h in range(back):
        hops.append(
            [
                n.copy(kx.at[h], kx.at[h + 1], ahead),
                n.copy(vx.at[h, :, pl.ds(0, d)], vx.at[h + 1, :, pl.ds(0, d)], ahead),
            ]
        )

    def hop_start(h):
        @pl.when((n.quad >= h) & (n.quad < n.quads - 1))
        def _():
            for c in hops[h]:
                c.start()

    def hop_sent(h):
        @pl.when((n.quad >= h) & (n.quad < n.quads - 1))
        def _():
            for c in hops[h]:
                c.wait_send()

    def hop_arrived(h):
        @pl.when(n.quad >= h + 1)
        def _():
            for c in hops[h]:
                c.wait_recv()

    factor = LOG2E / math.sqrt(d)

    def attend(h, i, j):
        q_at = pl.ds(pl.multiple_of(i * rows, rows), rows)
        k_at = pl.ds(pl.multiple_of(j * rows, rows), rows)
        q2 = jnp.concatenate([plane[q_at, pl.ds(0, d)], plane[q_at, pl.ds(d, d)]], axis=0)
        prob = jnp.exp2(dot(q2, kx[h, k_at, :], NT) * factor)
        k_pos = (4 * (n.quad - h) + j) * rows + lax.broadcasted_iota(jnp.int32, (rows, rows), 1)
        keep = k_pos >= start[q_at, :]
        if h == 0:
            q_pos = (4 * n.quad + i) * rows + lax.broadcasted_iota(jnp.int32, (rows, rows), 0)
            keep = keep & (k_pos <= q_pos)
        prob = jnp.where(jnp.concatenate([keep, keep], axis=0), prob, 0.0)
        acc[i] += dot(prob.astype(BF16), vx[h, k_at, :])

    def sweep(h, i, lo, hi):
        def body(j, carry):
            attend(h, i, j)
            return carry

        lax.fori_loop(lo, hi, body, 0)

    def over_q(fn):
        def body(i, carry):
            fn(i)
            return carry

        lax.fori_loop(0, 4, body, 0)

    hop_start(0)
    over_q(lambda i: sweep(0, i, 0, i + 1))
    hop_arrived(0)
    hop_start(1)

    @pl.when(n.quad >= 1)
    def _():
        over_q(lambda i: sweep(1, i, 0, 4))

    ff[0].forward_all()
    ff[1].start()
    hop_arrived(1)

    @pl.when(n.quad >= 2)
    def _():
        over_q(lambda i: sweep(2, i, i, 4))

    for i in range(4):
        at = pl.ds(i * rows, rows)
        total = acc[i, :, d:]
        done = acc[i, :, :d] / total
        heads[at, pl.ds(0, d)] = done[:rows]
        heads[at, pl.ds(d, d)] = done[rows:]
        logs = jnp.log2(total)
        stat[0:1, pl.ds(i * rows, rows)] = logs[:rows].T[0:1]
        stat[1:2, pl.ds(i * rows, rows)] = logs[rows:].T[0:1]
    theirs = pl.ds(pl.multiple_of((1 - n.x) * 2 * rows, 2 * rows), 2 * rows)
    plane_attn = low.at[0, :, pl.ds(0, 2 * d)]
    head_copy.wait_send()
    n.pending.remove(head_copy.wait_send)
    low[0, :, : 2 * d] = heads[theirs, :].astype(BF16)
    attn_copy = n.send(plane_attn, attn.at[n.x], n.other_x())
    attn[n.x] = heads[chip_rows, :].astype(BF16)
    n.keep(heads, heads_out)
    n.keep(stat, stat_out)
    for h in range(back + 1):
        n.keep(kx.at[h], k_out.at[pl.ds(h * 4 * rows, 4 * rows)])
        n.keep(vx.at[h, :, pl.ds(0, d)], v_out.at[pl.ds(h * 4 * rows, 4 * rows)])
    o_w.arrived()
    load_o = pltpu.make_async_copy(o_full, w_o, n.sem())
    load_o.start()
    load_o.wait()
    attn_copy.wait_recv()
    n.keep(attn, attn_out)

    def o_rows(at):
        return dot(attn[0, at, :], w_o[:, : 2 * d], NT) + dot(attn[1, at, :], w_o[:, 2 * d :], NT)

    parts = rows // step
    core_copies, low_copies, second_copies = [], [], []
    for i in range(parts):
        at = pl.ds(i * step, step)
        core_send[at, :] = o_rows(
            pl.ds(pl.multiple_of((1 - n.core) * rows + i * step, step), step)
        ).astype(BF16)
        core_copies.append(n.send(core_send.at[at], core_recv.at[at], n.other_core()))
    for i in range(parts):
        at = pl.ds(i * step, step)
        part = o_rows(pl.ds(pl.multiple_of(n.core * rows + i * step, step), step))
        core_copies[i].wait_recv()
        low_send[at, :] = (part + core_recv[at, :].astype(F32)).astype(BF16)
        low_copies.append(n.send(low_send.at[at], low_recv.at[at], n.other_tensor()))
    ff[1].forward_all()
    ff[2].start()
    for i in range(parts):
        at = pl.ds(i * step, step)
        low_copies[i].wait_recv()
        mid = tokens[at, :].astype(F32) + (low_send[at, :].astype(F32) + low_recv[at, :].astype(F32))
        middle[at, :] = mid
        to = pl.ds(pl.multiple_of(n.core * rows + i * step, step), step)
        second[to, :] = rms_rows(mid, mlp_gain[...]).astype(BF16)
        second_copies.append(n.send(second.at[to], second.at[to], n.other_core()))
    n.keep(middle, middle_out)
    n.keep(first, first_out)
    for c in second_copies:
        c.wait_recv()
    n.keep(second, second_out)
    grad_copy.wait_recv()
    ff[2].forward_all()
    for g in ff:
        g.arrived()
    for h in range(back):
        hop_sent(h)
    n.finish()
    for g in [qkv, o_w] + ff:
        g.finish()


def forward(tokens, out_grad, attn_gain, mlp_gain, q_gain, k_gain, cosine, sine, start, *weights):
    rows, width = tokens.shape
    d = q_gain.shape[0]
    wq, wg = weights[0], weights[4]
    quads = lax.axis_size("dp") // 4
    back = REACH // 4
    units = wg.shape[1] // 2 // 3
    vmem = pl.BlockSpec(memory_space=pltpu.VMEM)
    hbm = pl.BlockSpec(memory_space=pl.ANY)
    shape = jax.ShapeDtypeStruct
    return pl.pallas_call(
        forward_kernel,
        in_specs=[vmem, hbm] + [vmem] * 7 + [hbm] * 7,
        out_specs=[hbm] * 16,
        out_shape=[
            shape((2 * rows, width), BF16),
            shape((2 * rows, width), BF16),
            shape((2 * rows, 8 * d), F32),
            shape((4 * rows, 4 * d), BF16),
            shape((4 * rows * (back + 1), d), BF16),
            shape((4 * rows * (back + 1), d), BF16),
            shape((4 * rows, 2 * d), F32),
            shape((2, 4 * rows), F32),
            shape((2, 2 * rows, 2 * d), BF16),
            shape((rows, width), F32),
            shape((2 * rows, width), BF16),
            shape((width, 8 * d), BF16),
            shape((width, 4 * d), BF16),
        ]
        + [shape((width, 3 * units), BF16)] * 3,
        scratch_shapes=[
            pltpu.SemaphoreType.DMA((80 + 5 * (2 * quads + 3),)),
            pltpu.VMEM((2 * rows, width), BF16),
            pltpu.VMEM((width, 8 * d), BF16),
            pltpu.VMEM((2 * rows, 8 * d), F32),
            pltpu.VMEM((2, 2 * rows, 4 * d), BF16),
            pltpu.VMEM((4 * rows, 4 * d), BF16),
            pltpu.VMEM((back + 1, 4 * rows, d), BF16),
            pltpu.VMEM((back + 1, 4 * rows, 2 * d), BF16),
            pltpu.VMEM((4, 2 * rows, 2 * d), F32),
            pltpu.VMEM((4 * rows, 2 * d), F32),
            pltpu.VMEM((2, 4 * rows), F32),
            pltpu.VMEM((2, 2 * rows, 2 * d), BF16),
            pltpu.VMEM((width, 4 * d), BF16),
            pltpu.VMEM((rows, width), BF16),
            pltpu.VMEM((rows, width), BF16),
            pltpu.VMEM((rows, width), BF16),
            pltpu.VMEM((rows, width), BF16),
            pltpu.VMEM((rows, width), F32),
            pltpu.VMEM((2 * rows, width), BF16),
        ],
        compiler_params=pltpu.CompilerParams(
            collective_id=0, has_side_effects=True, vmem_limit_bytes=VMEM_LIMIT
        ),
        name="forward",
    )(
        tokens,
        out_grad,
        attn_gain[None],
        mlp_gain[None],
        q_gain[None],
        k_gain[None],
        cosine,
        sine,
        start,
        *weights,
    )


def local(
    tokens,
    out_grad,
    lengths,
    attn_gain,
    q_weight,
    key_matrix,
    value_matrix,
    o_weight,
    q_gain,
    k_gain,
    mlp_gain,
    gate_weight,
    up_weight,
    down_weight,
):
    rows, width = tokens.shape
    d = q_gain.shape[0]
    devices = lax.axis_size("dp")
    quads = devices // 4
    me = lax.axis_index("dp")
    quad, x, core = me // 4, (me // 2) % 2, me % 2
    shard = q_weight.shape[0]
    block = 2 * shard
    kv_here = key_matrix.shape[1] // d
    group = q_weight.shape[1] // key_matrix.shape[1]
    assert kv_here == 4 and group == 2

    def pick(arr, index, count, axis):
        size = arr.shape[axis] // count
        return lax.dynamic_slice_in_dim(arr, index * size, size, axis)

    def ordered(mine, other, flag, axis):
        return jnp.where(
            flag == 0,
            jnp.concatenate([mine, other], axis),
            jnp.concatenate([other, mine], axis),
        )

    offs = jnp.stack(
        [
            ((quad - s) % quads) * 2 * block + jnp.where(xr == 0, x, 1 - x) * block
            for xr in range(2)
            for s in range(quads)
        ]
    ).astype(jnp.int32)

    def both(mine_rows):
        return ordered(mine_rows, swap_core(mine_rows), core, 0)

    chip_index = (me // 2) * 2 * rows + jnp.arange(2 * rows, dtype=jnp.int32)
    cosine, sine_vals = angles(chip_index - starts_of(chip_index, lengths), d)
    sine_signed = jnp.concatenate([-sine_vals[:, : d // 2], sine_vals[:, d // 2 :]], 1)
    q_index = quad * 4 * rows + jnp.arange(4 * rows, dtype=jnp.int32)
    q_start = starts_of(q_index, lengths)
    tokens_wide = tokens.astype(F32)
    (
        first_chip,
        grad_chip,
        proj,
        plane,
        k_all,
        v_all,
        heads_out,
        log_total,
        attn_halves,
        middle,
        second_chip,
        qkv_full,
        o_full,
        *ff_full,
    ) = forward(
        tokens,
        out_grad,
        attn_gain,
        mlp_gain,
        q_gain,
        k_gain,
        cosine,
        sine_signed,
        q_start[:, None],
        q_weight,
        key_matrix,
        value_matrix,
        o_weight,
        gate_weight,
        up_weight,
        down_weight,
    )
    q_plane = plane[:, : group * d]
    attn_low = jnp.concatenate([attn_halves[0], attn_halves[1]], 1)
    back_hops = REACH // 4
    q_blocks = 4 * quad + jnp.arange(4)
    k_blocks = jnp.concatenate([q_blocks - 4 * h for h in range(back_hops + 1)])
    by_block = q_start.reshape(-1, rows)
    lanes = k_blocks.shape[0]
    info = jnp.stack(
        [
            jnp.pad(v, (0, lanes - v.shape[0]))
            for v in (q_blocks, k_blocks, by_block[:, 0], by_block[:, -1])
        ]
    ).astype(jnp.int32)

    def prep_q(p, gain):
        return head_prep(p.reshape(2 * rows, 2 * group, d), gain, cosine, sine_vals)

    def prep_k(p, gain):
        return head_prep(p.reshape(2 * rows, 2, d), gain, cosine, sine_vals)

    q_in, k_in = proj[:, : 4 * d], proj[:, 4 * d : 6 * d]

    def core_sum(part):
        low_part = pick(part, 1 - core, 2, 0).astype(BF16)
        return pick(part, core, 2, 0) + swap_core(low_part).astype(F32)

    second_t, grad_t = second_chip.T, grad_chip.T

    def scatter(keep, send):
        got = swap_x(send)
        sums = [
            (keep[s].astype(F32) + got[s].astype(F32)).astype(BF16) for s in range(quads)
        ]
        total = sums[0].astype(F32)
        for s in range(1, quads):
            total = total + over_quads(sums[s], -s).astype(F32)
        return total

    def to_cores(total):
        own = pick(total, core, 2, 0)
        return ordered(own, swap_core(pick(total, 1 - core, 2, 0)), core, 1)

    ff_grads = [[], [], []]
    mlp_part, d_second_part = 0.0, 0.0
    for full_w in ff_full:
        got = ffn_chunk(offs, second_chip, grad_chip, second_t, grad_t, full_w, block)
        mlp_part, d_second_part = mlp_part + got[0], d_second_part + got[1]
        for n in range(3):
            ff_grads[n].append(scatter(got[2 + 2 * n], got[3 + 2 * n]))
    grad_gate, grad_up, grad_down = (to_cores(jnp.concatenate(g, 1)) for g in ff_grads)

    d_second = tensor_sum(core_sum(d_second_part))
    mlp_out = tensor_sum(core_sum(mlp_part))
    output = (middle + mlp_out).astype(BF16)
    unused_mid, norm_back_mid = jax.vjp(rms_rows, middle, mlp_gain)
    d_middle_norm, grad_mlp_local = norm_back_mid(d_second)
    d_middle = out_grad.astype(F32) + d_middle_norm
    d_attn = both(d_middle.astype(BF16))

    def split_rows(grad):
        by = grad.reshape(quads, 2, block, -1)
        order = (quad - jnp.arange(quads)) % quads
        keep = lax.dynamic_index_in_dim(by, x, 1, False)
        send = lax.dynamic_index_in_dim(by, 1 - x, 1, False)

        def rel(a):
            return [lax.dynamic_index_in_dim(a, order[s], 0, False) for s in range(quads)]

        return jnp.stack(rel(keep)), jnp.stack(rel(send))

    grad_o = to_cores(scatter(*split_rows(dot(d_attn, attn_low, TN).astype(BF16))))
    d_heads = dot(d_attn, o_full).astype(BF16)
    d_heads_plane = ordered(pick(d_heads, x, 2, 1), swap_x(pick(d_heads, 1 - x, 2, 1)), x, 0)
    row_dot = jnp.sum(
        (d_heads_plane.astype(F32) * heads_out).reshape(4 * rows, group, d), axis=-1
    ).T
    d_q, d_k, d_v = attn_bwd(
        info, q_plane, d_heads_plane, k_all, v_all, q_start[None, :], log_total, row_dot, rows
    )
    scale = 1.0 / math.sqrt(d)
    d_kv = jnp.concatenate([d_k * scale, d_v], 1).reshape(back_hops + 1, 4 * rows, 2 * d)
    carried = d_kv[back_hops]
    for h in reversed(range(back_hops)):
        carried = d_kv[h] + shift_quads(carried.astype(BF16), -1).astype(F32)
    d_plane = jnp.concatenate([d_q * scale, carried], 1)
    d_mine = pick(d_plane, x, 2, 0)
    d_back = swap_x(pick(d_plane, 1 - x, 2, 0).astype(BF16)).astype(F32)
    d_low = jnp.where(x == 0, jnp.stack([d_mine, d_back], 1), jnp.stack([d_back, d_mine], 1))
    unused_q, q_back = jax.vjp(prep_q, q_in, q_gain)
    d_q_proj, q_gain_local = q_back(d_low[:, :, : group * d].reshape(2 * rows, 2 * group, d))
    unused_k, k_back = jax.vjp(prep_k, k_in, k_gain)
    d_k_proj, k_gain_local = k_back(d_low[:, :, group * d : (group + 1) * d])
    d_proj = jnp.concatenate(
        [d_q_proj, d_k_proj, d_low[:, :, (group + 1) * d :].reshape(2 * rows, -1)], 1
    ).astype(BF16)
    grad_qkv = scatter(*split_rows(dot(first_chip, d_proj, TN).astype(BF16)))
    grad_q = to_cores(grad_qkv[:, : 4 * d])
    grad_k = to_cores(grad_qkv[:, 4 * d : 6 * d])
    grad_v = to_cores(grad_qkv[:, 6 * d :])
    d_first = tensor_sum(core_sum(dot(d_proj, qkv_full, NT)))
    unused_in, norm_back_in = jax.vjp(rms_rows, tokens_wide, attn_gain)
    d_tokens_norm, grad_attn_local = norm_back_in(d_first)
    input_grad = d_middle + d_tokens_norm
    grad_attn_gain, grad_mlp_gain, grad_q_gain, grad_k_gain = lax.psum(
        (0.5 * grad_attn_local, 0.5 * grad_mlp_local, q_gain_local, k_gain_local),
        ("dp", "tensor"),
    )
    return (
        output,
        input_grad,
        grad_attn_gain,
        grad_q,
        grad_k,
        grad_v,
        grad_o,
        grad_q_gain,
        grad_k_gain,
        grad_mlp_gain,
        grad_gate,
        grad_up,
        grad_down,
    )


def solution(mesh):
    rows, weight = P("dp", None), P("dp", "tensor")
    placed = (
        (rows, rows) + (P(),) * 2 + (weight,) * 4 + (P(),) * 3 + (weight,) * 3
    )
    return jax.shard_map(
        local,
        mesh=mesh,
        in_specs=placed,
        out_specs=(rows, rows, P()) + (weight,) * 4 + (P(),) * 3 + (weight,) * 3,
        check_vma=False,
    )
```

```python
from functools import partial
import math

import jax
import jax.numpy as jnp
from jax import lax
from jax.experimental import pallas as pl
from jax.experimental.pallas import tpu as pltpu
from jax.sharding import PartitionSpec as P

REACH = 8
EPS = 1e-06
THETA = 1000000.0
LOG2E = 1.4426950408889634
F32 = jnp.float32
BF16 = jnp.bfloat16
VMEM_LIMIT = 60 * 1024 * 1024

NT = (((1,), (1,)), ((), ()))
NN = (((1,), (0,)), ((), ()))
TN = (((0,), (0,)), ((), ()))
MESH = pl.DeviceIdType.MESH


def dot(a, b, dims=NN):
    return lax.dot_general(a, b, dims, preferred_element_type=F32)


def over_quads(value, by):
    n = lax.axis_size("dp")
    return lax.ppermute(value, "dp", [(i, (i + 4 * by) % n) for i in range(n)])


def shift_quads(value, by):
    n = lax.axis_size("dp")
    return lax.ppermute(
        value, "dp", [(i, i + 4 * by) for i in range(n) if 0 <= i + 4 * by < n]
    )


def swap_x(value):
    return lax.ppermute(value, "dp", [(i, i ^ 2) for i in range(lax.axis_size("dp"))])


def swap_core(value):
    return lax.ppermute(value, "dp", [(i, i ^ 1) for i in range(lax.axis_size("dp"))])


def swap_tensor(value):
    return lax.ppermute(value, "tensor", [(0, 1), (1, 0)])


def tensor_sum(part):
    low = part.astype(BF16)
    return low.astype(F32) + swap_tensor(low).astype(F32)


def rms_rows(values, gain_vec):
    return values * lax.rsqrt(jnp.mean(values * values, axis=-1, keepdims=True) + EPS) * gain_vec


def rotate(values):
    half_size = values.shape[-1] // 2
    return jnp.concatenate([-values[..., half_size:], values[..., :half_size]], axis=-1)


def head_prep(heads_view, gain_vec, cosine, sine_vals):
    normed = rms_rows(heads_view, gain_vec)
    return normed * cosine[:, None, :] + rotate(normed) * sine_vals[:, None, :]


def starts_of(index, lengths):
    ends = jnp.cumsum(lengths)
    starts = ends - lengths
    inside = (index[:, None] >= starts[None, :]) & (index[:, None] < ends[None, :])
    return jnp.sum(jnp.where(inside, starts[None, :], 0), axis=1)


def angles(position, head_dim):
    freq = THETA ** (-(jnp.arange(0, head_dim, 2, dtype=F32) / head_dim))
    turn = position.astype(F32)[:, None] * freq[None, :]
    turn = jnp.concatenate([turn, turn], axis=-1)
    return (jnp.cos(turn), jnp.sin(turn))


class Net:
    def __init__(self, sems):
        me = lax.axis_index("dp")
        self.me, self.tensor = me, lax.axis_index("tensor")
        self.core = lax.rem(me, 2)
        self.x = lax.rem(lax.div(me, 2), 2)
        self.quad = lax.div(me, 4)
        self.quads = lax.axis_size("dp") // 4
        self.sems, self.used = sems, 0
        self.pending = []
        self.to_core = self.at(core=1 - self.core)
        self.to_x = self.at(x=1 - self.x)
        self.to_tensor = self.at(tensor=1 - self.tensor)

    def sem(self):
        self.used += 1
        return self.sems.at[self.used - 1]

    def at(self, quad=None, x=None, core=None, tensor=None):
        quad = self.quad if quad is None else quad
        x = self.x if x is None else x
        core = self.core if core is None else core
        tensor = self.tensor if tensor is None else tensor
        return (quad * 4 + x * 2 + core, tensor)

    def other_core(self):
        return self.to_core

    def other_x(self):
        return self.to_x

    def other_tensor(self):
        return self.to_tensor

    def greet(self):
        targets = [self.other_core(), self.other_x(), self.other_tensor()]
        for s in range(1, self.quads):
            for c in range(2):
                targets.append(self.at(quad=lax.rem(self.quad + s, self.quads), core=c))
        barrier = pltpu.get_barrier_semaphore()
        for t in targets:
            pl.semaphore_signal(barrier, inc=1, device_id=t, device_id_type=MESH)
        pl.semaphore_wait(barrier, len(targets))

    def copy(self, src, dst, to, send=None, recv=None):
        return pltpu.make_async_remote_copy(
            src_ref=src,
            dst_ref=dst,
            send_sem=self.sem() if send is None else send,
            recv_sem=self.sem() if recv is None else recv,
            device_id=to,
            device_id_type=MESH,
        )

    def send(self, src, dst, to):
        c = self.copy(src, dst, to)
        c.start()
        self.pending.append(c.wait_send)
        return c

    def keep(self, src, dst):
        c = pltpu.make_async_copy(src, dst, self.sem())
        c.start()
        self.pending.append(c.wait)
        return c

    def finish(self):
        for wait in self.pending:
            wait()
        self.pending = []


def wait_bytes(ref, sem):
    pltpu.make_async_copy(ref, ref, sem).wait()


class Gather:
    def __init__(self, net, full, shard, kinds):
        self.net, self.full, self.shard, self.kinds = net, full, shard, kinds
        self.z_sem = [net.sem() for _ in range(net.quads)]
        self.x_sem = [net.sem() for _ in range(net.quads)]
        self.z_sent, self.x_sent, self.own = net.sem(), net.sem(), net.sem()

    def rows(self, s, x):
        n = self.net
        at = (lax.rem(n.quad + n.quads - s, n.quads) * 4 + 2 * x) * self.shard
        return self.full.at[pl.ds(pl.multiple_of(at, self.shard), 2 * self.shard)]

    def start(self):
        n = self.net
        mine = pl.ds(pl.multiple_of(n.me * self.shard, self.shard), self.shard)
        for arr, first, wide, into in self.kinds:
            half = arr.shape[1] // 2
            there = self.full.at[mine, pl.ds(into, wide)]

            def cut(core):
                return arr.at[:, pl.ds(pl.multiple_of(core * half + first, 128), wide)]

            pltpu.make_async_copy(cut(n.core), there, self.own).start()
            n.copy(cut(1 - n.core), there, n.other_core(), self.z_sent, self.z_sem[0]).start()
            for s in range(1, n.quads):
                to = lax.rem(n.quad + s, n.quads)
                for c in range(2):
                    n.copy(cut(c), there, n.at(quad=to, core=c), self.z_sent, self.z_sem[s]).start()

    def forward(self, s):
        n = self.net
        if s == 0:
            half = self.full.at[pl.ds(0, self.shard)]
            wait_bytes(half, self.own)
            wait_bytes(half, self.z_sem[0])
        else:
            wait_bytes(self.rows(s, n.x), self.z_sem[s])
        block = self.rows(s, n.x)
        n.copy(block, block, n.other_x(), self.x_sent, self.x_sem[s]).start()

    def forward_all(self):
        for s in range(self.net.quads):
            self.forward(s)

    def arrived(self):
        n = self.net
        for s in range(n.quads):
            wait_bytes(self.rows(s, 1 - n.x), self.x_sem[s])

    def finish(self):
        q = self.net.quads
        wait_bytes(self.full.at[pl.ds(0, (2 * q - 1) * self.shard)], self.z_sent)
        wait_bytes(self.full.at[pl.ds(0, 2 * q * self.shard)], self.x_sent)


def forward_kernel(
    tokens,
    out_grad,
    attn_gain,
    mlp_gain,
    q_gain,
    k_gain,
    cosine,
    sine,
    start,
    wq,
    wk,
    wv,
    wo,
    wg,
    wu,
    wd,
    first_out,
    grad_out,
    proj_out,
    plane_out,
    k_out,
    v_out,
    heads_out,
    stat_out,
    attn_out,
    middle_out,
    second_out,
    qkv_full,
    o_full,
    ff_full,
    sems,
    first,
    w_qkv,
    proj,
    low,
    plane,
    kx,
    vx,
    acc,
    heads,
    stat,
    attn,
    w_o,
    core_send,
    core_recv,
    low_send,
    low_recv,
    middle,
    second,
):
    n = Net(sems)
    rows, width = tokens.shape
    d = q_gain.shape[1]
    shard = wq.shape[0]
    units = ff_full.shape[2] // 3
    my_rows = pl.ds(pl.multiple_of(n.core * rows, rows), rows)
    chip_rows = pl.ds(pl.multiple_of(n.x * 2 * rows, 2 * rows), 2 * rows)
    back = kx.shape[0] - 1
    n.greet()

    qkv = Gather(n, qkv_full, shard, [(wq, 0, 4 * d, 0), (wk, 0, 2 * d, 4 * d), (wv, 0, 2 * d, 6 * d)])
    o_w = Gather(n, o_full, shard, [(wo, 0, 4 * d, 0)])
    ff = [
        Gather(
            n,
            ff_full.at[i],
            shard,
            [(wg, i * units, units, 0), (wu, i * units, units, units), (wd, i * units, units, 2 * units)],
        )
        for i in range(ff_full.shape[0])
    ]
    qkv.start()
    o_w.start()

    step = 128

    def norm_first(i, carry):
        at = pl.ds(pl.multiple_of(i * step, step), step)
        to = pl.ds(pl.multiple_of(n.core * rows + i * step, step), step)
        first[to, :] = rms_rows(tokens[at, :].astype(F32), attn_gain[...]).astype(BF16)
        return carry

    lax.fori_loop(0, rows // step, norm_first, 0)
    first_copy = n.send(first.at[my_rows], first.at[my_rows], n.other_core())
    grad_copy = n.send(out_grad, grad_out.at[my_rows], n.other_core())
    n.keep(out_grad, grad_out.at[my_rows])
    vx[:, :, d:] = jnp.ones(vx.shape[:2] + (d,), BF16)
    acc[...] = jnp.zeros_like(acc)

    qkv.forward_all()
    first_copy.wait_recv()
    o_w.forward_all()
    ff[0].start()
    qkv.arrived()
    load = pltpu.make_async_copy(qkv_full, w_qkv, n.sem())
    load.start()
    load.wait()

    tall = 256

    def project(i, carry):
        at = pl.ds(pl.multiple_of(i * tall, tall), tall)
        proj[at, :] = dot(first[at, :], w_qkv[...])
        cos, sin = cosine[at, :], sine[at, :]

        def prep(col, gain):
            u = proj[at, pl.ds(col, d)]
            u = rms_rows(u, gain[...])
            return (u * cos + pltpu.roll(u, d // 2, 1) * sin).astype(BF16)

        for h in range(2):
            for g in range(2):
                low[h, at, pl.ds(g * d, d)] = prep((2 * h + g) * d, q_gain)
            low[h, at, pl.ds(2 * d, d)] = prep((4 + h) * d, k_gain)
            low[h, at, pl.ds(3 * d, d)] = proj[at, pl.ds((6 + h) * d, d)].astype(BF16)
        return carry

    lax.fori_loop(0, 2 * rows // tall, project, 0)
    head_copy = n.send(low.at[1 - n.x], plane.at[chip_rows], n.other_x())
    n.keep(proj, proj_out)
    plane[chip_rows, :] = low[n.x]
    head_copy.wait_recv()
    kx[0] = plane[:, 2 * d : 3 * d]
    vx[0, :, :d] = plane[:, 3 * d :]
    n.keep(plane, plane_out)

    ahead = n.at(quad=jnp.minimum(n.quad + 1, n.quads - 1))
    hops = []
    for h in range(back):
        hops.append(
            [
                n.copy(kx.at[h], kx.at[h + 1], ahead),
                n.copy(vx.at[h, :, pl.ds(0, d)], vx.at[h + 1, :, pl.ds(0, d)], ahead),
            ]
        )

    def hop_start(h):
        @pl.when((n.quad >= h) & (n.quad < n.quads - 1))
        def _():
            for c in hops[h]:
                c.start()

    def hop_sent(h):
        @pl.when((n.quad >= h) & (n.quad < n.quads - 1))
        def _():
            for c in hops[h]:
                c.wait_send()

    def hop_arrived(h):
        @pl.when(n.quad >= h + 1)
        def _():
            for c in hops[h]:
                c.wait_recv()

    factor = LOG2E / math.sqrt(d)

    def attend(h, i, j):
        q_at = pl.ds(pl.multiple_of(i * rows, rows), rows)
        k_at = pl.ds(pl.multiple_of(j * rows, rows), rows)
        q2 = jnp.concatenate([plane[q_at, pl.ds(0, d)], plane[q_at, pl.ds(d, d)]], axis=0)
        prob = jnp.exp2(dot(q2, kx[h, k_at, :], NT) * factor)
        k_pos = (4 * (n.quad - h) + j) * rows + lax.broadcasted_iota(jnp.int32, (rows, rows), 1)
        keep = k_pos >= start[q_at, :]
        if h == 0:
            q_pos = (4 * n.quad + i) * rows + lax.broadcasted_iota(jnp.int32, (rows, rows), 0)
            keep = keep & (k_pos <= q_pos)
        prob = jnp.where(jnp.concatenate([keep, keep], axis=0), prob, 0.0)
        acc[i] += dot(prob.astype(BF16), vx[h, k_at, :])

    def sweep(h, i, lo, hi):
        def body(j, carry):
            attend(h, i, j)
            return carry

        lax.fori_loop(lo, hi, body, 0)

    def over_q(fn):
        def body(i, carry):
            fn(i)
            return carry

        lax.fori_loop(0, 4, body, 0)

    hop_start(0)
    over_q(lambda i: sweep(0, i, 0, i + 1))
    hop_arrived(0)
    hop_start(1)

    @pl.when(n.quad >= 1)
    def _():
        over_q(lambda i: sweep(1, i, 0, 4))

    ff[0].forward_all()
    ff[1].start()
    hop_arrived(1)

    @pl.when(n.quad >= 2)
    def _():
        over_q(lambda i: sweep(2, i, i, 4))

    for i in range(4):
        at = pl.ds(i * rows, rows)
        total = acc[i, :, d:]
        done = acc[i, :, :d] / total
        heads[at, pl.ds(0, d)] = done[:rows]
        heads[at, pl.ds(d, d)] = done[rows:]
        logs = jnp.log2(total)
        stat[0:1, pl.ds(i * rows, rows)] = logs[:rows].T[0:1]
        stat[1:2, pl.ds(i * rows, rows)] = logs[rows:].T[0:1]
    theirs = pl.ds(pl.multiple_of((1 - n.x) * 2 * rows, 2 * rows), 2 * rows)
    plane_attn = low.at[0, :, pl.ds(0, 2 * d)]
    head_copy.wait_send()
    n.pending.remove(head_copy.wait_send)
    low[0, :, : 2 * d] = heads[theirs, :].astype(BF16)
    attn_copy = n.send(plane_attn, attn.at[n.x], n.other_x())
    attn[n.x] = heads[chip_rows, :].astype(BF16)
    n.keep(heads, heads_out)
    n.keep(stat, stat_out)
    for h in range(back + 1):
        n.keep(kx.at[h], k_out.at[pl.ds(h * 4 * rows, 4 * rows)])
        n.keep(vx.at[h, :, pl.ds(0, d)], v_out.at[pl.ds(h * 4 * rows, 4 * rows)])
    o_w.arrived()
    load_o = pltpu.make_async_copy(o_full, w_o, n.sem())
    load_o.start()
    load_o.wait()
    attn_copy.wait_recv()
    n.keep(attn, attn_out)

    def o_rows(at):
        return dot(attn[0, at, :], w_o[:, : 2 * d], NT) + dot(attn[1, at, :], w_o[:, 2 * d :], NT)

    parts = rows // step
    core_copies, low_copies, second_copies = [], [], []
    for i in range(parts):
        at = pl.ds(i * step, step)
        core_send[at, :] = o_rows(
            pl.ds(pl.multiple_of((1 - n.core) * rows + i * step, step), step)
        ).astype(BF16)
        core_copies.append(n.send(core_send.at[at], core_recv.at[at], n.other_core()))
    for i in range(parts):
        at = pl.ds(i * step, step)
        part = o_rows(pl.ds(pl.multiple_of(n.core * rows + i * step, step), step))
        core_copies[i].wait_recv()
        low_send[at, :] = (part + core_recv[at, :].astype(F32)).astype(BF16)
        low_copies.append(n.send(low_send.at[at], low_recv.at[at], n.other_tensor()))
    ff[1].forward_all()
    ff[2].start()
    for i in range(parts):
        at = pl.ds(i * step, step)
        low_copies[i].wait_recv()
        mid = tokens[at, :].astype(F32) + (low_send[at, :].astype(F32) + low_recv[at, :].astype(F32))
        middle[at, :] = mid
        to = pl.ds(pl.multiple_of(n.core * rows + i * step, step), step)
        second[to, :] = rms_rows(mid, mlp_gain[...]).astype(BF16)
        second_copies.append(n.send(second.at[to], second.at[to], n.other_core()))
    n.keep(middle, middle_out)
    n.keep(first, first_out)
    for c in second_copies:
        c.wait_recv()
    n.keep(second, second_out)
    grad_copy.wait_recv()
    ff[2].forward_all()
    for g in ff:
        g.arrived()
    for h in range(back):
        hop_sent(h)
    n.finish()
    for g in [qkv, o_w] + ff:
        g.finish()


def forward(tokens, out_grad, attn_gain, mlp_gain, q_gain, k_gain, cosine, sine, start, *weights):
    rows, width = tokens.shape
    d = q_gain.shape[0]
    wq, wg = weights[0], weights[4]
    quads = lax.axis_size("dp") // 4
    back = REACH // 4
    units = wg.shape[1] // 2 // 3
    vmem = pl.BlockSpec(memory_space=pltpu.VMEM)
    hbm = pl.BlockSpec(memory_space=pl.ANY)
    shape = jax.ShapeDtypeStruct
    return pl.pallas_call(
        forward_kernel,
        in_specs=[vmem, hbm] + [vmem] * 7 + [hbm] * 7,
        out_specs=[hbm] * 14,
        out_shape=[
            shape((2 * rows, width), BF16),
            shape((2 * rows, width), BF16),
            shape((2 * rows, 8 * d), F32),
            shape((4 * rows, 4 * d), BF16),
            shape((4 * rows * (back + 1), d), BF16),
            shape((4 * rows * (back + 1), d), BF16),
            shape((4 * rows, 2 * d), F32),
            shape((2, 4 * rows), F32),
            shape((2, 2 * rows, 2 * d), BF16),
            shape((rows, width), F32),
            shape((2 * rows, width), BF16),
            shape((width, 8 * d), BF16),
            shape((width, 4 * d), BF16),
            shape((3, width, 3 * units), BF16),
        ],
        scratch_shapes=[
            pltpu.SemaphoreType.DMA((80 + 5 * (2 * quads + 3),)),
            pltpu.VMEM((2 * rows, width), BF16),
            pltpu.VMEM((width, 8 * d), BF16),
            pltpu.VMEM((2 * rows, 8 * d), F32),
            pltpu.VMEM((2, 2 * rows, 4 * d), BF16),
            pltpu.VMEM((4 * rows, 4 * d), BF16),
            pltpu.VMEM((back + 1, 4 * rows, d), BF16),
            pltpu.VMEM((back + 1, 4 * rows, 2 * d), BF16),
            pltpu.VMEM((4, 2 * rows, 2 * d), F32),
            pltpu.VMEM((4 * rows, 2 * d), F32),
            pltpu.VMEM((2, 4 * rows), F32),
            pltpu.VMEM((2, 2 * rows, 2 * d), BF16),
            pltpu.VMEM((width, 4 * d), BF16),
            pltpu.VMEM((rows, width), BF16),
            pltpu.VMEM((rows, width), BF16),
            pltpu.VMEM((rows, width), BF16),
            pltpu.VMEM((rows, width), BF16),
            pltpu.VMEM((rows, width), F32),
            pltpu.VMEM((2 * rows, width), BF16),
        ],
        compiler_params=pltpu.CompilerParams(
            collective_id=0, has_side_effects=True, vmem_limit_bytes=VMEM_LIMIT
        ),
        name="forward",
    )(
        tokens,
        out_grad,
        attn_gain[None],
        mlp_gain[None],
        q_gain[None],
        k_gain[None],
        cosine,
        sine,
        start,
        *weights,
    )


class Scatter:
    def __init__(self, net, keep, send, x_land, z_land, loaded, added, slot):
        self.net, self.keep, self.send, self.x_land, self.z_land = net, keep, send, x_land, z_land
        self.loaded, self.added, self.slot = loaded, added, slot
        self.own_waited = False
        self.x_sent, self.x_got, self.z_sent, self.z_got, self.own, self.tmp = [net.sem() for _ in range(6)]

    def start(self):
        n = self.net
        n.copy(self.send, self.x_land, n.other_x(), self.x_sent, self.x_got).start()

    def add(self):
        n = self.net
        pieces, shard, cols = self.keep.shape
        total = self.added.at[self.slot, :, :, pl.ds(0, cols)]
        other = self.loaded.at[:, :, pl.ds(0, cols)]
        first = pltpu.make_async_copy(self.keep, total, self.tmp)
        first.start()
        wait_bytes(self.x_land, self.x_got)
        second = pltpu.make_async_copy(self.x_land, other, self.own)
        second.start()
        first.wait()
        second.wait()

        def one(i, carry):
            total[i] = (total[i].astype(F32) + other[i].astype(F32)).astype(BF16)
            return carry

        lax.fori_loop(0, pieces, one, 0)
        pltpu.make_async_copy(total.at[n.core], self.z_land.at[n.core], self.own).start()
        n.copy(
            total.at[1 - n.core], self.z_land.at[n.core], n.other_core(), self.z_sent, self.z_got
        ).start()
        for s in range(1, n.quads):
            to = lax.rem(n.quad + n.quads - s, n.quads)
            for c in range(2):
                n.copy(
                    total.at[2 * s + c],
                    self.z_land.at[2 * s + n.core],
                    n.at(quad=to, core=c),
                    self.z_sent,
                    self.z_got,
                ).start()

    def sent(self):
        pieces = self.keep.shape[0]
        wait_bytes(self.send, self.x_sent)
        wait_bytes(self.z_land.at[pl.ds(0, pieces - 1)], self.z_sent)
        self.own_done()

    def own_done(self):
        if not self.own_waited:
            wait_bytes(self.z_land.at[0], self.own)
        self.own_waited = True

    def final(self, out, write):
        pieces, shard, cols = self.keep.shape
        wait_bytes(self.z_land.at[pl.ds(0, pieces - 1)], self.z_got)
        self.own_done()
        got = self.loaded.at[:, :, pl.ds(0, cols)]
        load = pltpu.make_async_copy(self.z_land, got, self.tmp)
        load.start()
        load.wait()
        for c in range(2):
            total = got[c].astype(F32)
            for s in range(1, pieces // 2):
                total = total + got[2 * s + c].astype(F32)
            out[c, :, pl.ds(0, cols)] = total
        copies = []
        for c in range(2):
            for at, wide, dst, col in write(c):
                k = pltpu.make_async_copy(
                    out.at[c, :, pl.ds(at, wide)], dst.at[:, pl.ds(col, wide)], self.tmp
                )
                k.start()
                copies.append((at, wide))
        wait_bytes(out.at[:, :, pl.ds(0, cols)], self.tmp)


def norm_back(values, gain, grad):
    scale = lax.rsqrt(jnp.mean(values * values, axis=-1, keepdims=True) + EPS)
    scaled = grad * gain
    inner = jnp.mean(scaled * values, axis=-1, keepdims=True)
    gain_part = jnp.sum(grad * values * scale, axis=0, keepdims=True)
    return scale * scaled - values * (scale * scale * scale * inner), gain_part


def backward_kernel(*refs):
    (
        tokens,
        attn_gain,
        mlp_gain,
        q_gain,
        k_gain,
        cosine,
        sine,
        start,
        first_t_in,
        grad_in,
        grad_t_in,
        second_in,
        second_t_in,
        proj_in,
        plane_in,
        k_in,
        v_in,
        heads_in,
        stat_in,
        attn_in,
        middle_in,
        qkv_full,
        o_full,
        ff_full,
        output,
        input_grad,
        gain_out,
        g_q,
        g_k,
        g_v,
        g_o,
        g_gate,
        g_up,
        g_down,
        ff_keep,
        ff_send,
        ff_xland,
        ff_zland,
        at_keep,
        at_send,
        at_xland,
        at_zland,
        core_land,
        low_land,
        mlp_own,
        mlp_low,
        da_land,
        heads_land,
        kv_land,
        back_land,
        sems,
        loaded,
        added,
        summed,
        low_send,
        gains,
        gains_land,
    ) = refs
    n = Net(sems)
    rows, width = tokens.shape
    d = q_gain.shape[1]
    pieces, shard, ff_cols = ff_keep.shape[1:]
    tiles = ff_keep.shape[0]
    ft = ff_cols // 3
    per_chunk = tiles // ff_full.shape[0]
    units = ff_full.shape[2] // 3
    half_ff = tiles * ft
    quads = n.quads
    block = 2 * shard
    my_at = pl.multiple_of(n.core * rows, rows)
    their_at = pl.multiple_of((1 - n.core) * rows, rows)
    my_chip = pl.ds(pl.multiple_of(n.x * 2 * rows, 2 * rows), 2 * rows)
    other_chip = pl.ds(pl.multiple_of((1 - n.x) * 2 * rows, 2 * rows), 2 * rows)
    n.greet()
    step, tall = 128, 256
    steps = rows // step
    low_sent = [n.sem() for _ in range(steps)]
    low_got = [n.sem() for _ in range(steps)]

    ff = [
        Scatter(n, ff_keep.at[f], ff_send.at[f], ff_xland.at[f], ff_zland.at[f], loaded, added, f % 2)
        for f in range(tiles)
    ]
    at_groups = [
        Scatter(n, at_keep.at[f], at_send.at[f], at_xland.at[f], at_zland.at[f], loaded, added, f % 2)
        for f in range(3)
    ]

    def ff_write(f):
        def places(c):
            col = c * half_ff + f * ft
            return [(k * ft, ft, dst, col) for k, dst in enumerate((g_gate, g_up, g_down))]

        return places

    def row_block(xr, s):
        quad = lax.rem(n.quad + quads - s, quads)
        x = n.x if xr == 0 else 1 - n.x
        return pl.multiple_of((quad * 4 + 2 * x) * shard, block)

    def load(pairs):
        copies = [pltpu.make_async_copy(s, t, n.sem()) for s, t in pairs]
        for c in copies:
            c.start()
        return copies

    def ffn_phase(s, g, st, gt, w, mlp, ds, acts, stage, w_sem, stage_sem):
        first = load([(second_in, s), (grad_in, g), (second_t_in, st), (grad_t_in, gt)])

        def fetch(f, slot):
            chunk, sub = lax.div(f, per_chunk), lax.rem(f, per_chunk)
            for k in range(3):
                col = pl.multiple_of(k * units + sub * ft, ft)
                pltpu.make_async_copy(
                    ff_full.at[chunk, :, pl.ds(col, ft)], w.at[slot, k], w_sem.at[slot]
                ).start()

        fetch(0, 0)
        mlp[...] = jnp.zeros_like(mlp)
        ds[...] = jnp.zeros_like(ds)
        for c in first:
            c.wait()

        def staged(f):
            for k, dst in enumerate((ff_keep, ff_send)):
                yield pltpu.make_async_copy(stage.at[k], dst.at[f], stage_sem.at[k])

        def tile(f, carry):
            slot = lax.rem(f, 2)

            @pl.when(f + 1 < tiles)
            def _():
                fetch(f + 1, 1 - slot)

            wait_bytes(w.at[slot], w_sem.at[slot])
            def some_rows(i, inner):
                at = pl.ds(pl.multiple_of(i * rows, rows), rows)
                gate = dot(s[at, :], w[slot, 0])
                up = dot(s[at, :], w[slot, 1])
                d_act = dot(g[at, :], w[slot, 2])
                sig = 1.0 / (1.0 + jnp.exp(-gate))
                silu = gate * sig
                acts[at, pl.ds(2 * ft, ft)] = (silu * up).astype(BF16)
                acts[at, pl.ds(0, ft)] = (d_act * up * sig * (1.0 + gate * (1.0 - sig))).astype(BF16)
                acts[at, pl.ds(ft, ft)] = (d_act * silu).astype(BF16)
                mlp[at, :] += dot(acts[at, pl.ds(2 * ft, ft)], w[slot, 2], NT)
                ds[at, :] += dot(acts[at, pl.ds(0, ft)], w[slot, 0], NT) + dot(
                    acts[at, pl.ds(ft, ft)], w[slot, 1], NT
                )
                return inner

            lax.fori_loop(0, 2, some_rows, 0)

            @pl.when(f >= 1)
            def _():
                for c in staged(f - 1):
                    c.wait()

            for k in range(1, tiles):

                @pl.when(f == k)
                def _(k=k):
                    if k - 1 < 4:
                        ff[k - 1].start()

            for xr in range(2):
                for q in range(quads):
                    at = pl.ds(row_block(xr, q), block)
                    left = dot(st[at, :], acts[:, pl.ds(0, 2 * ft)]).astype(BF16)
                    right = dot(gt[at, :], acts[:, pl.ds(2 * ft, ft)]).astype(BF16)
                    for c in range(2):
                        cut = slice(c * shard, (c + 1) * shard)
                        stage[xr, 2 * q + c, :, pl.ds(0, 2 * ft)] = left[cut]
                        stage[xr, 2 * q + c, :, pl.ds(2 * ft, ft)] = right[cut]
            for c in staged(f):
                c.start()
            for k in range(3, tiles):

                @pl.when(f == k)
                def _(k=k):
                    if k >= 5:
                        ff[k - 5].sent()
                    ff[k - 3].add()

            return carry

        lax.fori_loop(0, tiles, tile, 0)
        core_copies = []
        for i in range(rows // step):
            at = pl.ds(i * step, step)
            g[at, :] = ds[pl.ds(their_at + i * step, step), :].astype(BF16)
            core_copies.append(n.copy(g.at[at], core_land.at[0, at], n.other_core()))
            core_copies[-1].start()
        for c in staged(tiles - 1):
            c.wait()

        def to_low(i, carry):
            at = pl.ds(pl.multiple_of(i * step, step), step)
            s[at, :] = mlp[at, :].astype(BF16)
            return carry

        lax.fori_loop(0, 2 * rows // step, to_low, 0)
        mlp_copy = n.copy(s.at[pl.ds(their_at, rows)], core_land.at[1], n.other_core())
        mlp_copy.start()
        mlp_keep = pltpu.make_async_copy(s.at[pl.ds(my_at, rows)], mlp_own, n.sem())
        mlp_keep.start()
        for i in range(rows // step):
            at = pl.ds(i * step, step)
            core_copies[i].wait_recv()
            take = pltpu.make_async_copy(core_land.at[0, at], g.at[pl.ds(rows + i * step, step)], n.sem())
            take.start()
            take.wait()
            low_send[at, :] = (
                ds[pl.ds(my_at + i * step, step), :] + g[pl.ds(rows + i * step, step), :].astype(F32)
            ).astype(BF16)
            n.copy(
                low_send.at[at], low_land.at[0, at], n.other_tensor(), low_sent[i], low_got[i]
            ).start()
        for c in core_copies:
            c.wait_send()
        mlp_copy.wait_send()
        mlp_copy.wait_recv()
        mlp_keep.wait()

    bf = lambda *shape: pltpu.VMEM(shape, BF16)
    f32 = lambda *shape: pltpu.VMEM(shape, F32)
    pl.run_scoped(
        ffn_phase,
        bf(2 * rows, width),
        bf(2 * rows, width),
        bf(width, 2 * rows),
        bf(width, 2 * rows),
        bf(2, 3, width, ft),
        f32(2 * rows, width),
        f32(2 * rows, width),
        bf(2 * rows, ff_cols),
        bf(2, pieces, shard, ff_cols),
        pltpu.SemaphoreType.DMA((2,)),
        pltpu.SemaphoreType.DMA((2,)),
    )

    def rest(
        big,
        big_t,
        d_middle,
        tmp,
        tmp_low,
        w_o,
        plane,
        kx,
        vx,
        heads,
        stat,
        attn,
        d_out,
        d_q,
        d_kv,
        kv_low,
        d_low,
        d_proj,
        stage,
        proj,
    ):
        def load_now(pairs):
            for c in load(pairs):
                c.wait()

        loads = load(
            [
                (o_full, w_o),
                (plane_in, plane),
                (k_in, kx),
                (v_in, vx),
                (heads_in, heads),
                (stat_in, stat.at[pl.ds(0, 2)]),
                (attn_in, attn),
            ]
        )
        gains[...] = jnp.zeros_like(gains)
        ff[1].sent()
        ff[3].add()
        ff[0].final(summed, ff_write(0))

        for i in range(steps):
            at = pl.ds(i * step, step)
            load_now([(mlp_own.at[at], tmp_low.at[0]), (core_land.at[1, at], tmp_low.at[1])])
            tmp_low[0] = (tmp_low[0].astype(F32) + tmp_low[1].astype(F32)).astype(BF16)
            load_now([(tmp_low.at[0], mlp_low.at[at])])

        da_copies = []
        for i in range(steps):
            at = pl.ds(i * step, step)
            to = pl.ds(my_at + i * step, step)
            wait_bytes(low_land.at[0, at], low_got[i])
            load_now(
                [
                    (low_land.at[0, at], tmp_low.at[0]),
                    (middle_in.at[at], tmp),
                    (grad_in.at[to], tmp_low.at[1]),
                ]
            )
            d_second = low_send[at, :].astype(F32) + tmp_low[0].astype(F32)
            back, part = norm_back(tmp[...], mlp_gain[...], d_second)
            gains[1:2, :] += part
            d_mid = tmp_low[1].astype(F32) + back
            d_middle[at, :] = d_mid
            big[to, :] = d_mid.astype(BF16)
            da_copies.append(n.copy(big.at[to], da_land.at[at], n.other_core()))
            da_copies[-1].start()
        mlp_copy = n.send(mlp_low, low_land.at[1], n.other_tensor())
        for i in range(steps):
            wait_bytes(low_send.at[pl.ds(i * step, step)], low_sent[i])
        for c in loads:
            c.wait()
        for c in da_copies:
            c.wait()
        load_now([(da_land, big.at[pl.ds(their_at, rows)])])

        def head_grads(i, carry):
            at = pl.ds(pl.multiple_of(i * tall, tall), tall)
            got = dot(big[at, :], w_o[...]).astype(BF16)
            d_low[0, at, pl.ds(0, 2 * d)] = got[:, : 2 * d]
            d_low[1, at, pl.ds(0, 2 * d)] = got[:, 2 * d :]
            return carry

        lax.fori_loop(0, 2 * rows // tall, head_grads, 0)
        heads_copy = n.copy(d_low.at[1 - n.x, :, pl.ds(0, 2 * d)], heads_land, n.other_x())
        heads_copy.start()
        ff[4].start()
        ff[5].start()
        d_out[my_chip, :] = d_low[n.x, :, pl.ds(0, 2 * d)]
        d_q[...] = jnp.zeros_like(d_q)

        def flip(i, carry):
            at = pl.ds(pl.multiple_of(i * tall, tall), tall)
            big_t[at, :] = big[:, at].T
            return carry

        lax.fori_loop(0, width // tall, flip, 0)
        both_halves = jnp.concatenate([attn[0], attn[1]], axis=1)

        def weight_pieces(right, into):
            for xr in range(2):
                for q in range(quads):
                    got = dot(big_t[pl.ds(row_block(xr, q), block), :], right).astype(BF16)
                    for k in range(got.shape[1] // (4 * d)):
                        for c in range(2):
                            stage[into + k, xr, 2 * q + c] = got[
                                c * shard : (c + 1) * shard, k * 4 * d : (k + 1) * 4 * d
                            ]

        def stage_out(k, g):
            return load([(stage.at[k, 0], at_keep.at[g]), (stage.at[k, 1], at_send.at[g])])

        weight_pieces(both_halves, 0)
        o_stage = stage_out(0, 0)
        heads_copy.wait_recv()
        load_now([(heads_land, d_out.at[other_chip])])
        for c in o_stage:
            c.wait()
        at_groups[0].start()

        for g in range(2):
            for i in range(4):
                at = pl.ds(i * rows, rows)
                cols = pl.ds(g * d, d)
                prod = d_out[at, cols].astype(F32) * heads[at, cols]
                stat[2 + g : 3 + g, at] = jnp.sum(prod.T, axis=0, keepdims=True)
        scale = 1.0 / math.sqrt(d)

        def attend_back(h, i, j):
            q_at = pl.ds(pl.multiple_of(i * rows, rows), rows)
            k_at = pl.ds(pl.multiple_of(j * rows, rows), rows)
            kv_at = pl.ds(pl.multiple_of(h * 4 * rows + j * rows, rows), rows)
            q2 = jnp.concatenate([plane[q_at, pl.ds(0, d)], plane[q_at, pl.ds(d, d)]], axis=0)
            g2 = jnp.concatenate([d_out[q_at, pl.ds(0, d)], d_out[q_at, pl.ds(d, d)]], axis=0)
            log_total = jnp.concatenate([stat[0:1, q_at], stat[1:2, q_at]], axis=1)
            row_dot = jnp.concatenate([stat[2:3, q_at], stat[3:4, q_at]], axis=1)
            k_now = kx[kv_at, :]
            prob = jnp.exp2(dot(k_now, q2, NT) * (scale * LOG2E) - log_total)
            k_pos = (4 * (n.quad - h) + j) * rows + lax.broadcasted_iota(jnp.int32, (rows, rows), 0)
            keep = k_pos >= start[:, q_at]
            if h == 0:
                q_pos = (4 * n.quad + i) * rows + lax.broadcasted_iota(jnp.int32, (rows, rows), 1)
                keep = keep & (k_pos <= q_pos)
            prob = jnp.where(jnp.concatenate([keep, keep], axis=1), prob, 0.0)
            d_prob = dot(vx[kv_at, :], g2, NT)
            d_score = (prob * (d_prob - row_dot)).astype(BF16)
            d_kv[k_at, pl.ds(d, d)] += dot(prob.astype(BF16), g2)
            d_kv[k_at, pl.ds(0, d)] += dot(d_score, q2)
            got = dot(d_score, k_now, TN)
            d_q[q_at, pl.ds(0, d)] += got[:rows]
            d_q[q_at, pl.ds(d, d)] += got[rows:]

        def plane_back(h, lo, hi):
            d_kv[...] = jnp.zeros_like(d_kv)

            def over_i(i, carry):
                def over_j(j, inner):
                    attend_back(h, i, j)
                    return inner

                lax.fori_loop(lo(i), hi(i), over_j, 0)
                return carry

            lax.fori_loop(0, 4, over_i, 0)
            d_kv[:, pl.ds(0, d)] = d_kv[:, pl.ds(0, d)] * scale

        behind = n.at(quad=jnp.maximum(n.quad - 1, 0))
        ranges = {
            0: (lambda i: 0, lambda i: i + 1),
            1: (lambda i: 0, lambda i: 4),
            2: (lambda i: i, lambda i: 4),
        }
        top = kv_low.shape[0]
        hops = [n.copy(kv_low.at[k], kv_land.at[k], behind) for k in range(top)]
        kv_sem = n.sem()

        def add_landed(k):
            hops[k].wait_recv()
            for part in range(2):
                at = pl.ds(part * 2 * rows, 2 * rows)
                c = pltpu.make_async_copy(
                    kv_land.at[k, at], d_low.at[part, :, pl.ds(0, 2 * d)], kv_sem
                )
                c.start()
                c.wait()
                d_kv[at, :] += d_low[part, :, pl.ds(0, 2 * d)].astype(F32)

        heads_copy.wait_send()
        for h in range(top, 0, -1):

            @pl.when(n.quad >= h)
            def _(h=h):
                plane_back(h, *ranges[h])
                if h < top:

                    @pl.when(n.quad < quads - 1)
                    def _():
                        add_landed(top - h - 1)

                kv_low[top - h] = d_kv[...].astype(BF16)
                hops[top - h].start()

            if h == top:
                ff[1].final(summed, ff_write(1))
                ff[2].sent()
                ff[4].add()
                ff[2].final(summed, ff_write(2))
        plane_back(0, *ranges[0])
        ff[3].sent()
        ff[5].add()
        ff[3].final(summed, ff_write(3))

        @pl.when(n.quad < quads - 1)
        def _():
            add_landed(top - 1)

        def put_back(x):
            def body(i, carry):
                at = pl.ds(pl.multiple_of(i * tall, tall), tall)
                src = pl.ds(pl.multiple_of(x * 2 * rows + i * tall, tall), tall)
                d_low[x, at, pl.ds(0, 2 * d)] = (d_q[src, :] * scale).astype(BF16)
                d_low[x, at, pl.ds(2 * d, 2 * d)] = d_kv[src, :].astype(BF16)
                return carry

            lax.fori_loop(0, 2 * rows // tall, body, 0)

        put_back(1 - n.x)
        back_copy = n.copy(d_low.at[1 - n.x], back_land, n.other_x())
        back_copy.start()
        put_back(n.x)
        late = load([(qkv_full, big_t)])
        ff[4].sent()
        at_groups[0].add()
        ff[4].final(summed, ff_write(4))
        back_copy.wait_send()
        back_copy.wait_recv()
        load_now([(back_land, d_low.at[1 - n.x])])

        def prep_back(i, carry):
            at = pl.ds(pl.multiple_of(i * step, step), step)
            got = pltpu.make_async_copy(proj_in.at[at], proj, kv_sem)
            got.start()
            got.wait()
            cos, sin = cosine[at, :], sine[at, :]

            def back(col, h, src, gain, row):
                grad = d_low[h, at, pl.ds(src, d)].astype(F32)
                turned = grad * cos + pltpu.roll(grad * sin, d // 2, 1)
                res, part = norm_back(proj[:, pl.ds(col, d)], gain[...], turned)
                gains[pl.ds(row, 1), pl.ds(0, d)] += part
                d_proj[at, pl.ds(col, d)] = res.astype(BF16)

            for h in range(2):
                for g in range(2):
                    back((2 * h + g) * d, h, g * d, q_gain, 2)
                back((4 + h) * d, h, 2 * d, k_gain, 3)
                d_proj[at, pl.ds((6 + h) * d, d)] = d_low[h, at, pl.ds(3 * d, d)]
            return carry

        lax.fori_loop(0, 2 * rows // step, prep_back, 0)
        for c in late:
            c.wait()

        core_copies, low_copies = [], []
        for i in range(steps):
            at = pl.ds(i * step, step)
            big[at, :] = dot(d_proj[pl.ds(their_at + i * step, step), :], big_t[...], NT).astype(BF16)
            core_copies.append(n.send(big.at[at], core_land.at[2, at], n.other_core()))
        for i in range(steps):
            at = pl.ds(i * step, step)
            part = dot(d_proj[pl.ds(my_at + i * step, step), :], big_t[...], NT)
            core_copies[i].wait_recv()
            load_now([(core_land.at[2, at], tmp_low.at[0])])
            low_send[at, :] = (part + tmp_low[0].astype(F32)).astype(BF16)
            low_copies.append(n.send(low_send.at[at], low_land.at[2, at], n.other_tensor()))

        load_now([(first_t_in, big_t)])
        weight_pieces(d_proj[...], 0)
        for c in stage_out(0, 1) + stage_out(1, 2):
            c.wait()
        at_groups[1].start()
        at_groups[2].start()
        ff[5].final(summed, ff_write(5))

        mlp_copy.wait_recv()
        for i in range(steps):
            at = pl.ds(i * step, step)
            load_now(
                [
                    (low_land.at[1, at], tmp_low.at[0]),
                    (mlp_low.at[at], tmp_low.at[1]),
                    (middle_in.at[at], tmp),
                ]
            )
            tmp_low[0] = (tmp[...] + (tmp_low[1].astype(F32) + tmp_low[0].astype(F32))).astype(BF16)
            load_now([(tmp_low.at[0], output.at[at])])
        for i in range(steps):
            at = pl.ds(i * step, step)
            low_copies[i].wait_recv()
            load_now([(low_land.at[2, at], tmp_low.at[0]), (tokens.at[at], tmp_low.at[1])])
            d_first = low_send[at, :].astype(F32) + tmp_low[0].astype(F32)
            back, part = norm_back(tmp_low[1].astype(F32), attn_gain[...], d_first)
            gains[0:1, :] += part
            d_middle[at, :] = d_middle[at, :] + back
            n.keep(d_middle.at[at], input_grad.at[at])

        for k, to in enumerate((n.other_core(), n.other_x(), n.other_tensor())):
            c = n.copy(gains, gains_land.at[k], to)
            c.start()
            c.wait()
            if k < 2:
                gains[...] += gains_land[k]
            else:
                gains[2:4, :] += gains_land[k, 2:4, :]
        gains_land[3 + n.quad] = gains[...]
        quad_copies = []
        for s in range(1, quads):
            to = n.at(quad=lax.rem(n.quad + s, quads))
            quad_copies.append(n.copy(gains, gains_land.at[3 + n.quad], to))
            quad_copies[-1].start()
        for c in quad_copies:
            c.wait()
        total = gains_land[3]
        for k in range(1, quads):
            total = total + gains_land[3 + k]
        gains[...] = total
        n.keep(gains, gain_out)

        ff[5].sent()
        at_groups[1].add()

        def simple(places):
            return lambda c: [(at, wide, dst, c * wide) for at, wide, dst in places]

        at_groups[0].final(summed, simple([(0, 4 * d, g_o)]))
        at_groups[0].sent()
        at_groups[2].add()
        at_groups[1].final(summed, simple([(0, 4 * d, g_q)]))
        at_groups[2].final(summed, simple([(0, 2 * d, g_k), (2 * d, 2 * d, g_v)]))
        at_groups[1].sent()
        at_groups[2].sent()
        for k in range(top):

            @pl.when(n.quad >= top - k)
            def _(k=k):
                hops[k].wait_send()

        n.finish()

    top = kv_land.shape[0]
    pl.run_scoped(
        rest,
        bf(2 * rows, width),
        bf(width, 2 * rows),
        f32(rows, width),
        f32(128, width),
        bf(2, 128, width),
        bf(width, 4 * d),
        bf(4 * rows, 4 * d),
        bf(4 * rows * (top + 1), d),
        bf(4 * rows * (top + 1), d),
        f32(4 * rows, 2 * d),
        f32(4, 4 * rows),
        bf(2, 2 * rows, 2 * d),
        bf(4 * rows, 2 * d),
        f32(4 * rows, 2 * d),
        f32(4 * rows, 2 * d),
        bf(top, 4 * rows, 2 * d),
        bf(2, 2 * rows, 4 * d),
        bf(2 * rows, 8 * d),
        bf(2, 2, pieces, shard, 4 * d),
        f32(128, 8 * d),
    )


def backward(tokens, attn_gain, mlp_gain, q_gain, k_gain, cosine, sine, start, *arrays):
    rows, width = tokens.shape
    d = q_gain.shape[0]
    ff_full = arrays[-1]
    quads = lax.axis_size("dp") // 4
    shard = width // (4 * quads)
    chunks, half_ff = ff_full.shape[0], ff_full.shape[0] * ff_full.shape[2] // 3
    tiles = 2 * chunks
    cols = 3 * half_ff // tiles
    top = REACH // 4
    vmem = pl.BlockSpec(memory_space=pltpu.VMEM)
    hbm = pl.BlockSpec(memory_space=pl.ANY)
    shape = jax.ShapeDtypeStruct
    out_shape = [
        shape((rows, width), BF16),
        shape((rows, width), F32),
        shape((4, width), F32),
        shape((shard, 8 * d), F32),
        shape((shard, 4 * d), F32),
        shape((shard, 4 * d), F32),
        shape((shard, 8 * d), F32),
        shape((shard, 2 * half_ff), F32),
        shape((shard, 2 * half_ff), F32),
        shape((shard, 2 * half_ff), F32),
    ]
    out_shape += [shape((tiles, 2 * quads, shard, cols), BF16)] * 4
    out_shape += [shape((3, 2 * quads, shard, 4 * d), BF16)] * 4
    out_shape += [shape((3, rows, width), BF16)] * 2
    out_shape += [shape((rows, width), BF16)] * 3
    out_shape += [
        shape((2 * rows, 2 * d), BF16),
        shape((top, 4 * rows, 2 * d), BF16),
        shape((2 * rows, 4 * d), BF16),
    ]
    return pl.pallas_call(
        backward_kernel,
        in_specs=[hbm] + [vmem] * 7 + [hbm] * len(arrays),
        out_specs=[hbm] * len(out_shape),
        out_shape=out_shape,
        scratch_shapes=[
            pltpu.SemaphoreType.DMA((260,)),
            pltpu.VMEM((2 * quads, shard, max(cols, 4 * d)), BF16),
            pltpu.VMEM((2, 2 * quads, shard, max(cols, 4 * d)), BF16),
            pltpu.VMEM((2, shard, max(cols, 4 * d)), F32),
            pltpu.VMEM((rows, width), BF16),
            pltpu.VMEM((4, width), F32),
            pltpu.VMEM((3 + quads, 4, width), F32),
        ],
        compiler_params=pltpu.CompilerParams(
            collective_id=1, has_side_effects=True, vmem_limit_bytes=VMEM_LIMIT
        ),
        name="backward",
    )(
        tokens,
        attn_gain[None],
        mlp_gain[None],
        q_gain[None],
        k_gain[None],
        cosine,
        sine,
        start,
        *arrays,
    )[:10]


def local(
    tokens,
    out_grad,
    lengths,
    attn_gain,
    q_weight,
    key_matrix,
    value_matrix,
    o_weight,
    q_gain,
    k_gain,
    mlp_gain,
    gate_weight,
    up_weight,
    down_weight,
):
    rows = tokens.shape[0]
    d = q_gain.shape[0]
    me = lax.axis_index("dp")
    assert key_matrix.shape[1] == 4 * d and q_weight.shape[1] == 8 * d
    chip_index = (me // 2) * 2 * rows + jnp.arange(2 * rows, dtype=jnp.int32)
    cosine, sine_vals = angles(chip_index - starts_of(chip_index, lengths), d)
    sine_signed = jnp.concatenate([-sine_vals[:, : d // 2], sine_vals[:, d // 2 :]], 1)
    q_index = (me // 4) * 4 * rows + jnp.arange(4 * rows, dtype=jnp.int32)
    q_start = starts_of(q_index, lengths)
    (
        first_chip,
        grad_chip,
        proj,
        plane,
        k_all,
        v_all,
        heads_out,
        log_total,
        attn_halves,
        middle,
        second_chip,
        qkv_full,
        o_full,
        ff_full,
    ) = forward(
        tokens,
        out_grad,
        attn_gain,
        mlp_gain,
        q_gain,
        k_gain,
        cosine,
        sine_signed,
        q_start[:, None],
        q_weight,
        key_matrix,
        value_matrix,
        o_weight,
        gate_weight,
        up_weight,
        down_weight,
    )
    output, input_grad, gains, g_q, g_k, g_v, g_o, g_gate, g_up, g_down = backward(
        tokens,
        attn_gain,
        mlp_gain,
        q_gain,
        k_gain,
        cosine,
        sine_signed,
        q_start[None, :],
        first_chip.T,
        grad_chip,
        grad_chip.T,
        second_chip,
        second_chip.T,
        proj,
        plane,
        k_all,
        v_all,
        heads_out,
        log_total,
        attn_halves,
        middle,
        qkv_full,
        o_full,
        ff_full,
    )
    return (
        output,
        input_grad,
        gains[0],
        g_q,
        g_k,
        g_v,
        g_o,
        gains[2, :d],
        gains[3, :d],
        gains[1],
        g_gate,
        g_up,
        g_down,
    )


def solution(mesh):
    rows, weight = P("dp", None), P("dp", "tensor")
    placed = (
        (rows, rows) + (P(),) * 2 + (weight,) * 4 + (P(),) * 3 + (weight,) * 3
    )
    return jax.shard_map(
        local,
        mesh=mesh,
        in_specs=placed,
        out_specs=(rows, rows, P()) + (weight,) * 4 + (P(),) * 3 + (weight,) * 3,
        check_vma=False,
    )
```

```python
from functools import partial
import math

import jax
import jax.numpy as jnp
from jax import lax
from jax.experimental import pallas as pl
from jax.experimental.pallas import tpu as pltpu
from jax.sharding import PartitionSpec as P

REACH = 8
EPS = 1e-06
THETA = 1000000.0
LOG2E = 1.4426950408889634
F32 = jnp.float32
BF16 = jnp.bfloat16
VMEM_LIMIT = 62 * 1024 * 1024

NT = (((1,), (1,)), ((), ()))
NN = (((1,), (0,)), ((), ()))
TN = (((0,), (0,)), ((), ()))
MESH = pl.DeviceIdType.MESH


def dot(a, b, dims=NN):
    return lax.dot_general(a, b, dims, preferred_element_type=F32)


def over_quads(value, by):
    n = lax.axis_size("dp")
    return lax.ppermute(value, "dp", [(i, (i + 4 * by) % n) for i in range(n)])


def shift_quads(value, by):
    n = lax.axis_size("dp")
    return lax.ppermute(
        value, "dp", [(i, i + 4 * by) for i in range(n) if 0 <= i + 4 * by < n]
    )


def swap_x(value):
    return lax.ppermute(value, "dp", [(i, i ^ 2) for i in range(lax.axis_size("dp"))])


def swap_core(value):
    return lax.ppermute(value, "dp", [(i, i ^ 1) for i in range(lax.axis_size("dp"))])


def swap_tensor(value):
    return lax.ppermute(value, "tensor", [(0, 1), (1, 0)])


def tensor_sum(part):
    low = part.astype(BF16)
    return low.astype(F32) + swap_tensor(low).astype(F32)


def rms_rows(values, gain_vec):
    return values * lax.rsqrt(jnp.mean(values * values, axis=-1, keepdims=True) + EPS) * gain_vec


def rotate(values):
    half_size = values.shape[-1] // 2
    return jnp.concatenate([-values[..., half_size:], values[..., :half_size]], axis=-1)


def head_prep(heads_view, gain_vec, cosine, sine_vals):
    normed = rms_rows(heads_view, gain_vec)
    return normed * cosine[:, None, :] + rotate(normed) * sine_vals[:, None, :]


def starts_of(index, lengths):
    ends = jnp.cumsum(lengths)
    starts = ends - lengths
    inside = (index[:, None] >= starts[None, :]) & (index[:, None] < ends[None, :])
    return jnp.sum(jnp.where(inside, starts[None, :], 0), axis=1)


def angles(position, head_dim):
    freq = THETA ** (-(jnp.arange(0, head_dim, 2, dtype=F32) / head_dim))
    turn = position.astype(F32)[:, None] * freq[None, :]
    turn = jnp.concatenate([turn, turn], axis=-1)
    return (jnp.cos(turn), jnp.sin(turn))


class Net:
    def __init__(self, sems):
        me = lax.axis_index("dp")
        self.me, self.tensor = me, lax.axis_index("tensor")
        self.core = lax.rem(me, 2)
        self.x = lax.rem(lax.div(me, 2), 2)
        self.quad = lax.div(me, 4)
        self.quads = lax.axis_size("dp") // 4
        self.sems, self.used = sems, 0
        self.pending = []
        self.to_core = self.at(core=1 - self.core)
        self.to_x = self.at(x=1 - self.x)
        self.to_tensor = self.at(tensor=1 - self.tensor)

    def sem(self):
        self.used += 1
        return self.sems.at[self.used - 1]

    def at(self, quad=None, x=None, core=None, tensor=None):
        quad = self.quad if quad is None else quad
        x = self.x if x is None else x
        core = self.core if core is None else core
        tensor = self.tensor if tensor is None else tensor
        return (quad * 4 + x * 2 + core, tensor)

    def flipped(self, bits):
        quad, bit = self.quad, 1
        while bit <= bits:
            if bits & bit:
                quad = quad + bit * (1 - 2 * lax.rem(lax.div(self.quad, bit), 2))
            bit *= 2
        return quad

    def other_core(self):
        return self.to_core

    def other_x(self):
        return self.to_x

    def other_tensor(self):
        return self.to_tensor

    def greet(self):
        targets = [self.other_core(), self.other_x(), self.other_tensor()]
        for s in range(1, self.quads):
            for c in range(2):
                targets.append(self.at(quad=lax.rem(self.quad + s, self.quads), core=c))
        barrier = pltpu.get_barrier_semaphore()
        for t in targets:
            pl.semaphore_signal(barrier, inc=1, device_id=t, device_id_type=MESH)
        pl.semaphore_wait(barrier, len(targets))

    def copy(self, src, dst, to, send=None, recv=None):
        return pltpu.make_async_remote_copy(
            src_ref=src,
            dst_ref=dst,
            send_sem=self.sem() if send is None else send,
            recv_sem=self.sem() if recv is None else recv,
            device_id=to,
            device_id_type=MESH,
        )

    def send(self, src, dst, to):
        c = self.copy(src, dst, to)
        c.start()
        self.pending.append(c.wait_send)
        return c

    def keep(self, src, dst):
        c = pltpu.make_async_copy(src, dst, self.sem())
        c.start()
        self.pending.append(c.wait)
        return c

    def finish(self):
        for wait in self.pending:
            wait()
        self.pending = []


def wait_bytes(ref, sem):
    pltpu.make_async_copy(ref, ref, sem).wait()


class Gather:
    def __init__(self, net, full, shard, kinds, paired=False):
        self.net, self.full, self.shard, self.kinds, self.paired = net, full, shard, kinds, paired
        self.z_rows = (4 if paired else 2) * shard
        rounds = range(net.quads)
        self.z_got = [[net.sem() for _ in rounds[1:]] for _ in range(2)]
        self.x_got = [[net.sem() for _ in rounds[1:]] for _ in range(2)]
        self.z_sent = [net.sem(), net.sem()]
        self.x_own, self.x_sent, self.own, self.core_got, self.core_sent = [net.sem() for _ in range(5)]

    def rows(self, quad, x):
        at = (quad * 4 + 2 * x) * self.shard
        return self.full.at[pl.ds(pl.multiple_of(at, self.shard), 2 * self.shard)]

    def z_block(self, quad):
        if self.paired:
            return self.full.at[pl.ds(pl.multiple_of(quad * self.z_rows, self.z_rows), self.z_rows)]
        return self.rows(quad, self.net.x)

    def start(self):
        n = self.net
        mine = pl.ds(pl.multiple_of(n.me * self.shard, self.shard), self.shard)
        for arr, first, wide, into in self.kinds:
            half = arr.shape[1] // 2
            there = self.full.at[mine, pl.ds(into, wide)]

            def cut(core):
                return arr.at[:, pl.ds(pl.multiple_of(core * half + first, 128), wide)]

            pltpu.make_async_copy(cut(n.core), there, self.own).start()
            n.copy(cut(1 - n.core), there, n.other_core(), self.core_sent, self.core_got).start()

    def sides(self, r):
        n = self.net
        for side, way in enumerate((1, -1)):
            quad = n.quad - way * r
            near = n.quad + way
            last = n.quads - 1
            here = (quad >= 0) & (quad <= last)
            on = here & (near >= 0) & (near <= last)
            yield side, here, jnp.clip(quad, 0, last), on, jnp.clip(near, 0, last)

    def z(self, r):
        n = self.net
        if r == 0:
            if self.paired:
                wait_bytes(self.rows(n.quad, 1 - n.x), self.x_own)
            else:
                self.own_here()
        for side, here, quad, on, near in self.sides(r):
            if r > 0:

                @pl.when(here)
                def _():
                    wait_bytes(self.z_block(quad), self.z_got[side][r - 1])

            if r < n.quads - 1:

                @pl.when(on)
                def _():
                    block = self.z_block(quad)
                    n.copy(block, block, n.at(quad=near), self.z_sent[side], self.z_got[side][r]).start()

    def own_here(self):
        half = self.full.at[pl.ds(0, self.shard)]
        wait_bytes(half, self.own)
        wait_bytes(half, self.core_got)

    def x(self, r):
        n = self.net
        if r == 0:
            if self.paired:
                self.own_here()
            block = self.rows(n.quad, n.x)
            n.copy(block, block, n.other_x(), self.x_sent, self.x_own).start()
            return
        if self.paired:
            return
        for side, here, quad, on, near in self.sides(r):

            @pl.when(here)
            def _():
                block = self.rows(quad, n.x)
                n.copy(block, block, n.other_x(), self.x_sent, self.x_got[side][r - 1]).start()

    def arrived(self):
        n = self.net
        if self.paired:
            return
        wait_bytes(self.rows(n.quad, 1 - n.x), self.x_own)
        for r in range(1, n.quads):
            for side, here, quad, on, near in self.sides(r):

                @pl.when(here)
                def _():
                    wait_bytes(self.rows(quad, 1 - n.x), self.x_got[side][r - 1])

    def finish(self):
        n = self.net
        wait_bytes(self.full.at[pl.ds(0, self.shard)], self.core_sent)
        wait_bytes(self.full.at[pl.ds(0, 2 * (1 if self.paired else n.quads) * self.shard)], self.x_sent)
        for k in range(n.quads):

            @pl.when(n.quad == k)
            def _():
                for side, count in enumerate((k + 1, n.quads - k)):
                    if count < n.quads:
                        wait_bytes(self.full.at[pl.ds(0, count * self.z_rows)], self.z_sent[side])


class Scatter:
    def __init__(self, net, keep, send, x_land, z_land, loaded, added, slot):
        self.net, self.keep, self.send, self.x_land, self.z_land = net, keep, send, x_land, z_land
        self.loaded, self.added, self.slot = loaded, added, slot
        self.shard = keep.shape[0] // (2 * net.quads)
        self.stages = net.quads.bit_length() - 1
        self.own_waited = False
        self.z_got = [net.sem() for _ in range(self.stages)]
        self.z_sent = [net.sem() for _ in range(self.stages)]
        self.x_sent, self.x_got, self.own, self.tmp = [net.sem() for _ in range(4)]

    def start(self):
        n = self.net
        n.copy(self.send, self.x_land, n.other_x(), self.x_sent, self.x_got).start()

    def left(self, stage):
        return self.keep.shape[0] >> stage

    def landing(self, stage):
        rows = self.keep.shape[0]
        return self.z_land.at[pl.ds(rows - self.left(stage), self.left(stage + 1))]

    def last(self, far, core, count=1):
        at = self.keep.shape[0] + (2 * far + core) * self.shard
        at = at if isinstance(at, int) else pl.multiple_of(at, self.shard)
        return self.z_land.at[pl.ds(at, count * self.shard)]

    def total(self):
        return self.added.at[self.slot, :, pl.ds(0, self.keep.shape[1])]

    def add_in(self, rows):
        total, other = self.total(), self.loaded.at[:, pl.ds(0, self.keep.shape[1])]

        def one(i, carry):
            at = pl.ds(pl.multiple_of(i * 128, 128), 128)
            total[at, :] = (total[at, :].astype(F32) + other[at, :].astype(F32)).astype(BF16)
            return carry

        lax.fori_loop(0, rows // 128, one, 0)

    def add(self):
        first = pltpu.make_async_copy(self.keep, self.total(), self.tmp)
        first.start()
        wait_bytes(self.x_land, self.x_got)
        second = pltpu.make_async_copy(
            self.x_land, self.loaded.at[:, pl.ds(0, self.keep.shape[1])], self.own
        )
        second.start()
        first.wait()
        second.wait()
        self.add_in(self.keep.shape[0])
        self.send_half(0)

    def pass_on(self):
        for stage in range(1, self.stages):
            rows = self.left(stage)
            wait_bytes(self.landing(stage - 1), self.z_got[stage - 1])
            load = pltpu.make_async_copy(
                self.landing(stage - 1),
                self.loaded.at[pl.ds(0, rows), pl.ds(0, self.keep.shape[1])],
                self.tmp,
            )
            load.start()
            load.wait()
            self.add_in(rows)
            self.send_half(stage)

    def send_half(self, stage):
        n, total = self.net, self.total()
        quad = n.flipped(1 << stage)
        sent, got = self.z_sent[stage], self.z_got[stage]
        if stage < self.stages - 1:
            half = total.at[pl.ds(self.left(stage + 1), self.left(stage + 1))]
            n.copy(half, self.landing(stage), n.at(quad=quad), sent, got).start()
            return

        def rows(far, core):
            at = (2 * far + core) * self.shard
            at = at if isinstance(at, int) else pl.multiple_of(at, self.shard)
            return total.at[pl.ds(at, self.shard)]

        for c in range(2):
            n.copy(rows(1, c), self.last(1, n.core), n.at(quad=quad, core=c), sent, got).start()
        n.copy(rows(0, 1 - n.core), self.last(0, n.core), n.other_core(), sent, got).start()
        pltpu.make_async_copy(rows(0, n.core), self.last(0, n.core), self.own).start()

    def sent(self):
        wait_bytes(self.send, self.x_sent)
        for stage in range(self.stages - 1):
            wait_bytes(self.landing(stage), self.z_sent[stage])
        wait_bytes(self.last(0, 0, 3), self.z_sent[-1])
        self.own_done()

    def own_done(self):
        if not self.own_waited:
            wait_bytes(self.last(0, 0), self.own)
        self.own_waited = True

    def final(self, out, write):
        shard, cols = self.shard, self.keep.shape[1]
        wait_bytes(self.last(0, 0, 3), self.z_got[-1])
        self.own_done()
        got = self.loaded.at[pl.ds(0, 4 * shard), pl.ds(0, cols)]
        load = pltpu.make_async_copy(self.last(0, 0, 4), got, self.tmp)
        load.start()
        load.wait()
        for c in range(2):
            near, far = pl.ds(c * shard, shard), pl.ds((2 + c) * shard, shard)
            out[c, :, pl.ds(0, cols)] = got[near, :].astype(F32) + got[far, :].astype(F32)
        for c in range(2):
            for at, wide, dst, col in write(c):
                pltpu.make_async_copy(
                    out.at[c, :, pl.ds(at, wide)], dst.at[:, pl.ds(col, wide)], self.tmp
                ).start()
        wait_bytes(out.at[:, :, pl.ds(0, cols)], self.tmp)


def norm_back(values, gain, grad):
    scale = lax.rsqrt(jnp.mean(values * values, axis=-1, keepdims=True) + EPS)
    scaled = grad * gain
    inner = jnp.mean(scaled * values, axis=-1, keepdims=True)
    gain_part = jnp.sum(grad * values * scale, axis=0, keepdims=True)
    return scale * scaled - values * (scale * scale * scale * inner), gain_part


SLOTS = 3
MID = {0: 3, 1: 2, 2: 1}
PAIRED = (4, 5)
SCHEDULE = {
    "G": (
        ("z", 0, 0),
        ("z", 6, 0),
    ),
    "P0": (
        ("z", 3, 0),
        ("z", 1, 0),
        ("z", 0, 1),
    ),
    "P1": (
        ("x", 0, 0),
        ("z", 6, 1),
    ),
    "P1b": (
        ("x", 6, 1),
        ("x", 0, 1),
        ("z", 6, 2),
    ),
    "P2": (
        ("x", 5, 0),
    ),
    "P3": (
        ("x", 4, 0),
        ("z", 1, 1),
        ("x", 6, 0),
        ("z", 6, 3),
    ),
    "P3b": (
        ("x", 6, 3),
        ("x", 1, 1),
        ("x", 6, 2),
        ("z", 1, 2),
    ),
    "P4": (
        ("z", 1, 3),
        ("z", 0, 2),
        ("x", 0, 2),
    ),
    "P5": (
        ("z", 3, 1),
    ),
    "P6": (
        ("z", 0, 3),
        ("z", 2, 0),
    ),
    "P7": (
        ("x", 0, 3),
        ("x", 1, 0),
        ("z", 3, 2),
        ("z", 2, 1),
    ),
    "P8": (
        ("x", 2, 0),
        ("x", 3, 0),
        ("z", 2, 2),
        ("x", 1, 2),
        ("x", 1, 3),
        ("x", 2, 1),
    ),
    "P8b": (
        ("z", 4, 0),
        ("x", 3, 2),
        ("z", 4, 1),
        ("z", 2, 3),
    ),
    "P9": (
        ("x", 2, 3),
        ("z", 5, 0),
        ("x", 2, 2),
    ),
    "F0b": (
        ("z", 3, 3),
    ),
    "F1a": (
        ("x", 3, 3),
        ("x", 3, 1),
    ),
    "F1b": (
        ("z", 4, 2),
        ("s", 0),
    ),
    "F2a": (
        ("z", 5, 1),
    ),
    "F2b": (
        ("z", 5, 2),
    ),
    "F3a": (
        ("z", 4, 3),
        ("s", 1),
    ),
    "F4a": (
        ("z", 5, 3),
    ),
    "F5a": (
        ("a", 0),
        ("s", 2),
    ),
    "B0": (
        ("a", 1),
    ),
    "B1": (
        ("p", 0),
        ("s", 3),
    ),
    "B2": (
        ("a", 2),
    ),
    "B3": (
        ("p", 1),
        ("f", 0),
        ("s", 4),
        ("a", 3),
    ),
    "B4": (
        ("p", 2),
    ),
    "C2": (
        ("s", 5),
    ),
    "C1e": (
        ("s", 6),
    ),
    "C0": (
        ("a", 4),
    ),
    "D0": (
        ("p", 3),
        ("a", 5),
        ("f", 1),
    ),
    "D1": (
        ("f", 2),
    ),
    "D2": (
        ("p", 4),
        ("a", 6),
    ),
    "D3": (
        ("p", 5),
        ("f", 3),
        ("a", 7),
        ("f", 4),
    ),
    "D4": (
        ("p", 6),
        ("p", 7),
        ("a", 8),
    ),
    "D5": (
        ("p", 8),
        ("f", 5),
        ("f", 6),
        ("f", 7),
        ("f", 8),
    ),
}


def layer_kernel(*refs):
    (
        tokens,
        out_grad,
        attn_gain,
        mlp_gain,
        q_gain,
        k_gain,
        cosine,
        sine,
        start_in,
        start_row,
        wq,
        wk,
        wv,
        wo,
        wg,
        wu,
        wd,
        output,
        input_grad,
        gain_out,
        g_q,
        g_k,
        g_v,
        g_o,
        g_gate,
        g_up,
        g_down,
        qkv_full,
        o_full,
        ff_full,
        grad_full,
        first_t,
        proj_s,
        plane_s,
        k_s,
        v_s,
        heads_s,
        stat_s,
        middle_s,
        ff_keep,
        ff_send,
        ff_xland,
        ff_zland,
        at_keep,
        at_send,
        at_xland,
        at_zland,
        core_land,
        low_land,
        mlp_own,
        mlp_low,
        da_land,
        heads_land,
        kv_land,
        back_land,
        sems,
        xa,
        sa,
        ta,
        tb,
        attn,
        loaded,
        added,
        summed,
        low_send,
        gains,
        gains_land,
    ) = refs
    n = Net(sems)
    rows, width = tokens.shape
    d = q_gain.shape[1]
    shard = wq.shape[0]
    block = 2 * shard
    quads = n.quads
    tiles, _, ff_cols = ff_keep.shape
    ft = ff_cols // 3
    half_ff = tiles * ft
    top = kv_land.shape[0]
    step, tall = 128, 256
    steps = rows // step
    my_at = pl.multiple_of(n.core * rows, rows)
    their_at = pl.multiple_of((1 - n.core) * rows, rows)
    my_rows = pl.ds(my_at, rows)
    my_chip = pl.ds(pl.multiple_of(n.x * 2 * rows, 2 * rows), 2 * rows)
    other_chip = pl.ds(pl.multiple_of((1 - n.x) * 2 * rows, 2 * rows), 2 * rows)
    scale = 1.0 / math.sqrt(d)
    bf = lambda *shape: pltpu.VMEM(shape, BF16)
    f32 = lambda *shape: pltpu.VMEM(shape, F32)

    def load(pairs):
        copies = [pltpu.make_async_copy(s, t, n.sem()) for s, t in pairs]
        for c in copies:
            c.start()
        return copies

    def load_now(pairs):
        for c in load(pairs):
            c.wait()

    def loop(count, fn):
        def body(i, carry):
            fn(i)
            return carry

        lax.fori_loop(0, count, body, 0)

    def part(i, size):
        return pl.ds(pl.multiple_of(i * size, size), size)

    n.greet()

    qkv = Gather(n, qkv_full, shard, [(wq, 0, 4 * d, 0), (wk, 0, 2 * d, 4 * d), (wv, 0, 2 * d, 6 * d)])
    o_w = Gather(n, o_full, shard, [(wo, 0, 4 * d, 0)])
    ffw = [
        Gather(
            n,
            ff_full.at[f],
            shard,
            [(arr, f * ft, ft, kind * ft) for kind, arr in enumerate((wg, wu, wd))],
            paired=f in PAIRED,
        )
        for f in range(tiles)
    ]
    ff = [
        Scatter(n, ff_keep.at[f], ff_send.at[f], ff_xland.at[f], ff_zland.at[f], loaded, added, f % SLOTS)
        for f in range(tiles)
    ]
    at_groups = [
        Scatter(n, at_keep.at[f], at_send.at[f], at_xland.at[f], at_zland.at[f], loaded, added, (tiles + f) % SLOTS)
        for f in range(3)
    ]

    def ff_write(f):
        def places(c):
            col = c * half_ff + f * ft
            return [(k * ft, ft, dst, col) for k, dst in enumerate((g_gate, g_up, g_down))]

        return places

    def simple(places):
        return lambda c: [(at, wide, dst, c * wide) for at, wide, dst in places]

    groups = ffw + [o_w]
    sums = ff + at_groups
    writes = [ff_write(f) for f in range(tiles)] + [
        simple([(0, 4 * d, g_o)]),
        simple([(0, 4 * d, g_q)]),
        simple([(0, 2 * d, g_k), (2 * d, 2 * d, g_v)]),
    ]
    planned = 1 + max(step[2] for steps_at in SCHEDULE.values() for step in steps_at if step[0] in "zx")

    def tick(name):
        for what, g, *r in SCHEDULE.get(name, ()):
            if what in "zx":
                if r[0] < quads:
                    getattr(groups[g], what)(r[0])
            elif what == "s":
                sums[g].start()
            elif what == "a":
                if g >= SLOTS:
                    sums[g - SLOTS].sent()
                sums[g].add()
            elif what == "p":
                sums[g].pass_on()
            else:
                sums[g].final(summed, writes[g])

    def need(g):
        for r in range(planned, quads):
            groups[g].z(r)
            groups[g].x(r)
        groups[g].arrived()

    def tick_within(h, sweeps, name):
        flags = [s.own_waited for s in sums]
        pl.when(n.quad >= h)(lambda: sweeps(lambda: tick(name)))
        for s, flag in zip(sums, flags):
            s.own_waited = flag
        pl.when(n.quad < h)(lambda: tick(name))

    plane = ta.at[:, pl.ds(0, 4 * d)]
    keys = [tb.at[:, pl.ds(h * d, d)] for h in range(top + 1)]
    vals = [ta.at[:, pl.ds(4 * d, 2 * d)], ta.at[:, pl.ds(6 * d, 2 * d)], tb.at[:, pl.ds(3 * d, 2 * d)]]
    ones = [ta.at[:, pl.ds(5 * d, d)], ta.at[:, pl.ds(7 * d, d)], tb.at[:, pl.ds(4 * d, d)]]

    def core_then_tensor(product, sending, k, tmp_low):
        core_copies, low_copies = [], []
        for i in range(rows // tall):
            at = pl.ds(i * tall, tall)
            sending[at, :] = product(pl.ds(their_at + i * tall, tall)).astype(BF16)
            core_copies.append(n.send(sending.at[at], core_land.at[k, at], n.other_core()))
        for i in range(rows // tall):
            got = product(pl.ds(my_at + i * tall, tall))
            core_copies[i].wait_recv()
            for p in range(tall // step):
                at = pl.ds(i * tall + p * step, step)
                load_now([(core_land.at[k, at], tmp_low.at[0])])
                low_send[at, :] = (got[p * step : (p + 1) * step] + tmp_low[0].astype(F32)).astype(BF16)
                low_copies.append(n.send(low_send.at[at], low_land.at[k, at], n.other_tensor()))
        return low_copies

    def forward(w_qkv, proj, low, acc, heads, stat, w_o, core_send, tmp, tmp_low, start_col):
        qkv.start()
        o_w.start()
        qkv.z(0)
        qkv.x(0)
        for g in ffw:
            g.start()

        def norm_first(i):
            load_tok = pltpu.make_async_copy(tokens.at[part(i, step)], tmp_low.at[0], tok_sem)
            load_tok.start()
            load_tok.wait()
            to = pl.ds(pl.multiple_of(n.core * rows + i * step, step), step)
            xa[to, :] = rms_rows(tmp_low[0].astype(F32), attn_gain[...]).astype(BF16)

        tok_sem = n.sem()
        loop(steps, norm_first)
        first_copy = n.send(xa.at[my_rows], xa.at[my_rows], n.other_core())
        for r in range(1, quads):
            qkv.z(r)
            qkv.x(r)
        tick("G")
        grad_copy = n.send(out_grad, grad_full.at[my_rows], n.other_core())
        grad_keep = n.keep(out_grad, grad_full.at[my_rows])
        start_load = load([(start_in, start_col)])
        for o in ones:
            o[...] = jnp.ones((4 * rows, d), BF16)
        acc[...] = jnp.zeros_like(acc)
        first_copy.wait_recv()
        qkv.arrived()
        load_now([(qkv_full, w_qkv)])

        def project(i):
            at = part(i, tall)
            proj[at, :] = dot(xa[at, :], w_qkv[...])
            cos, sin = cosine[at, :], sine[at, :]

            def prep(col, gain):
                u = rms_rows(proj[at, pl.ds(col, d)], gain[...])
                return (u * cos + pltpu.roll(u, d // 2, 1) * sin).astype(BF16)

            for h in range(2):
                for g in range(2):
                    low[h, at, pl.ds(g * d, d)] = prep((2 * h + g) * d, q_gain)
                low[h, at, pl.ds(2 * d, d)] = prep((4 + h) * d, k_gain)
                low[h, at, pl.ds(3 * d, d)] = proj[at, pl.ds((6 + h) * d, d)].astype(BF16)

        loop(2 * rows // tall, project)
        head_copy = n.copy(low.at[1 - n.x], plane.at[my_chip], n.other_x())
        head_copy.start()
        n.keep(proj, proj_s)
        plane[my_chip, :] = low[n.x]
        tick("P0")

        def flip_first(i):
            at = part(i, tall)
            w_qkv[at, :] = xa[:, at].T

        loop(width // tall, flip_first)
        n.keep(w_qkv, first_t)
        head_copy.wait()
        keys[0][...] = plane[:, pl.ds(2 * d, d)]
        vals[0][:, pl.ds(0, d)] = plane[:, pl.ds(3 * d, d)]

        ahead = n.at(quad=jnp.minimum(n.quad + 1, quads - 1))
        hops = [
            [
                n.copy(keys[h], keys[h + 1], ahead),
                n.copy(vals[h].at[:, pl.ds(0, d)], vals[h + 1].at[:, pl.ds(0, d)], ahead),
            ]
            for h in range(top)
        ]

        def hop_start(h):
            @pl.when((n.quad >= h) & (n.quad < quads - 1))
            def _():
                for c in hops[h]:
                    c.start()

        def hop_sent(h):
            @pl.when((n.quad >= h) & (n.quad < quads - 1))
            def _():
                for c in hops[h]:
                    c.wait_send()

        def hop_arrived(h):
            @pl.when(n.quad >= h + 1)
            def _():
                for c in hops[h]:
                    c.wait_recv()

        def attend(h, i, j):
            q_at, k_at = part(i, rows), part(j, rows)
            q2 = jnp.concatenate([plane[q_at, pl.ds(0, d)], plane[q_at, pl.ds(d, d)]], axis=0)
            prob = jnp.exp2(dot(q2, keys[h][k_at, :], NT) * (scale * LOG2E))
            k_pos = (4 * (n.quad - h) + j) * rows + lax.broadcasted_iota(jnp.int32, (rows, rows), 1)
            keep = k_pos >= start_col[q_at, :]
            if h == 0:
                q_pos = (4 * n.quad + i) * rows + lax.broadcasted_iota(jnp.int32, (rows, rows), 0)
                keep = keep & (k_pos <= q_pos)
            prob = jnp.where(jnp.concatenate([keep, keep], axis=0), prob, 0.0)
            acc[i] += dot(prob.astype(BF16), vals[h][k_at, :])

        def sweep(h, lo, hi, mid):
            def over_i(i, carry):
                pl.when(i == MID[h])(mid)

                def over_j(j, inner):
                    attend(h, i, j)
                    return inner

                lax.fori_loop(lo(i), hi(i), over_j, 0)
                return carry

            lax.fori_loop(0, 4, over_i, 0)

        start_load[0].wait()
        hop_start(0)
        tick("P1")
        sweep(0, *ranges[0], lambda: tick("P1b"))
        tick("P2")
        hop_arrived(0)
        hop_start(1)
        tick("P3")

        tick_within(1, lambda mid: sweep(1, *ranges[1], mid), "P3b")

        tick("P4")
        need(tiles)
        load_o = load([(o_full, w_o)])
        saves = load([(plane, plane_s)])
        hop_arrived(1)
        tick("P5")

        @pl.when(n.quad >= 2)
        def _():
            sweep(2, *ranges[2], lambda: None)

        for i in range(4):
            at = pl.ds(i * rows, rows)
            total = acc[i, :, d:]
            done = acc[i, :, :d] / total
            heads[at, pl.ds(0, d)] = done[:rows]
            heads[at, pl.ds(d, d)] = done[rows:]
            logs = jnp.log2(total)
            stat[0:1, at] = logs[:rows].T[0:1]
            stat[1:2, at] = logs[rows:].T[0:1]
        low[0, :, pl.ds(0, 2 * d)] = heads[other_chip, :].astype(BF16)
        attn_copy = n.send(low.at[0, :, pl.ds(0, 2 * d)], attn.at[n.x], n.other_x())
        tick("P6")
        attn[n.x] = heads[my_chip, :].astype(BF16)
        n.keep(heads, heads_s)
        n.keep(stat, stat_s)
        for h in range(top + 1):
            at = pl.ds(h * 4 * rows, 4 * rows)
            saves += load([(keys[h], k_s.at[at]), (vals[h].at[:, pl.ds(0, d)], v_s.at[at])])
        for h in range(top):
            hop_sent(h)
        grad_copy.wait_recv()
        grad_keep.wait()
        n.pending.remove(grad_keep.wait)
        first_copy.wait_send()
        n.pending.remove(first_copy.wait_send)
        g_load = load([(grad_full, xa)])
        for c in load_o + saves:
            c.wait()
        attn_copy.wait_recv()
        tick("P7")

        def o_rows(at):
            return dot(attn[0, at, :], w_o[:, : 2 * d], NT) + dot(attn[1, at, :], w_o[:, 2 * d :], NT)

        second_copies = []
        low_copies = core_then_tensor(o_rows, core_send, 3, tmp_low)
        tick("P8")
        for c in g_load:
            c.wait()

        def flip_grad(i):
            at = part(i, tall)
            tb[at, :] = xa[:, at].T

        loop(width // tall, flip_grad)
        tick("P8b")
        for i in range(steps):
            at = pl.ds(i * step, step)
            low_copies[i].wait_recv()
            load_now([(low_land.at[3, at], tmp_low.at[0]), (tokens.at[at], tmp_low.at[1])])
            mid = tmp_low[1].astype(F32) + (low_send[at, :].astype(F32) + tmp_low[0].astype(F32))
            tmp[...] = mid
            mid_copy = load([(tmp, middle_s.at[at])])
            to = pl.ds(my_at + i * step, step)
            sa[to, :] = rms_rows(mid, mlp_gain[...]).astype(BF16)
            second_copies.append(n.send(sa.at[to], sa.at[to], n.other_core()))
            ta[:, to] = sa[to, :].T
            mid_copy[0].wait()
        for i in range(steps):
            second_copies[i].wait_recv()
            to = pl.ds(their_at + i * step, step)
            ta[:, to] = sa[to, :].T
        tick("P9")
        n.finish()

    ranges = {
        0: (lambda i: 0, lambda i: i + 1),
        1: (lambda i: 0, lambda i: 4),
        2: (lambda i: i, lambda i: 4),
    }
    pl.run_scoped(
        forward,
        bf(width, 8 * d),
        f32(2 * rows, 8 * d),
        bf(2, 2 * rows, 4 * d),
        f32(4, 2 * rows, 2 * d),
        f32(4 * rows, 2 * d),
        f32(2, 4 * rows),
        bf(width, 4 * d),
        bf(rows, width),
        f32(step, width),
        bf(2, step, width),
        pltpu.VMEM((4 * rows, 1), jnp.int32),
    )

    def row_block(xr, s):
        bits = quads.bit_length() - 1
        quad = n.flipped(sum(((s >> b) & 1) << (bits - 1 - b) for b in range(bits)))
        x = n.x if xr == 0 else 1 - n.x
        return pl.multiple_of((quad * 4 + 2 * x) * shard, block)

    low_sent = [n.sem() for _ in range(steps)]
    low_got = [n.sem() for _ in range(steps)]

    def feed_forward(w, mlp, ds, acts, stage, w_sem, stage_sem):
        def fetch(f, slot):
            pltpu.make_async_copy(ff_full.at[f], w.at[slot], w_sem.at[slot]).start()

        tick("F0a")
        need(0)
        fetch(0, 0)
        mlp[...] = jnp.zeros_like(mlp)
        ds[...] = jnp.zeros_like(ds)

        def staged(f):
            for k, dst in enumerate((ff_keep, ff_send)):
                yield pltpu.make_async_copy(stage.at[k], dst.at[f], stage_sem.at[k])

        def at_tile(f, k, fn):
            pl.when(f == k)(fn)

        def tile(f, carry):
            slot = lax.rem(f, 2)

            def before(c):
                if c > 0:
                    tick("F%da" % c)
                if c + 1 < tiles:
                    need(c + 1)

            for c in range(tiles):
                at_tile(f, c, partial(before, c))

            @pl.when(f + 1 < tiles)
            def _():
                fetch(f + 1, 1 - slot)

            wait_bytes(w.at[slot], w_sem.at[slot])

            def some_rows(i):
                at = part(i, rows)
                gate = dot(sa[at, :], w[slot, :, pl.ds(0, ft)])
                up = dot(sa[at, :], w[slot, :, pl.ds(ft, ft)])
                d_act = dot(xa[at, :], w[slot, :, pl.ds(2 * ft, ft)])
                sig = 1.0 / (1.0 + jnp.exp(-gate))
                silu = gate * sig
                acts[at, pl.ds(2 * ft, ft)] = (silu * up).astype(BF16)
                acts[at, pl.ds(0, ft)] = (d_act * up * sig * (1.0 + gate * (1.0 - sig))).astype(BF16)
                acts[at, pl.ds(ft, ft)] = (d_act * silu).astype(BF16)
                mlp[at, :] += dot(acts[at, pl.ds(2 * ft, ft)], w[slot, :, pl.ds(2 * ft, ft)], NT)
                ds[at, :] += dot(acts[at, pl.ds(0, ft)], w[slot, :, pl.ds(0, ft)], NT) + dot(
                    acts[at, pl.ds(ft, ft)], w[slot, :, pl.ds(ft, ft)], NT
                )

            loop(2, some_rows)

            @pl.when(f >= 1)
            def _():
                for c in staged(f - 1):
                    c.wait()

            for c in range(tiles):
                at_tile(f, c, partial(tick, "F%db" % c))
            for xr in range(2):
                for q in range(quads):
                    at = pl.ds(row_block(xr, q), block)
                    to = pl.ds(q * block, block)
                    stage[xr, to, pl.ds(0, 2 * ft)] = dot(ta[at, :], acts[:, pl.ds(0, 2 * ft)]).astype(BF16)
                    stage[xr, to, pl.ds(2 * ft, ft)] = dot(tb[at, :], acts[:, pl.ds(2 * ft, ft)]).astype(BF16)
            for c in staged(f):
                c.start()

            return carry

        lax.fori_loop(0, tiles, tile, 0)
        core_copies = []
        for i in range(steps):
            at = pl.ds(i * step, step)
            xa[at, :] = ds[pl.ds(their_at + i * step, step), :].astype(BF16)
            core_copies.append(n.copy(xa.at[at], core_land.at[0, at], n.other_core()))
            core_copies[-1].start()
        for c in staged(tiles - 1):
            c.wait()
        for i in range(steps):
            at = pl.ds(i * step, step)
            core_copies[i].wait_recv()
            spare = xa.at[pl.ds(rows + i * step, step)]
            load_now([(core_land.at[0, at], spare)])
            low_send[at, :] = (ds[pl.ds(my_at + i * step, step), :] + spare[...].astype(F32)).astype(BF16)
            n.copy(
                low_send.at[at], low_land.at[0, at], n.other_tensor(), low_sent[i], low_got[i]
            ).start()

        tick("B0")
        def to_low(i):
            at = part(i, step)
            sa[at, :] = mlp[at, :].astype(BF16)

        loop(2 * rows // step, to_low)
        mlp_copy = n.copy(sa.at[pl.ds(their_at, rows)], core_land.at[1], n.other_core())
        mlp_copy.start()
        mlp_keep = load([(sa.at[my_rows], mlp_own)])
        for c in core_copies:
            c.wait_send()
        mlp_copy.wait()
        mlp_keep[0].wait()

    pl.run_scoped(
        feed_forward,
        bf(2, width, ff_cols),
        f32(2 * rows, width),
        f32(2 * rows, width),
        bf(2 * rows, ff_cols),
        bf(2, 2 * rows, ff_cols),
        pltpu.SemaphoreType.DMA((2,)),
        pltpu.SemaphoreType.DMA((2,)),
    )

    def backward(
        d_middle, tmp, tmp_low, vx, heads, stat, d_out, d_q, d_kv, kv_low, d_low, d_proj
    ):
        loads = load(
            [(o_full, ta.at[:, pl.ds(0, 4 * d)]), (plane_s, tb.at[:, pl.ds(0, 4 * d)]), (v_s, vx), (heads_s, heads)]
            + [(stat_s, stat.at[pl.ds(0, 2)])]
            + [
                (k_s.at[pl.ds(h * 4 * rows, 4 * rows)], tb.at[:, pl.ds((4 + h) * d, d)])
                for h in range(top + 1)
            ]
        )
        early = load([(middle_s, d_middle), (out_grad, xa.at[my_rows])])
        gains[...] = jnp.zeros_like(gains)

        tick("B1")
        for i in range(steps):
            at = pl.ds(i * step, step)
            load_now([(mlp_own.at[at], tmp_low.at[0]), (core_land.at[1, at], tmp_low.at[1])])
            tmp_low[0] = (tmp_low[0].astype(F32) + tmp_low[1].astype(F32)).astype(BF16)
            load_now([(tmp_low.at[0], mlp_low.at[at])])

        tick("B2")
        for c in early:
            c.wait()
        da_copies = []
        for i in range(steps):
            at = pl.ds(i * step, step)
            to = pl.ds(my_at + i * step, step)
            wait_bytes(low_land.at[0, at], low_got[i])
            load_now([(low_land.at[0, at], tmp_low.at[0])])
            d_second = low_send[at, :].astype(F32) + tmp_low[0].astype(F32)
            back, gain_part = norm_back(d_middle[at, :], mlp_gain[...], d_second)
            gains[1:2, :] += gain_part
            d_mid = xa[to, :].astype(F32) + back
            d_middle[at, :] = d_mid
            xa[to, :] = d_mid.astype(BF16)
            da_copies.append(n.copy(xa.at[to], da_land.at[at], n.other_core()))
            da_copies[-1].start()
        mlp_copy = n.send(mlp_low, low_land.at[1], n.other_tensor())
        for i in range(steps):
            wait_bytes(low_send.at[pl.ds(i * step, step)], low_sent[i])
        for c in loads:
            c.wait()
        for c in da_copies:
            c.wait()
        load_now([(da_land, xa.at[pl.ds(their_at, rows)])])

        def head_grads(i):
            at = part(i, tall)
            got = dot(xa[at, :], ta[:, pl.ds(0, 4 * d)]).astype(BF16)
            d_low[0, at, pl.ds(0, 2 * d)] = got[:, : 2 * d]
            d_low[1, at, pl.ds(0, 2 * d)] = got[:, 2 * d :]

        loop(2 * rows // tall, head_grads)
        heads_copy = n.copy(d_low.at[1 - n.x, :, pl.ds(0, 2 * d)], heads_land, n.other_x())
        heads_copy.start()
        tick("B3")
        d_out[my_chip, :] = d_low[n.x, :, pl.ds(0, 2 * d)]
        d_q[...] = jnp.zeros_like(d_q)

        def flip(i):
            at = part(i, tall)
            ta[at, :] = xa[:, at].T

        loop(width // tall, flip)

        def weight_pieces(right, k):
            for xr in range(2):
                for q in range(quads):
                    sa[pl.ds(q * block, block), pl.ds((2 * k + xr) * 4 * d, 4 * d)] = dot(
                        ta[pl.ds(row_block(xr, q), block), :], right
                    ).astype(BF16)

        def stage_out(k, g):
            return load(
                [
                    (sa.at[:, pl.ds((2 * k + xr) * 4 * d, 4 * d)], dst.at[g])
                    for xr, dst in enumerate((at_keep, at_send))
                ]
            )

        weight_pieces(jnp.concatenate([attn[0], attn[1]], axis=1), 0)
        o_stage = stage_out(0, 0)
        heads_copy.wait()
        load_now([(heads_land, d_out.at[other_chip])])
        for c in o_stage:
            c.wait()
        tick("B4")

        for g in range(2):
            for i in range(4):
                at = pl.ds(i * rows, rows)
                cols = pl.ds(g * d, d)
                prod = d_out[at, cols].astype(F32) * heads[at, cols]
                stat[2 + g : 3 + g, at] = jnp.sum(prod.T, axis=0, keepdims=True)
        q_proj = load(
            [
                (proj_s.at[:, pl.ds(h * 2 * d, 2 * d)], heads.at[pl.ds(h * 2 * rows, 2 * rows)])
                for h in range(2)
            ]
        )

        def attend_back(h, i, j):
            q_at, k_at = part(i, rows), part(j, rows)
            q2 = jnp.concatenate([tb[q_at, pl.ds(0, d)], tb[q_at, pl.ds(d, d)]], axis=0)
            g2 = jnp.concatenate([d_out[q_at, pl.ds(0, d)], d_out[q_at, pl.ds(d, d)]], axis=0)
            log_total = jnp.concatenate([stat[0:1, q_at], stat[1:2, q_at]], axis=1)
            row_dot = jnp.concatenate([stat[2:3, q_at], stat[3:4, q_at]], axis=1)
            k_now = tb[k_at, pl.ds((4 + h) * d, d)]
            v_now = vx[pl.ds(pl.multiple_of(h * 4 * rows + j * rows, rows), rows), :]
            prob = jnp.exp2(dot(k_now, q2, NT) * (scale * LOG2E) - log_total)
            k_pos = (4 * (n.quad - h) + j) * rows + lax.broadcasted_iota(jnp.int32, (rows, rows), 0)
            keep = k_pos >= start_row[:, q_at]
            if h == 0:
                q_pos = (4 * n.quad + i) * rows + lax.broadcasted_iota(jnp.int32, (rows, rows), 1)
                keep = keep & (k_pos <= q_pos)
            prob = jnp.where(jnp.concatenate([keep, keep], axis=1), prob, 0.0)
            d_prob = dot(v_now, g2, NT)
            d_score = (prob * (d_prob - row_dot)).astype(BF16)
            d_kv[k_at, pl.ds(d, d)] += dot(prob.astype(BF16), g2)
            d_kv[k_at, pl.ds(0, d)] += dot(d_score, q2)
            got = dot(d_score, k_now, TN)
            d_q[q_at, pl.ds(0, d)] += got[:rows]
            d_q[q_at, pl.ds(d, d)] += got[rows:]

        def plane_back(h, lo, hi, mid):
            d_kv[...] = jnp.zeros_like(d_kv)

            def over_i(i, carry):
                pl.when(i == MID[h])(mid)

                def over_j(j, inner):
                    attend_back(h, i, j)
                    return inner

                lax.fori_loop(lo(i), hi(i), over_j, 0)
                return carry

            lax.fori_loop(0, 4, over_i, 0)
            d_kv[:, pl.ds(0, d)] = d_kv[:, pl.ds(0, d)] * scale

        behind = n.at(quad=jnp.maximum(n.quad - 1, 0))
        hops = [n.copy(kv_low.at[k], kv_land.at[k], behind) for k in range(top)]
        kv_sem = n.sem()

        def add_landed(k):
            hops[k].wait_recv()
            for p in range(2):
                at = pl.ds(p * 2 * rows, 2 * rows)
                c = pltpu.make_async_copy(kv_land.at[k, at], d_low.at[p, :, pl.ds(2 * d, 2 * d)], kv_sem)
                c.start()
                c.wait()
                d_kv[at, :] += d_low[p, :, pl.ds(2 * d, 2 * d)].astype(F32)

        for h in range(top, 0, -1):

            def one_plane(mid, h=h):
                plane_back(h, *ranges[h], mid)
                if h < top:

                    @pl.when(n.quad < quads - 1)
                    def _():
                        add_landed(top - h - 1)

                kv_low[top - h] = d_kv[...].astype(BF16)
                hops[top - h].start()

            tick_within(h, one_plane, "C%d" % h)
            tick("C%de" % h)
        plane_back(0, *ranges[0], lambda: tick("C0"))

        def put_back(x, first, source, factor):
            def body(i):
                at = part(i, tall)
                src = pl.ds(pl.multiple_of(x * 2 * rows + i * tall, tall), tall)
                d_low[x, at, pl.ds(first, 2 * d)] = (source[src, :] * factor).astype(BF16)

            loop(2 * rows // tall, body)

        q_cols, kv_cols = pl.ds(0, 2 * d), pl.ds(2 * d, 2 * d)
        put_back(1 - n.x, 0, d_q, scale)
        q_back = n.copy(d_low.at[1 - n.x, :, q_cols], back_land.at[:, q_cols], n.other_x())
        q_back.start()
        put_back(n.x, 0, d_q, scale)
        k_proj = load([(proj_s.at[:, pl.ds(4 * d, 2 * d)], d_q.at[pl.ds(0, 2 * rows)])])
        late = load([(first_t, ta), (qkv_full, tb)])

        tick("D0")
        @pl.when(n.quad < quads - 1)
        def _():
            add_landed(top - 1)

        put_back(1 - n.x, 2 * d, d_kv, 1.0)
        kv_back = n.copy(d_low.at[1 - n.x, :, kv_cols], back_land.at[:, kv_cols], n.other_x())
        kv_back.start()
        put_back(n.x, 2 * d, d_kv, 1.0)
        tick("D1")
        q_back.wait()
        load_now([(back_land.at[:, q_cols], d_low.at[1 - n.x, :, q_cols])])

        def prep_back(cols):
            def body(i):
                at = part(i, tall)
                cos, sin = cosine[at, :], sine[at, :]
                for col, h, src, gain, row, read in cols:
                    grad = d_low[h, at, pl.ds(src, d)]
                    if gain is not None:
                        grad = grad.astype(F32)
                        grad = grad * cos + pltpu.roll(grad * sin, d // 2, 1)
                        grad, gain_part = norm_back(read(i), gain[...], grad)
                        gains[pl.ds(row, 1), pl.ds(0, d)] += gain_part
                    d_proj[at, pl.ds(col, d)] = grad.astype(BF16)

            loop(2 * rows // tall, body)

        def q_read(h, g):
            return lambda i: heads[
                pl.ds(pl.multiple_of(h * 2 * rows + i * tall, tall), tall), pl.ds(g * d, d)
            ]

        def k_read(h):
            return lambda i: d_q[part(i, tall), pl.ds(h * d, d)]

        for c in q_proj:
            c.wait()
        prep_back(
            [
                ((2 * h + g) * d, h, g * d, q_gain, 2, q_read(h, g))
                for h in range(2)
                for g in range(2)
            ]
        )
        for c in late:
            c.wait()
        weight_pieces(d_proj[:, pl.ds(0, 4 * d)], 0)
        for c in stage_out(0, 1):
            c.wait()
        at_groups[1].start()
        tick("D2")
        kv_back.wait()
        load_now([(back_land.at[:, kv_cols], d_low.at[1 - n.x, :, kv_cols])])
        for c in k_proj:
            c.wait()
        prep_back(
            [((4 + h) * d, h, 2 * d, k_gain, 3, k_read(h)) for h in range(2)]
            + [((6 + h) * d, h, 3 * d, None, None, None) for h in range(2)]
        )

        low_copies = core_then_tensor(
            lambda at: dot(d_proj[at, :], tb[...], NT), xa.at[pl.ds(0, rows)], 2, tmp_low
        )

        weight_pieces(d_proj[:, pl.ds(4 * d, 4 * d)], 1)
        for c in stage_out(1, 2):
            c.wait()
        at_groups[2].start()
        tick("D3")

        mlp_copy.wait_recv()
        for i in range(steps):
            at = pl.ds(i * step, step)
            load_now(
                [
                    (low_land.at[1, at], tmp_low.at[0]),
                    (mlp_low.at[at], tmp_low.at[1]),
                    (middle_s.at[at], tmp),
                ]
            )
            tmp_low[0] = (tmp[...] + (tmp_low[1].astype(F32) + tmp_low[0].astype(F32))).astype(BF16)
            load_now([(tmp_low.at[0], output.at[at])])
        tick("D4")
        for i in range(steps):
            at = pl.ds(i * step, step)
            low_copies[i].wait_recv()
            load_now([(low_land.at[2, at], tmp_low.at[0]), (tokens.at[at], tmp_low.at[1])])
            d_first = low_send[at, :].astype(F32) + tmp_low[0].astype(F32)
            back, gain_part = norm_back(tmp_low[1].astype(F32), attn_gain[...], d_first)
            gains[0:1, :] += gain_part
            d_middle[at, :] = d_middle[at, :] + back
            n.keep(d_middle.at[at], input_grad.at[at])

        for k, to in enumerate((n.other_core(), n.other_x(), n.other_tensor())):
            c = n.copy(gains, gains_land.at[k], to)
            c.start()
            c.wait()
            if k < 2:
                gains[...] += gains_land[k]
            else:
                gains[2:4, :] += gains_land[k, 2:4, :]
        gains_land[3 + n.quad] = gains[...]
        quad_copies = []
        for s in range(1, quads):
            to = n.at(quad=lax.rem(n.quad + s, quads))
            quad_copies.append(n.copy(gains, gains_land.at[3 + n.quad], to))
            quad_copies[-1].start()
        for c in quad_copies:
            c.wait()
        total = gains_land[3]
        for k in range(1, quads):
            total = total + gains_land[3 + k]
        gains[...] = total
        n.keep(gains, gain_out)
        tick("D5")
        for g in (ff + at_groups)[-SLOTS:]:
            g.sent()
        for k in range(top):

            @pl.when(n.quad >= top - k)
            def _(k=k):
                hops[k].wait_send()

        n.finish()
        for g in [qkv, o_w] + ffw:
            g.finish()
        assert n.used <= sems.shape[0], n.used


    pl.run_scoped(
        backward,
        f32(rows, width),
        f32(step, width),
        bf(2, step, width),
        bf(4 * rows * (top + 1), d),
        f32(4 * rows, 2 * d),
        f32(4, 4 * rows),
        bf(4 * rows, 2 * d),
        f32(4 * rows, 2 * d),
        f32(4 * rows, 2 * d),
        bf(top, 4 * rows, 2 * d),
        bf(2, 2 * rows, 4 * d),
        bf(2 * rows, 8 * d),
    )


def whole_layer(tokens, out_grad, attn_gain, mlp_gain, q_gain, k_gain, *arrays):
    rows, width = tokens.shape
    d = q_gain.shape[0]
    wg = arrays[-1]
    shard = wg.shape[0]
    quads = lax.axis_size("dp") // 4
    tiles, half_ff = 6, wg.shape[1] // 2
    cols = 3 * half_ff // tiles
    top = REACH // 4
    widest = max(cols, 4 * d)
    assert top == 2 and width == 4 * rows and 2 * rows == 8 * d
    vmem = pl.BlockSpec(memory_space=pltpu.VMEM)
    hbm = pl.BlockSpec(memory_space=pl.ANY)

    def bf(*shape):
        return jax.ShapeDtypeStruct(shape, BF16)

    def f32(*shape):
        return jax.ShapeDtypeStruct(shape, F32)

    out_shape = [bf(rows, width), f32(rows, width), f32(4, width)]
    out_shape += [f32(shard, 8 * d), f32(shard, 4 * d), f32(shard, 4 * d), f32(shard, 8 * d)]
    out_shape += [f32(shard, 2 * half_ff)] * 3
    out_shape += [bf(width, 8 * d), bf(width, 4 * d), bf(tiles, width, cols)]
    out_shape += [bf(2 * rows, width), bf(width, 2 * rows), f32(2 * rows, 8 * d), bf(4 * rows, 4 * d)]
    out_shape += [bf(4 * rows * (top + 1), d)] * 2
    out_shape += [f32(4 * rows, 2 * d), f32(2, 4 * rows), f32(rows, width)]
    out_shape += [bf(tiles, width // 2, cols)] * 3 + [bf(tiles, width // 2 + 4 * shard, cols)]
    out_shape += [bf(3, width // 2, 4 * d)] * 3 + [bf(3, width // 2 + 4 * shard, 4 * d)]
    out_shape += [bf(4, rows, width)] * 2
    out_shape += [bf(rows, width)] * 3
    out_shape += [bf(2 * rows, 2 * d), bf(top, 4 * rows, 2 * d), bf(2 * rows, 4 * d)]
    return pl.pallas_call(
        layer_kernel,
        in_specs=[hbm] * 2 + [vmem] * 6 + [hbm, vmem] + [hbm] * 7,
        out_specs=[hbm] * len(out_shape),
        out_shape=out_shape,
        scratch_shapes=[
            pltpu.SemaphoreType.DMA((330 + 36 * quads,)),
            pltpu.VMEM((2 * rows, width), BF16),
            pltpu.VMEM((2 * rows, width), BF16),
            pltpu.VMEM((width, 2 * rows), BF16),
            pltpu.VMEM((width, 2 * rows), BF16),
            pltpu.VMEM((2, 2 * rows, 2 * d), BF16),
            pltpu.VMEM((width // 2, widest), BF16),
            pltpu.VMEM((SLOTS, width // 2, widest), BF16),
            pltpu.VMEM((2, shard, widest), F32),
            pltpu.VMEM((rows, width), BF16),
            pltpu.VMEM((4, width), F32),
            pltpu.VMEM((3 + quads, 4, width), F32),
        ],
        compiler_params=pltpu.CompilerParams(
            collective_id=0, has_side_effects=True, vmem_limit_bytes=VMEM_LIMIT
        ),
        name="layer",
    )(
        tokens,
        out_grad,
        attn_gain[None],
        mlp_gain[None],
        q_gain[None],
        k_gain[None],
        *arrays,
    )[:10]


def local(
    tokens,
    out_grad,
    lengths,
    attn_gain,
    q_weight,
    key_matrix,
    value_matrix,
    o_weight,
    q_gain,
    k_gain,
    mlp_gain,
    gate_weight,
    up_weight,
    down_weight,
):
    rows = tokens.shape[0]
    d = q_gain.shape[0]
    me = lax.axis_index("dp")
    assert key_matrix.shape[1] == 4 * d and q_weight.shape[1] == 8 * d
    chip_index = (me // 2) * 2 * rows + jnp.arange(2 * rows, dtype=jnp.int32)
    cosine, sine_vals = angles(chip_index - starts_of(chip_index, lengths), d)
    sine_signed = jnp.concatenate([-sine_vals[:, : d // 2], sine_vals[:, d // 2 :]], 1)
    q_index = (me // 4) * 4 * rows + jnp.arange(4 * rows, dtype=jnp.int32)
    q_start = starts_of(q_index, lengths)
    output, input_grad, gains, g_q, g_k, g_v, g_o, g_gate, g_up, g_down = whole_layer(
        tokens,
        out_grad,
        attn_gain,
        mlp_gain,
        q_gain,
        k_gain,
        cosine,
        sine_signed,
        q_start[:, None],
        q_start[None, :],
        q_weight,
        key_matrix,
        value_matrix,
        o_weight,
        gate_weight,
        up_weight,
        down_weight,
    )
    return (
        output,
        input_grad,
        gains[0],
        g_q,
        g_k,
        g_v,
        g_o,
        gains[2, :d],
        gains[3, :d],
        gains[1],
        g_gate,
        g_up,
        g_down,
    )


def solution(mesh):
    rows, weight = P("dp", None), P("dp", "tensor")
    placed = (
        (rows, rows) + (P(),) * 2 + (weight,) * 4 + (P(),) * 3 + (weight,) * 3
    )
    return jax.shard_map(
        local,
        mesh=mesh,
        in_specs=placed,
        out_specs=(rows, rows, P()) + (weight,) * 4 + (P(),) * 3 + (weight,) * 3,
        check_vma=False,
    )
```

```python
from functools import partial
import math

import jax
import jax.numpy as jnp
from jax import lax
from jax.experimental import pallas as pl
from jax.experimental.pallas import tpu as pltpu
from jax.sharding import PartitionSpec as P

REACH = 8
EPS = 1e-06
THETA = 1000000.0
LOG2E = 1.4426950408889634
F32 = jnp.float32
BF16 = jnp.bfloat16
VMEM_LIMIT = 62 * 1024 * 1024

NT = (((1,), (1,)), ((), ()))
NN = (((1,), (0,)), ((), ()))
TN = (((0,), (0,)), ((), ()))
MESH = pl.DeviceIdType.MESH


def dot(a, b, dims=NN):
    return lax.dot_general(a, b, dims, preferred_element_type=F32)


def over_quads(value, by):
    n = lax.axis_size("dp")
    return lax.ppermute(value, "dp", [(i, (i + 4 * by) % n) for i in range(n)])


def shift_quads(value, by):
    n = lax.axis_size("dp")
    return lax.ppermute(
        value, "dp", [(i, i + 4 * by) for i in range(n) if 0 <= i + 4 * by < n]
    )


def swap_x(value):
    return lax.ppermute(value, "dp", [(i, i ^ 2) for i in range(lax.axis_size("dp"))])


def swap_core(value):
    return lax.ppermute(value, "dp", [(i, i ^ 1) for i in range(lax.axis_size("dp"))])


def swap_tensor(value):
    return lax.ppermute(value, "tensor", [(0, 1), (1, 0)])


def tensor_sum(part):
    low = part.astype(BF16)
    return low.astype(F32) + swap_tensor(low).astype(F32)


def rms_rows(values, gain_vec):
    return values * lax.rsqrt(jnp.mean(values * values, axis=-1, keepdims=True) + EPS) * gain_vec


def rotate(values):
    half_size = values.shape[-1] // 2
    return jnp.concatenate([-values[..., half_size:], values[..., :half_size]], axis=-1)


def head_prep(heads_view, gain_vec, cosine, sine_vals):
    normed = rms_rows(heads_view, gain_vec)
    return normed * cosine[:, None, :] + rotate(normed) * sine_vals[:, None, :]


def starts_of(index, lengths):
    ends = jnp.cumsum(lengths)
    starts = ends - lengths
    inside = (index[:, None] >= starts[None, :]) & (index[:, None] < ends[None, :])
    return jnp.sum(jnp.where(inside, starts[None, :], 0), axis=1)


def angles(position, head_dim):
    freq = THETA ** (-(jnp.arange(0, head_dim, 2, dtype=F32) / head_dim))
    turn = position.astype(F32)[:, None] * freq[None, :]
    turn = jnp.concatenate([turn, turn], axis=-1)
    return (jnp.cos(turn), jnp.sin(turn))


class Net:
    def __init__(self, sems):
        me = lax.axis_index("dp")
        self.me, self.tensor = me, lax.axis_index("tensor")
        self.core = lax.rem(me, 2)
        self.x = lax.rem(lax.div(me, 2), 2)
        self.quad = lax.div(me, 4)
        self.quads = lax.axis_size("dp") // 4
        self.sems, self.used = sems, 0
        self.pending = []
        self.to_core = self.at(core=1 - self.core)
        self.to_x = self.at(x=1 - self.x)
        self.to_tensor = self.at(tensor=1 - self.tensor)

    def sem(self):
        self.used += 1
        return self.sems.at[self.used - 1]

    def at(self, quad=None, x=None, core=None, tensor=None):
        quad = self.quad if quad is None else quad
        x = self.x if x is None else x
        core = self.core if core is None else core
        tensor = self.tensor if tensor is None else tensor
        return (quad * 4 + x * 2 + core, tensor)

    def flipped(self, bits):
        quad, bit = self.quad, 1
        while bit <= bits:
            if bits & bit:
                quad = quad + bit * (1 - 2 * lax.rem(lax.div(self.quad, bit), 2))
            bit *= 2
        return quad

    def other_core(self):
        return self.to_core

    def other_x(self):
        return self.to_x

    def other_tensor(self):
        return self.to_tensor

    def greet(self):
        targets = [self.other_core(), self.other_x(), self.other_tensor()]
        for s in range(1, self.quads):
            for c in range(2):
                targets.append(self.at(quad=lax.rem(self.quad + s, self.quads), core=c))
        barrier = pltpu.get_barrier_semaphore()
        for t in targets:
            pl.semaphore_signal(barrier, inc=1, device_id=t, device_id_type=MESH)
        pl.semaphore_wait(barrier, len(targets))

    def copy(self, src, dst, to, send=None, recv=None):
        return pltpu.make_async_remote_copy(
            src_ref=src,
            dst_ref=dst,
            send_sem=self.sem() if send is None else send,
            recv_sem=self.sem() if recv is None else recv,
            device_id=to,
            device_id_type=MESH,
        )

    def send(self, src, dst, to):
        c = self.copy(src, dst, to)
        c.start()
        self.pending.append(c.wait_send)
        return c

    def keep(self, src, dst):
        c = pltpu.make_async_copy(src, dst, self.sem())
        c.start()
        self.pending.append(c.wait)
        return c

    def finish(self):
        for wait in self.pending:
            wait()
        self.pending = []


def wait_bytes(ref, sem):
    pltpu.make_async_copy(ref, ref, sem).wait()


class Gather:
    def __init__(self, net, full, shard, kinds, paired=False):
        self.net, self.full, self.shard, self.kinds, self.paired = net, full, shard, kinds, paired
        self.z_rows = (4 if paired else 2) * shard
        rounds = range(net.quads)
        self.z_got = [[net.sem() for _ in rounds[1:]] for _ in range(2)]
        self.x_got = [[net.sem() for _ in rounds[1:]] for _ in range(2)]
        self.z_sent = [net.sem(), net.sem()]
        self.x_own, self.x_sent, self.own, self.core_got, self.core_sent = [net.sem() for _ in range(5)]

    def rows(self, quad, x):
        at = (quad * 4 + 2 * x) * self.shard
        return self.full.at[pl.ds(pl.multiple_of(at, self.shard), 2 * self.shard)]

    def z_block(self, quad):
        if self.paired:
            return self.full.at[pl.ds(pl.multiple_of(quad * self.z_rows, self.z_rows), self.z_rows)]
        return self.rows(quad, self.net.x)

    def start(self):
        n = self.net
        mine = pl.ds(pl.multiple_of(n.me * self.shard, self.shard), self.shard)
        for arr, first, wide, into in self.kinds:
            half = arr.shape[1] // 2
            there = self.full.at[mine, pl.ds(into, wide)]

            def cut(core):
                return arr.at[:, pl.ds(pl.multiple_of(core * half + first, 128), wide)]

            pltpu.make_async_copy(cut(n.core), there, self.own).start()
            n.copy(cut(1 - n.core), there, n.other_core(), self.core_sent, self.core_got).start()

    def sides(self, r):
        n = self.net
        for side, way in enumerate((1, -1)):
            quad = n.quad - way * r
            near = n.quad + way
            last = n.quads - 1
            here = (quad >= 0) & (quad <= last)
            on = here & (near >= 0) & (near <= last)
            yield side, here, jnp.clip(quad, 0, last), on, jnp.clip(near, 0, last)

    def z(self, r):
        n = self.net
        if r == 0:
            if self.paired:
                wait_bytes(self.rows(n.quad, 1 - n.x), self.x_own)
            else:
                self.own_here()
        for side, here, quad, on, near in self.sides(r):
            if r > 0:

                @pl.when(here)
                def _():
                    wait_bytes(self.z_block(quad), self.z_got[side][r - 1])

            if r < n.quads - 1:

                @pl.when(on)
                def _():
                    block = self.z_block(quad)
                    n.copy(block, block, n.at(quad=near), self.z_sent[side], self.z_got[side][r]).start()

    def own_here(self):
        half = self.full.at[pl.ds(0, self.shard)]
        wait_bytes(half, self.own)
        wait_bytes(half, self.core_got)

    def x(self, r):
        n = self.net
        if r == 0:
            if self.paired:
                self.own_here()
            block = self.rows(n.quad, n.x)
            n.copy(block, block, n.other_x(), self.x_sent, self.x_own).start()
            return
        if self.paired:
            return
        for side, here, quad, on, near in self.sides(r):

            @pl.when(here)
            def _():
                block = self.rows(quad, n.x)
                n.copy(block, block, n.other_x(), self.x_sent, self.x_got[side][r - 1]).start()

    def arrived(self):
        n = self.net
        if self.paired:
            return
        wait_bytes(self.rows(n.quad, 1 - n.x), self.x_own)
        for r in range(1, n.quads):
            for side, here, quad, on, near in self.sides(r):

                @pl.when(here)
                def _():
                    wait_bytes(self.rows(quad, 1 - n.x), self.x_got[side][r - 1])

    def finish(self):
        n = self.net
        wait_bytes(self.full.at[pl.ds(0, self.shard)], self.core_sent)
        wait_bytes(self.full.at[pl.ds(0, 2 * (1 if self.paired else n.quads) * self.shard)], self.x_sent)
        for k in range(n.quads):

            @pl.when(n.quad == k)
            def _():
                for side, count in enumerate((k + 1, n.quads - k)):
                    if count < n.quads:
                        wait_bytes(self.full.at[pl.ds(0, count * self.z_rows)], self.z_sent[side])


class Scatter:
    def __init__(self, net, keep, send, x_land, z_land, loaded, added, slot):
        self.net, self.keep, self.send, self.x_land, self.z_land = net, keep, send, x_land, z_land
        self.loaded, self.added, self.slot = loaded, added, slot
        self.shard = keep.shape[0] // (2 * net.quads)
        self.stages = net.quads.bit_length() - 1
        self.own_waited = False
        self.z_got = [net.sem() for _ in range(self.stages)]
        self.z_sent = [net.sem() for _ in range(self.stages)]
        self.x_sent, self.x_got, self.own, self.tmp = [net.sem() for _ in range(4)]

    def start(self):
        n = self.net
        n.copy(self.send, self.x_land, n.other_x(), self.x_sent, self.x_got).start()

    def left(self, stage):
        return self.keep.shape[0] >> stage

    def landing(self, stage):
        rows = self.keep.shape[0]
        return self.z_land.at[pl.ds(rows - self.left(stage), self.left(stage + 1))]

    def last(self, far, core, count=1):
        at = self.keep.shape[0] + (2 * far + core) * self.shard
        at = at if isinstance(at, int) else pl.multiple_of(at, self.shard)
        return self.z_land.at[pl.ds(at, count * self.shard)]

    def total(self):
        return self.added.at[self.slot, :, pl.ds(0, self.keep.shape[1])]

    def add_in(self, rows):
        total, other = self.total(), self.loaded.at[:, pl.ds(0, self.keep.shape[1])]

        def one(i, carry):
            at = pl.ds(pl.multiple_of(i * 128, 128), 128)
            total[at, :] = (total[at, :].astype(F32) + other[at, :].astype(F32)).astype(BF16)
            return carry

        lax.fori_loop(0, rows // 128, one, 0)

    def add(self):
        first = pltpu.make_async_copy(self.keep, self.total(), self.tmp)
        first.start()
        wait_bytes(self.x_land, self.x_got)
        second = pltpu.make_async_copy(
            self.x_land, self.loaded.at[:, pl.ds(0, self.keep.shape[1])], self.own
        )
        second.start()
        first.wait()
        second.wait()
        self.add_in(self.keep.shape[0])
        self.send_half(0)

    def pass_on(self):
        for stage in range(1, self.stages):
            rows = self.left(stage)
            wait_bytes(self.landing(stage - 1), self.z_got[stage - 1])
            load = pltpu.make_async_copy(
                self.landing(stage - 1),
                self.loaded.at[pl.ds(0, rows), pl.ds(0, self.keep.shape[1])],
                self.tmp,
            )
            load.start()
            load.wait()
            self.add_in(rows)
            self.send_half(stage)

    def send_half(self, stage):
        n, total = self.net, self.total()
        quad = n.flipped(1 << stage)
        sent, got = self.z_sent[stage], self.z_got[stage]
        if stage < self.stages - 1:
            half = total.at[pl.ds(self.left(stage + 1), self.left(stage + 1))]
            n.copy(half, self.landing(stage), n.at(quad=quad), sent, got).start()
            return

        def rows(far, core):
            at = (2 * far + core) * self.shard
            at = at if isinstance(at, int) else pl.multiple_of(at, self.shard)
            return total.at[pl.ds(at, self.shard)]

        for c in range(2):
            n.copy(rows(1, c), self.last(1, n.core), n.at(quad=quad, core=c), sent, got).start()
        n.copy(rows(0, 1 - n.core), self.last(0, n.core), n.other_core(), sent, got).start()
        pltpu.make_async_copy(rows(0, n.core), self.last(0, n.core), self.own).start()

    def sent(self):
        wait_bytes(self.send, self.x_sent)
        for stage in range(self.stages - 1):
            wait_bytes(self.landing(stage), self.z_sent[stage])
        wait_bytes(self.last(0, 0, 3), self.z_sent[-1])
        self.own_done()

    def own_done(self):
        if not self.own_waited:
            wait_bytes(self.last(0, 0), self.own)
        self.own_waited = True

    def final(self, out, write):
        shard, cols = self.shard, self.keep.shape[1]
        wait_bytes(self.last(0, 0, 3), self.z_got[-1])
        self.own_done()
        got = self.loaded.at[pl.ds(0, 4 * shard), pl.ds(0, cols)]
        load = pltpu.make_async_copy(self.last(0, 0, 4), got, self.tmp)
        load.start()
        load.wait()
        for c in range(2):
            near, far = pl.ds(c * shard, shard), pl.ds((2 + c) * shard, shard)
            out[c, :, pl.ds(0, cols)] = got[near, :].astype(F32) + got[far, :].astype(F32)
        for c in range(2):
            for at, wide, dst, col in write(c):
                pltpu.make_async_copy(
                    out.at[c, :, pl.ds(at, wide)], dst.at[:, pl.ds(col, wide)], self.tmp
                ).start()
        wait_bytes(out.at[:, :, pl.ds(0, cols)], self.tmp)


def norm_back(values, gain, grad):
    scale = lax.rsqrt(jnp.mean(values * values, axis=-1, keepdims=True) + EPS)
    scaled = grad * gain
    inner = jnp.mean(scaled * values, axis=-1, keepdims=True)
    gain_part = jnp.sum(grad * values * scale, axis=0, keepdims=True)
    return scale * scaled - values * (scale * scale * scale * inner), gain_part


SLOTS = 3
MID = {0: 3, 1: 2, 2: 1}
PAIRED = (4, 5)
SCHEDULE = {
    "G": (
        ("z", 6, 0),
    ),
    "P0": (
        ("z", 1, 0),
        ("z", 6, 1),
        ("z", 6, 2),
        ("z", 1, 1),
    ),
    "P1": (
        ("x", 6, 2),
        ("x", 6, 1),
    ),
    "P1b": (
        ("x", 1, 0),
        ("x", 5, 0),
        ("x", 1, 1),
    ),
    "P2": (
        ("z", 1, 2),
        ("z", 1, 3),
        ("x", 6, 0),
        ("x", 1, 2),
        ("z", 0, 0),
        ("z", 6, 3),
    ),
    "P3": (
        ("x", 4, 0),
        ("z", 0, 1),
    ),
    "P3b": (
        ("x", 1, 3),
        ("x", 6, 3),
        ("z", 5, 0),
        ("z", 0, 2),
    ),
    "P5": (
        ("z", 3, 0),
        ("x", 0, 0),
    ),
    "P6": (
        ("z", 0, 3),
        ("z", 2, 0),
    ),
    "P7": (
        ("x", 0, 3),
        ("x", 0, 1),
    ),
    "P8": (
        ("z", 2, 1),
        ("x", 0, 2),
        ("z", 2, 2),
        ("z", 4, 0),
        ("x", 2, 1),
        ("x", 2, 2),
    ),
    "P8b": (
        ("x", 2, 0),
        ("z", 3, 1),
        ("z", 3, 2),
        ("x", 3, 1),
        ("z", 2, 3),
        ("x", 3, 0),
    ),
    "P9": (
        ("z", 5, 1),
        ("x", 2, 3),
        ("z", 3, 3),
    ),
    "F0a": (
        ("z", 4, 1),
    ),
    "F1a": (
        ("x", 3, 2),
        ("x", 3, 3),
    ),
    "F1b": (
        ("s", 0),
    ),
    "F2a": (
        ("z", 4, 2),
    ),
    "F3a": (
        ("s", 1),
        ("z", 5, 2),
        ("z", 4, 3),
    ),
    "F4a": (
        ("z", 5, 3),
    ),
    "F5b": (
        ("a", 0),
        ("s", 2),
    ),
    "B0": (
        ("a", 1),
    ),
    "B1": (
        ("p", 0),
        ("s", 3),
    ),
    "B2": (
        ("a", 2),
    ),
    "B3": (
        ("p", 1),
        ("a", 3),
        ("s", 4),
    ),
    "B4": (
        ("p", 2),
        ("s", 6),
    ),
    "C2e": (
        ("f", 1),
    ),
    "C1": (
        ("s", 5),
    ),
    "C1e": (
        ("p", 3),
    ),
    "C0": (
        ("a", 4),
    ),
    "D0": (
        ("f", 3),
        ("f", 0),
        ("a", 5),
    ),
    "D1": (
        ("f", 2),
    ),
    "D2": (
        ("a", 6),
        ("p", 4),
    ),
    "D3": (
        ("p", 5),
        ("a", 7),
    ),
    "D4": (
        ("p", 6),
        ("a", 8),
        ("p", 7),
        ("f", 4),
    ),
    "D5": (
        ("p", 8),
        ("f", 5),
        ("f", 7),
        ("f", 6),
        ("f", 8),
    ),
}


def layer_kernel(*refs):
    (
        tokens,
        out_grad,
        attn_gain,
        mlp_gain,
        q_gain,
        k_gain,
        cosine,
        sine,
        start_in,
        start_row,
        wq,
        wk,
        wv,
        wo,
        wg,
        wu,
        wd,
        output,
        input_grad,
        gain_out,
        g_q,
        g_k,
        g_v,
        g_o,
        g_gate,
        g_up,
        g_down,
        qkv_full,
        o_full,
        ff_full,
        grad_full,
        first_t,
        proj_s,
        plane_s,
        k_s,
        v_s,
        heads_s,
        stat_s,
        middle_s,
        ff_keep,
        ff_send,
        ff_xland,
        ff_zland,
        at_keep,
        at_send,
        at_xland,
        at_zland,
        core_land,
        low_land,
        mlp_own,
        mlp_low,
        da_land,
        heads_land,
        kv_land,
        back_land,
        sems,
        xa,
        sa,
        ta,
        tb,
        attn,
        loaded,
        added,
        summed,
        low_send,
        gains,
        gains_land,
    ) = refs
    n = Net(sems)
    rows, width = tokens.shape
    d = q_gain.shape[1]
    shard = wq.shape[0]
    block = 2 * shard
    quads = n.quads
    tiles, _, ff_cols = ff_keep.shape
    ft = ff_cols // 3
    half_ff = tiles * ft
    top = kv_land.shape[0]
    step, tall = 128, 256
    steps = rows // step
    my_at = pl.multiple_of(n.core * rows, rows)
    their_at = pl.multiple_of((1 - n.core) * rows, rows)
    my_rows = pl.ds(my_at, rows)
    my_chip = pl.ds(pl.multiple_of(n.x * 2 * rows, 2 * rows), 2 * rows)
    other_chip = pl.ds(pl.multiple_of((1 - n.x) * 2 * rows, 2 * rows), 2 * rows)
    scale = 1.0 / math.sqrt(d)
    bf = lambda *shape: pltpu.VMEM(shape, BF16)
    f32 = lambda *shape: pltpu.VMEM(shape, F32)

    def load(pairs):
        copies = [pltpu.make_async_copy(s, t, n.sem()) for s, t in pairs]
        for c in copies:
            c.start()
        return copies

    def load_now(pairs):
        for c in load(pairs):
            c.wait()

    def loop(count, fn):
        def body(i, carry):
            fn(i)
            return carry

        lax.fori_loop(0, count, body, 0)

    def part(i, size):
        return pl.ds(pl.multiple_of(i * size, size), size)

    n.greet()

    qkv = Gather(n, qkv_full, shard, [(wq, 0, 4 * d, 0), (wk, 0, 2 * d, 4 * d), (wv, 0, 2 * d, 6 * d)])
    o_w = Gather(n, o_full, shard, [(wo, 0, 4 * d, 0)])
    ffw = [
        Gather(
            n,
            ff_full.at[f],
            shard,
            [(arr, f * ft, ft, kind * ft) for kind, arr in enumerate((wg, wu, wd))],
            paired=f in PAIRED,
        )
        for f in range(tiles)
    ]
    ff = [
        Scatter(n, ff_keep.at[f], ff_send.at[f], ff_xland.at[f], ff_zland.at[f], loaded, added, f % SLOTS)
        for f in range(tiles)
    ]
    at_groups = [
        Scatter(n, at_keep.at[f], at_send.at[f], at_xland.at[f], at_zland.at[f], loaded, added, (tiles + f) % SLOTS)
        for f in range(3)
    ]

    def ff_write(f):
        def places(c):
            col = c * half_ff + f * ft
            return [(k * ft, ft, dst, col) for k, dst in enumerate((g_gate, g_up, g_down))]

        return places

    def simple(places):
        return lambda c: [(at, wide, dst, c * wide) for at, wide, dst in places]

    groups = ffw + [o_w]
    sums = ff + at_groups
    writes = [ff_write(f) for f in range(tiles)] + [
        simple([(0, 4 * d, g_o)]),
        simple([(0, 4 * d, g_q)]),
        simple([(0, 2 * d, g_k), (2 * d, 2 * d, g_v)]),
    ]
    planned = 1 + max(step[2] for steps_at in SCHEDULE.values() for step in steps_at if step[0] in "zx")

    def tick(name):
        for what, g, *r in SCHEDULE.get(name, ()):
            if what in "zx":
                if r[0] < quads:
                    getattr(groups[g], what)(r[0])
            elif what == "s":
                sums[g].start()
            elif what == "a":
                if g >= SLOTS:
                    sums[g - SLOTS].sent()
                sums[g].add()
            elif what == "p":
                sums[g].pass_on()
            else:
                sums[g].final(summed, writes[g])

    def need(g):
        for r in range(planned, quads):
            groups[g].z(r)
            groups[g].x(r)
        groups[g].arrived()

    def tick_within(h, sweeps, name):
        flags = [s.own_waited for s in sums]
        pl.when(n.quad >= h)(lambda: sweeps(lambda: tick(name)))
        for s, flag in zip(sums, flags):
            s.own_waited = flag
        pl.when(n.quad < h)(lambda: tick(name))

    plane = ta.at[:, pl.ds(0, 4 * d)]
    keys = [tb.at[:, pl.ds(h * d, d)] for h in range(top + 1)]
    vals = [ta.at[:, pl.ds(4 * d, 2 * d)], ta.at[:, pl.ds(6 * d, 2 * d)], tb.at[:, pl.ds(3 * d, 2 * d)]]
    ones = [ta.at[:, pl.ds(5 * d, d)], ta.at[:, pl.ds(7 * d, d)], tb.at[:, pl.ds(4 * d, d)]]

    def core_then_tensor(product, sending, k, tmp_low):
        core_copies, low_copies = [], []
        for i in range(rows // tall):
            at = pl.ds(i * tall, tall)
            sending[at, :] = product(pl.ds(their_at + i * tall, tall)).astype(BF16)
            core_copies.append(n.send(sending.at[at], core_land.at[k, at], n.other_core()))
        for i in range(rows // tall):
            got = product(pl.ds(my_at + i * tall, tall))
            core_copies[i].wait_recv()
            for p in range(tall // step):
                at = pl.ds(i * tall + p * step, step)
                load_now([(core_land.at[k, at], tmp_low.at[0])])
                low_send[at, :] = (got[p * step : (p + 1) * step] + tmp_low[0].astype(F32)).astype(BF16)
                low_copies.append(n.send(low_send.at[at], low_land.at[k, at], n.other_tensor()))
        return low_copies

    def forward(w_qkv, proj, low, acc, heads, stat, w_o, core_send, tmp, tmp_low, start_col):
        qkv.start()
        o_w.start()
        qkv.z(0)
        qkv.x(0)
        for g in ffw:
            g.start()

        def norm_first(i):
            load_tok = pltpu.make_async_copy(tokens.at[part(i, step)], tmp_low.at[0], tok_sem)
            load_tok.start()
            load_tok.wait()
            to = pl.ds(pl.multiple_of(n.core * rows + i * step, step), step)
            xa[to, :] = rms_rows(tmp_low[0].astype(F32), attn_gain[...]).astype(BF16)

        tok_sem = n.sem()
        loop(steps, norm_first)
        first_copy = n.send(xa.at[my_rows], xa.at[my_rows], n.other_core())
        for r in range(1, quads):
            qkv.z(r)
            qkv.x(r)
        tick("G")
        grad_copy = n.send(out_grad, grad_full.at[my_rows], n.other_core())
        grad_keep = n.keep(out_grad, grad_full.at[my_rows])
        start_load = load([(start_in, start_col)])
        for o in ones:
            o[...] = jnp.ones((4 * rows, d), BF16)
        acc[...] = jnp.zeros_like(acc)
        first_copy.wait_recv()
        qkv.arrived()
        load_now([(qkv_full, w_qkv)])

        def project(i):
            at = part(i, tall)
            proj[at, :] = dot(xa[at, :], w_qkv[...])
            cos, sin = cosine[at, :], sine[at, :]

            def prep(col, gain):
                u = rms_rows(proj[at, pl.ds(col, d)], gain[...])
                return (u * cos + pltpu.roll(u, d // 2, 1) * sin).astype(BF16)

            for h in range(2):
                for g in range(2):
                    low[h, at, pl.ds(g * d, d)] = prep((2 * h + g) * d, q_gain)
                low[h, at, pl.ds(2 * d, d)] = prep((4 + h) * d, k_gain)
                low[h, at, pl.ds(3 * d, d)] = proj[at, pl.ds((6 + h) * d, d)].astype(BF16)

        loop(2 * rows // tall, project)
        head_copy = n.copy(low.at[1 - n.x], plane.at[my_chip], n.other_x())
        head_copy.start()
        n.keep(proj, proj_s)
        plane[my_chip, :] = low[n.x]
        tick("P0")

        def flip_first(i):
            at = part(i, tall)
            w_qkv[at, :] = xa[:, at].T

        loop(width // tall, flip_first)
        n.keep(w_qkv, first_t)
        head_copy.wait()
        keys[0][...] = plane[:, pl.ds(2 * d, d)]
        vals[0][:, pl.ds(0, d)] = plane[:, pl.ds(3 * d, d)]

        ahead = n.at(quad=jnp.minimum(n.quad + 1, quads - 1))
        hops = [
            [
                n.copy(keys[h], keys[h + 1], ahead),
                n.copy(vals[h].at[:, pl.ds(0, d)], vals[h + 1].at[:, pl.ds(0, d)], ahead),
            ]
            for h in range(top)
        ]

        def hop_start(h):
            @pl.when((n.quad >= h) & (n.quad < quads - 1))
            def _():
                for c in hops[h]:
                    c.start()

        def hop_sent(h):
            @pl.when((n.quad >= h) & (n.quad < quads - 1))
            def _():
                for c in hops[h]:
                    c.wait_send()

        def hop_arrived(h):
            @pl.when(n.quad >= h + 1)
            def _():
                for c in hops[h]:
                    c.wait_recv()

        def attend(h, i, j):
            q_at, k_at = part(i, rows), part(j, rows)
            q2 = jnp.concatenate([plane[q_at, pl.ds(0, d)], plane[q_at, pl.ds(d, d)]], axis=0)
            prob = jnp.exp2(dot(q2, keys[h][k_at, :], NT) * (scale * LOG2E))
            k_pos = (4 * (n.quad - h) + j) * rows + lax.broadcasted_iota(jnp.int32, (rows, rows), 1)
            keep = k_pos >= start_col[q_at, :]
            if h == 0:
                q_pos = (4 * n.quad + i) * rows + lax.broadcasted_iota(jnp.int32, (rows, rows), 0)
                keep = keep & (k_pos <= q_pos)
            prob = jnp.where(jnp.concatenate([keep, keep], axis=0), prob, 0.0)
            acc[i] += dot(prob.astype(BF16), vals[h][k_at, :])

        def sweep(h, lo, hi, mid):
            def over_i(i, carry):
                pl.when(i == MID[h])(mid)

                def over_j(j, inner):
                    attend(h, i, j)
                    return inner

                lax.fori_loop(lo(i), hi(i), over_j, 0)
                return carry

            lax.fori_loop(0, 4, over_i, 0)

        start_load[0].wait()
        hop_start(0)
        tick("P1")
        sweep(0, *ranges[0], lambda: tick("P1b"))
        tick("P2")
        hop_arrived(0)
        hop_start(1)
        tick("P3")

        tick_within(1, lambda mid: sweep(1, *ranges[1], mid), "P3b")

        tick("P4")
        need(tiles)
        load_o = load([(o_full, w_o)])
        saves = load([(plane, plane_s)])
        hop_arrived(1)
        tick("P5")

        @pl.when(n.quad >= 2)
        def _():
            sweep(2, *ranges[2], lambda: None)

        for i in range(4):
            at = pl.ds(i * rows, rows)
            total = acc[i, :, d:]
            done = acc[i, :, :d] / total
            heads[at, pl.ds(0, d)] = done[:rows]
            heads[at, pl.ds(d, d)] = done[rows:]
            logs = jnp.log2(total)
            stat[0:1, at] = logs[:rows].T[0:1]
            stat[1:2, at] = logs[rows:].T[0:1]
        low[0, :, pl.ds(0, 2 * d)] = heads[other_chip, :].astype(BF16)
        attn_copy = n.send(low.at[0, :, pl.ds(0, 2 * d)], attn.at[n.x], n.other_x())
        tick("P6")
        attn[n.x] = heads[my_chip, :].astype(BF16)
        n.keep(heads, heads_s)
        n.keep(stat, stat_s)
        for h in range(top + 1):
            at = pl.ds(h * 4 * rows, 4 * rows)
            saves += load([(keys[h], k_s.at[at]), (vals[h].at[:, pl.ds(0, d)], v_s.at[at])])
        for h in range(top):
            hop_sent(h)
        grad_copy.wait_recv()
        grad_keep.wait()
        n.pending.remove(grad_keep.wait)
        first_copy.wait_send()
        n.pending.remove(first_copy.wait_send)
        g_load = load([(grad_full, xa)])
        for c in load_o + saves:
            c.wait()
        attn_copy.wait_recv()
        tick("P7")

        def o_rows(at):
            return dot(attn[0, at, :], w_o[:, : 2 * d], NT) + dot(attn[1, at, :], w_o[:, 2 * d :], NT)

        second_copies = []
        low_copies = core_then_tensor(o_rows, core_send, 3, tmp_low)
        tick("P8")
        for c in g_load:
            c.wait()

        def flip_grad(i):
            at = part(i, tall)
            tb[at, :] = xa[:, at].T

        loop(width // tall, flip_grad)
        tick("P8b")
        for i in range(steps):
            at = pl.ds(i * step, step)
            low_copies[i].wait_recv()
            load_now([(low_land.at[3, at], tmp_low.at[0]), (tokens.at[at], tmp_low.at[1])])
            mid = tmp_low[1].astype(F32) + (low_send[at, :].astype(F32) + tmp_low[0].astype(F32))
            tmp[...] = mid
            mid_copy = load([(tmp, middle_s.at[at])])
            to = pl.ds(my_at + i * step, step)
            sa[to, :] = rms_rows(mid, mlp_gain[...]).astype(BF16)
            second_copies.append(n.send(sa.at[to], sa.at[to], n.other_core()))
            mid_copy[0].wait()
        for i in range(steps):
            second_copies[i].wait_recv()
        tick("P9")
        n.finish()

    ranges = {
        0: (lambda i: 0, lambda i: i + 1),
        1: (lambda i: 0, lambda i: 4),
        2: (lambda i: i, lambda i: 4),
    }
    pl.run_scoped(
        forward,
        bf(width, 8 * d),
        f32(2 * rows, 8 * d),
        bf(2, 2 * rows, 4 * d),
        f32(4, 2 * rows, 2 * d),
        f32(4 * rows, 2 * d),
        f32(2, 4 * rows),
        bf(width, 4 * d),
        bf(rows, width),
        f32(step, width),
        bf(2, step, width),
        pltpu.VMEM((4 * rows, 1), jnp.int32),
    )

    def row_block(xr, s):
        bits = quads.bit_length() - 1
        quad = n.flipped(sum(((s >> b) & 1) << (bits - 1 - b) for b in range(bits)))
        x = n.x if xr == 0 else 1 - n.x
        return pl.multiple_of((quad * 4 + 2 * x) * shard, block)

    low_sent = [n.sem() for _ in range(steps)]
    low_got = [n.sem() for _ in range(steps)]

    def feed_forward(w, mlp, ds, acts, stage, w_sem, stage_sem):
        def fetch(f, slot):
            pltpu.make_async_copy(ff_full.at[f], w.at[slot], w_sem.at[slot]).start()

        tick("F0a")
        need(0)
        fetch(0, 0)
        mlp[...] = jnp.zeros_like(mlp)
        ds[...] = jnp.zeros_like(ds)

        def staged(f):
            for k, dst in enumerate((ff_keep, ff_send)):
                yield pltpu.make_async_copy(stage.at[k], dst.at[f], stage_sem.at[k])

        def at_tile(f, k, fn):
            pl.when(f == k)(fn)

        def flip_second(i):
            at = part(i, step)
            ta[:, at] = sa[at, :].T

        def tile(f, carry):
            slot = lax.rem(f, 2)

            def before(c):
                if c > 0:
                    tick("F%da" % c)
                if c + 1 < tiles:
                    need(c + 1)

            for c in range(tiles):
                at_tile(f, c, partial(before, c))

            @pl.when(f + 1 < tiles)
            def _():
                fetch(f + 1, 1 - slot)

            wait_bytes(w.at[slot], w_sem.at[slot])

            def some_rows(i):
                at = part(i, rows)
                gate = dot(sa[at, :], w[slot, :, pl.ds(0, ft)])
                up = dot(sa[at, :], w[slot, :, pl.ds(ft, ft)])
                d_act = dot(xa[at, :], w[slot, :, pl.ds(2 * ft, ft)])
                sig = 1.0 / (1.0 + jnp.exp(-gate))
                silu = gate * sig
                acts[at, pl.ds(2 * ft, ft)] = (silu * up).astype(BF16)
                acts[at, pl.ds(0, ft)] = (d_act * up * sig * (1.0 + gate * (1.0 - sig))).astype(BF16)
                acts[at, pl.ds(ft, ft)] = (d_act * silu).astype(BF16)
                mlp[at, :] += dot(acts[at, pl.ds(2 * ft, ft)], w[slot, :, pl.ds(2 * ft, ft)], NT)
                ds[at, :] += dot(acts[at, pl.ds(0, ft)], w[slot, :, pl.ds(0, ft)], NT) + dot(
                    acts[at, pl.ds(ft, ft)], w[slot, :, pl.ds(ft, ft)], NT
                )

            loop(2, some_rows)

            @pl.when(f >= 1)
            def _():
                for c in staged(f - 1):
                    c.wait()

            for c in range(tiles):
                at_tile(f, c, partial(tick, "F%db" % c))
            @pl.when(f == 0)
            def _():
                loop(2 * rows // step, flip_second)

            for xr in range(2):
                for q in range(quads):
                    at = pl.ds(row_block(xr, q), block)
                    to = pl.ds(q * block, block)
                    stage[xr, to, pl.ds(0, 2 * ft)] = dot(ta[at, :], acts[:, pl.ds(0, 2 * ft)]).astype(BF16)
                    stage[xr, to, pl.ds(2 * ft, ft)] = dot(tb[at, :], acts[:, pl.ds(2 * ft, ft)]).astype(BF16)
            for c in staged(f):
                c.start()

            return carry

        lax.fori_loop(0, tiles, tile, 0)
        core_copies = []
        for i in range(steps):
            at = pl.ds(i * step, step)
            xa[at, :] = ds[pl.ds(their_at + i * step, step), :].astype(BF16)
            core_copies.append(n.copy(xa.at[at], core_land.at[0, at], n.other_core()))
            core_copies[-1].start()
        for c in staged(tiles - 1):
            c.wait()
        for i in range(steps):
            at = pl.ds(i * step, step)
            core_copies[i].wait_recv()
            spare = xa.at[pl.ds(rows + i * step, step)]
            load_now([(core_land.at[0, at], spare)])
            low_send[at, :] = (ds[pl.ds(my_at + i * step, step), :] + spare[...].astype(F32)).astype(BF16)
            n.copy(
                low_send.at[at], low_land.at[0, at], n.other_tensor(), low_sent[i], low_got[i]
            ).start()

        tick("B0")
        def to_low(i):
            at = part(i, step)
            sa[at, :] = mlp[at, :].astype(BF16)

        loop(2 * rows // step, to_low)
        mlp_copy = n.copy(sa.at[pl.ds(their_at, rows)], core_land.at[1], n.other_core())
        mlp_copy.start()
        mlp_keep = load([(sa.at[my_rows], mlp_own)])
        for c in core_copies:
            c.wait_send()
        mlp_copy.wait()
        mlp_keep[0].wait()

    pl.run_scoped(
        feed_forward,
        bf(2, width, ff_cols),
        f32(2 * rows, width),
        f32(2 * rows, width),
        bf(2 * rows, ff_cols),
        bf(2, 2 * rows, ff_cols),
        pltpu.SemaphoreType.DMA((2,)),
        pltpu.SemaphoreType.DMA((2,)),
    )

    def backward(
        d_middle, tmp, tmp_low, vx, heads, stat, d_out, d_q, d_kv, kv_low, d_low, d_proj
    ):
        loads = load(
            [(o_full, ta.at[:, pl.ds(0, 4 * d)]), (plane_s, tb.at[:, pl.ds(0, 4 * d)]), (v_s, vx), (heads_s, heads)]
            + [(stat_s, stat.at[pl.ds(0, 2)])]
            + [
                (k_s.at[pl.ds(h * 4 * rows, 4 * rows)], tb.at[:, pl.ds((4 + h) * d, d)])
                for h in range(top + 1)
            ]
        )
        early = load([(middle_s, d_middle), (out_grad, xa.at[my_rows])])
        gains[...] = jnp.zeros_like(gains)

        tick("B1")
        for i in range(steps):
            at = pl.ds(i * step, step)
            load_now([(mlp_own.at[at], tmp_low.at[0]), (core_land.at[1, at], tmp_low.at[1])])
            tmp_low[0] = (tmp_low[0].astype(F32) + tmp_low[1].astype(F32)).astype(BF16)
            load_now([(tmp_low.at[0], mlp_low.at[at])])

        tick("B2")
        for c in early:
            c.wait()
        da_copies = []
        for i in range(steps):
            at = pl.ds(i * step, step)
            to = pl.ds(my_at + i * step, step)
            wait_bytes(low_land.at[0, at], low_got[i])
            load_now([(low_land.at[0, at], tmp_low.at[0])])
            d_second = low_send[at, :].astype(F32) + tmp_low[0].astype(F32)
            back, gain_part = norm_back(d_middle[at, :], mlp_gain[...], d_second)
            gains[1:2, :] += gain_part
            d_mid = xa[to, :].astype(F32) + back
            d_middle[at, :] = d_mid
            xa[to, :] = d_mid.astype(BF16)
            da_copies.append(n.copy(xa.at[to], da_land.at[at], n.other_core()))
            da_copies[-1].start()
        mlp_copy = n.send(mlp_low, low_land.at[1], n.other_tensor())
        for i in range(steps):
            wait_bytes(low_send.at[pl.ds(i * step, step)], low_sent[i])
        for c in loads:
            c.wait()
        for c in da_copies:
            c.wait()
        load_now([(da_land, xa.at[pl.ds(their_at, rows)])])

        def head_grads(i):
            at = part(i, tall)
            got = dot(xa[at, :], ta[:, pl.ds(0, 4 * d)]).astype(BF16)
            d_low[0, at, pl.ds(0, 2 * d)] = got[:, : 2 * d]
            d_low[1, at, pl.ds(0, 2 * d)] = got[:, 2 * d :]

        loop(2 * rows // tall, head_grads)
        heads_copy = n.copy(d_low.at[1 - n.x, :, pl.ds(0, 2 * d)], heads_land, n.other_x())
        heads_copy.start()
        tick("B3")
        d_out[my_chip, :] = d_low[n.x, :, pl.ds(0, 2 * d)]
        d_q[...] = jnp.zeros_like(d_q)

        def flip(i):
            at = part(i, tall)
            ta[at, :] = xa[:, at].T

        loop(width // tall, flip)

        def weight_pieces(right, k):
            for xr in range(2):
                for q in range(quads):
                    sa[pl.ds(q * block, block), pl.ds((2 * k + xr) * 4 * d, 4 * d)] = dot(
                        ta[pl.ds(row_block(xr, q), block), :], right
                    ).astype(BF16)

        def stage_out(k, g):
            return load(
                [
                    (sa.at[:, pl.ds((2 * k + xr) * 4 * d, 4 * d)], dst.at[g])
                    for xr, dst in enumerate((at_keep, at_send))
                ]
            )

        weight_pieces(jnp.concatenate([attn[0], attn[1]], axis=1), 0)
        o_stage = stage_out(0, 0)
        heads_copy.wait()
        load_now([(heads_land, d_out.at[other_chip])])
        for c in o_stage:
            c.wait()
        tick("B4")

        for g in range(2):
            for i in range(4):
                at = pl.ds(i * rows, rows)
                cols = pl.ds(g * d, d)
                prod = d_out[at, cols].astype(F32) * heads[at, cols]
                stat[2 + g : 3 + g, at] = jnp.sum(prod.T, axis=0, keepdims=True)
        q_proj = load(
            [
                (proj_s.at[:, pl.ds(h * 2 * d, 2 * d)], heads.at[pl.ds(h * 2 * rows, 2 * rows)])
                for h in range(2)
            ]
        )

        def attend_back(h, i, j):
            q_at, k_at = part(i, rows), part(j, rows)
            q2 = jnp.concatenate([tb[q_at, pl.ds(0, d)], tb[q_at, pl.ds(d, d)]], axis=0)
            g2 = jnp.concatenate([d_out[q_at, pl.ds(0, d)], d_out[q_at, pl.ds(d, d)]], axis=0)
            log_total = jnp.concatenate([stat[0:1, q_at], stat[1:2, q_at]], axis=1)
            row_dot = jnp.concatenate([stat[2:3, q_at], stat[3:4, q_at]], axis=1)
            k_now = tb[k_at, pl.ds((4 + h) * d, d)]
            v_now = vx[pl.ds(pl.multiple_of(h * 4 * rows + j * rows, rows), rows), :]
            prob = jnp.exp2(dot(k_now, q2, NT) * (scale * LOG2E) - log_total)
            k_pos = (4 * (n.quad - h) + j) * rows + lax.broadcasted_iota(jnp.int32, (rows, rows), 0)
            keep = k_pos >= start_row[:, q_at]
            if h == 0:
                q_pos = (4 * n.quad + i) * rows + lax.broadcasted_iota(jnp.int32, (rows, rows), 1)
                keep = keep & (k_pos <= q_pos)
            prob = jnp.where(jnp.concatenate([keep, keep], axis=1), prob, 0.0)
            d_prob = dot(v_now, g2, NT)
            d_score = (prob * (d_prob - row_dot)).astype(BF16)
            d_kv[k_at, pl.ds(d, d)] += dot(prob.astype(BF16), g2)
            d_kv[k_at, pl.ds(0, d)] += dot(d_score, q2)
            got = dot(d_score, k_now, TN)
            d_q[q_at, pl.ds(0, d)] += got[:rows]
            d_q[q_at, pl.ds(d, d)] += got[rows:]

        def plane_back(h, lo, hi, mid):
            d_kv[...] = jnp.zeros_like(d_kv)

            def over_i(i, carry):
                pl.when(i == MID[h])(mid)

                def over_j(j, inner):
                    attend_back(h, i, j)
                    return inner

                lax.fori_loop(lo(i), hi(i), over_j, 0)
                return carry

            lax.fori_loop(0, 4, over_i, 0)
            d_kv[:, pl.ds(0, d)] = d_kv[:, pl.ds(0, d)] * scale

        behind = n.at(quad=jnp.maximum(n.quad - 1, 0))
        hops = [n.copy(kv_low.at[k], kv_land.at[k], behind) for k in range(top)]
        kv_sem = n.sem()

        def add_landed(k):
            hops[k].wait_recv()
            for p in range(2):
                at = pl.ds(p * 2 * rows, 2 * rows)
                c = pltpu.make_async_copy(kv_land.at[k, at], d_low.at[p, :, pl.ds(2 * d, 2 * d)], kv_sem)
                c.start()
                c.wait()
                d_kv[at, :] += d_low[p, :, pl.ds(2 * d, 2 * d)].astype(F32)

        for h in range(top, 0, -1):

            def one_plane(mid, h=h):
                plane_back(h, *ranges[h], mid)
                if h < top:

                    @pl.when(n.quad < quads - 1)
                    def _():
                        add_landed(top - h - 1)

                kv_low[top - h] = d_kv[...].astype(BF16)
                hops[top - h].start()

            tick_within(h, one_plane, "C%d" % h)
            tick("C%de" % h)
        plane_back(0, *ranges[0], lambda: tick("C0"))

        def put_back(x, first, source, factor):
            def body(i):
                at = part(i, tall)
                src = pl.ds(pl.multiple_of(x * 2 * rows + i * tall, tall), tall)
                d_low[x, at, pl.ds(first, 2 * d)] = (source[src, :] * factor).astype(BF16)

            loop(2 * rows // tall, body)

        q_cols, kv_cols = pl.ds(0, 2 * d), pl.ds(2 * d, 2 * d)
        put_back(1 - n.x, 0, d_q, scale)
        q_back = n.copy(d_low.at[1 - n.x, :, q_cols], back_land.at[:, q_cols], n.other_x())
        q_back.start()
        put_back(n.x, 0, d_q, scale)
        k_proj = load([(proj_s.at[:, pl.ds(4 * d, 2 * d)], d_q.at[pl.ds(0, 2 * rows)])])
        late = load([(first_t, ta), (qkv_full, tb)])

        tick("D0")
        @pl.when(n.quad < quads - 1)
        def _():
            add_landed(top - 1)

        put_back(1 - n.x, 2 * d, d_kv, 1.0)
        kv_back = n.copy(d_low.at[1 - n.x, :, kv_cols], back_land.at[:, kv_cols], n.other_x())
        kv_back.start()
        put_back(n.x, 2 * d, d_kv, 1.0)
        tick("D1")
        q_back.wait()
        load_now([(back_land.at[:, q_cols], d_low.at[1 - n.x, :, q_cols])])

        def prep_back(cols):
            def body(i):
                at = part(i, tall)
                cos, sin = cosine[at, :], sine[at, :]
                for col, h, src, gain, row, read in cols:
                    grad = d_low[h, at, pl.ds(src, d)]
                    if gain is not None:
                        grad = grad.astype(F32)
                        grad = grad * cos + pltpu.roll(grad * sin, d // 2, 1)
                        grad, gain_part = norm_back(read(i), gain[...], grad)
                        gains[pl.ds(row, 1), pl.ds(0, d)] += gain_part
                    d_proj[at, pl.ds(col, d)] = grad.astype(BF16)

            loop(2 * rows // tall, body)

        def q_read(h, g):
            return lambda i: heads[
                pl.ds(pl.multiple_of(h * 2 * rows + i * tall, tall), tall), pl.ds(g * d, d)
            ]

        def k_read(h):
            return lambda i: d_q[part(i, tall), pl.ds(h * d, d)]

        for c in q_proj:
            c.wait()
        prep_back(
            [
                ((2 * h + g) * d, h, g * d, q_gain, 2, q_read(h, g))
                for h in range(2)
                for g in range(2)
            ]
        )
        for c in late:
            c.wait()
        weight_pieces(d_proj[:, pl.ds(0, 4 * d)], 0)
        for c in stage_out(0, 1):
            c.wait()
        at_groups[1].start()
        tick("D2")
        kv_back.wait()
        load_now([(back_land.at[:, kv_cols], d_low.at[1 - n.x, :, kv_cols])])
        for c in k_proj:
            c.wait()
        prep_back(
            [((4 + h) * d, h, 2 * d, k_gain, 3, k_read(h)) for h in range(2)]
            + [((6 + h) * d, h, 3 * d, None, None, None) for h in range(2)]
        )

        low_copies = core_then_tensor(
            lambda at: dot(d_proj[at, :], tb[...], NT), xa.at[pl.ds(0, rows)], 2, tmp_low
        )

        weight_pieces(d_proj[:, pl.ds(4 * d, 4 * d)], 1)
        for c in stage_out(1, 2):
            c.wait()
        at_groups[2].start()
        tick("D3")

        tok_load = load([(tokens, xa.at[pl.ds(rows, rows)])])
        mlp_copy.wait_recv()
        for i in range(steps):
            at = pl.ds(i * step, step)
            load_now(
                [
                    (low_land.at[1, at], tmp_low.at[0]),
                    (mlp_low.at[at], tmp_low.at[1]),
                    (middle_s.at[at], tmp),
                ]
            )
            tmp_low[0] = (tmp[...] + (tmp_low[1].astype(F32) + tmp_low[0].astype(F32))).astype(BF16)
            load_now([(tmp_low.at[0], output.at[at])])
        tick("D4")
        tok_load[0].wait()
        for i in range(steps):
            at = pl.ds(i * step, step)
            low_copies[i].wait_recv()
            load_now([(low_land.at[2, at], tmp_low.at[0])])
            d_first = low_send[at, :].astype(F32) + tmp_low[0].astype(F32)
            back, gain_part = norm_back(xa[pl.ds(rows + i * step, step), :].astype(F32), attn_gain[...], d_first)
            gains[0:1, :] += gain_part
            d_middle[at, :] = d_middle[at, :] + back
            n.keep(d_middle.at[at], input_grad.at[at])

        for k, to in enumerate((n.other_core(), n.other_x(), n.other_tensor())):
            c = n.copy(gains, gains_land.at[k], to)
            c.start()
            c.wait()
            if k < 2:
                gains[...] += gains_land[k]
            else:
                gains[2:4, :] += gains_land[k, 2:4, :]
        gains_land[3 + n.quad] = gains[...]
        quad_copies = []
        for s in range(1, quads):
            to = n.at(quad=lax.rem(n.quad + s, quads))
            quad_copies.append(n.copy(gains, gains_land.at[3 + n.quad], to))
            quad_copies[-1].start()
        for c in quad_copies:
            c.wait()
        total = gains_land[3]
        for k in range(1, quads):
            total = total + gains_land[3 + k]
        gains[...] = total
        n.keep(gains, gain_out)
        tick("D5")
        for g in (ff + at_groups)[-SLOTS:]:
            g.sent()
        for k in range(top):

            @pl.when(n.quad >= top - k)
            def _(k=k):
                hops[k].wait_send()

        n.finish()
        for g in [qkv, o_w] + ffw:
            g.finish()
        assert n.used <= sems.shape[0], n.used


    pl.run_scoped(
        backward,
        f32(rows, width),
        f32(step, width),
        bf(2, step, width),
        bf(4 * rows * (top + 1), d),
        f32(4 * rows, 2 * d),
        f32(4, 4 * rows),
        bf(4 * rows, 2 * d),
        f32(4 * rows, 2 * d),
        f32(4 * rows, 2 * d),
        bf(top, 4 * rows, 2 * d),
        bf(2, 2 * rows, 4 * d),
        bf(2 * rows, 8 * d),
    )


def whole_layer(tokens, out_grad, attn_gain, mlp_gain, q_gain, k_gain, *arrays):
    rows, width = tokens.shape
    d = q_gain.shape[0]
    wg = arrays[-1]
    shard = wg.shape[0]
    quads = lax.axis_size("dp") // 4
    tiles, half_ff = 6, wg.shape[1] // 2
    cols = 3 * half_ff // tiles
    top = REACH // 4
    widest = max(cols, 4 * d)
    assert top == 2 and width == 4 * rows and 2 * rows == 8 * d
    vmem = pl.BlockSpec(memory_space=pltpu.VMEM)
    hbm = pl.BlockSpec(memory_space=pl.ANY)

    def bf(*shape):
        return jax.ShapeDtypeStruct(shape, BF16)

    def f32(*shape):
        return jax.ShapeDtypeStruct(shape, F32)

    out_shape = [bf(rows, width), f32(rows, width), f32(4, width)]
    out_shape += [f32(shard, 8 * d), f32(shard, 4 * d), f32(shard, 4 * d), f32(shard, 8 * d)]
    out_shape += [f32(shard, 2 * half_ff)] * 3
    out_shape += [bf(width, 8 * d), bf(width, 4 * d), bf(tiles, width, cols)]
    out_shape += [bf(2 * rows, width), bf(width, 2 * rows), f32(2 * rows, 8 * d), bf(4 * rows, 4 * d)]
    out_shape += [bf(4 * rows * (top + 1), d)] * 2
    out_shape += [f32(4 * rows, 2 * d), f32(2, 4 * rows), f32(rows, width)]
    out_shape += [bf(tiles, width // 2, cols)] * 3 + [bf(tiles, width // 2 + 4 * shard, cols)]
    out_shape += [bf(3, width // 2, 4 * d)] * 3 + [bf(3, width // 2 + 4 * shard, 4 * d)]
    out_shape += [bf(4, rows, width)] * 2
    out_shape += [bf(rows, width)] * 3
    out_shape += [bf(2 * rows, 2 * d), bf(top, 4 * rows, 2 * d), bf(2 * rows, 4 * d)]
    return pl.pallas_call(
        layer_kernel,
        in_specs=[hbm] * 2 + [vmem] * 6 + [hbm, vmem] + [hbm] * 7,
        out_specs=[hbm] * len(out_shape),
        out_shape=out_shape,
        scratch_shapes=[
            pltpu.SemaphoreType.DMA((330 + 36 * quads,)),
            pltpu.VMEM((2 * rows, width), BF16),
            pltpu.VMEM((2 * rows, width), BF16),
            pltpu.VMEM((width, 2 * rows), BF16),
            pltpu.VMEM((width, 2 * rows), BF16),
            pltpu.VMEM((2, 2 * rows, 2 * d), BF16),
            pltpu.VMEM((width // 2, widest), BF16),
            pltpu.VMEM((SLOTS, width // 2, widest), BF16),
            pltpu.VMEM((2, shard, widest), F32),
            pltpu.VMEM((rows, width), BF16),
            pltpu.VMEM((4, width), F32),
            pltpu.VMEM((3 + quads, 4, width), F32),
        ],
        compiler_params=pltpu.CompilerParams(
            collective_id=0, has_side_effects=True, vmem_limit_bytes=VMEM_LIMIT
        ),
        name="layer",
    )(
        tokens,
        out_grad,
        attn_gain[None],
        mlp_gain[None],
        q_gain[None],
        k_gain[None],
        *arrays,
    )[:10]


def local(
    tokens,
    out_grad,
    lengths,
    attn_gain,
    q_weight,
    key_matrix,
    value_matrix,
    o_weight,
    q_gain,
    k_gain,
    mlp_gain,
    gate_weight,
    up_weight,
    down_weight,
):
    rows = tokens.shape[0]
    d = q_gain.shape[0]
    me = lax.axis_index("dp")
    assert key_matrix.shape[1] == 4 * d and q_weight.shape[1] == 8 * d
    chip_index = (me // 2) * 2 * rows + jnp.arange(2 * rows, dtype=jnp.int32)
    cosine, sine_vals = angles(chip_index - starts_of(chip_index, lengths), d)
    sine_signed = jnp.concatenate([-sine_vals[:, : d // 2], sine_vals[:, d // 2 :]], 1)
    q_index = (me // 4) * 4 * rows + jnp.arange(4 * rows, dtype=jnp.int32)
    q_start = starts_of(q_index, lengths)
    output, input_grad, gains, g_q, g_k, g_v, g_o, g_gate, g_up, g_down = whole_layer(
        tokens,
        out_grad,
        attn_gain,
        mlp_gain,
        q_gain,
        k_gain,
        cosine,
        sine_signed,
        q_start[:, None],
        q_start[None, :],
        q_weight,
        key_matrix,
        value_matrix,
        o_weight,
        gate_weight,
        up_weight,
        down_weight,
    )
    return (
        output,
        input_grad,
        gains[0],
        g_q,
        g_k,
        g_v,
        g_o,
        gains[2, :d],
        gains[3, :d],
        gains[1],
        g_gate,
        g_up,
        g_down,
    )


def solution(mesh):
    rows, weight = P("dp", None), P("dp", "tensor")
    placed = (
        (rows, rows) + (P(),) * 2 + (weight,) * 4 + (P(),) * 3 + (weight,) * 3
    )
    return jax.shard_map(
        local,
        mesh=mesh,
        in_specs=placed,
        out_specs=(rows, rows, P()) + (weight,) * 4 + (P(),) * 3 + (weight,) * 3,
        check_vma=False,
    )
```
